256 devices in a mesh: tm: 16 (over y_hi, x, core), space: 16 (over y_lo, z).
Axes of the slice: x: 4, y: 4 (y_hi: 2, y_lo: 2; y = y_hi * 2 + y_lo), z: 8, core: 2. Of those that a mesh axis runs over, the one named last changes fastest.
Arguments:
- initial_starts: float32 [16, 1024, 2048], P('tm', None, 'space'), may hold values from -6 to 6
- source: float32 [16, 1024, 2048], P('tm', None, 'space'), may hold values from -12 to 12
- region: int32 [1024, 2048], P(None, 'space'), may hold values from 0 to 7
- base_reluctivity: float32 [8], replicated, may hold values from 0.4 to 1
- saturation: float32 [8], replicated, may hold values from 0.2 to 1
- mobility: float32 [8], replicated, may hold values from 0.01 to 0.12
Outputs:
- final_starts: float32 [16, 1024, 2048], P('tm', None, 'space')
- fine_ends: float32 [16, 1024, 2048], P('tm', None, 'space')
The draws below stay inside these ranges and needn't reach their ends.
All inputs are finite; a program needn't handle non-finite values.
Results may differ from the reference program's by a relative error of at most 0.00002.
Values sent between devices are 32-bit elements; how exact they have to be, the bound alone decides.
A program may use at most 64 MiB of HBM per device.

```python
import math
import jax
import jax.numpy as jnp
from jax import lax

RADIAL = 1024
REGIONS = 8
STEPS = 3
ITERS = 2
SLICES = 16
ANGLES = 2048


def with_ends(values, stream_key, smallest, top_value):
    longest = values.shape.index(max(values.shape))
    spots = []
    for shift in (0, 1):
        where = [jax.random.randint(jax.random.fold_in(stream_key, axis), (), 0, length) for axis, length in enumerate(values.shape)]
        where[longest] = (where[longest] + shift) % values.shape[longest]
        spots.append(tuple(where))
    return values.at[spots[0]].set(smallest).at[spots[1]].set(top_value)


def shard_levels(stream_key, extent, split, low, largest):
    loudness, own = 1.0, jax.random.fold_in(stream_key, 6)
    for dim, shards_of in split:
        draws = jnp.exp(jax.random.uniform(jax.random.fold_in(own, dim), (shards_of,), jnp.float32, low / len(split), largest / len(split)))
        loudness = loudness * jnp.repeat(draws, extent[dim] // shards_of).reshape([-1 if axis == dim else 1 for axis in range(len(extent))])
    return loudness


def normal_values(stream_key, shape, width, bound, shards=(), kind=jnp.bfloat16):
    gain = shard_levels(stream_key, shape, shards, -0.22, 0.18) if shards else 1.0
    drawn = jax.random.normal(stream_key, shape, jnp.float32) * width * gain
    return jnp.minimum(jnp.maximum(drawn, -bound), bound).astype(kind)


def setup_inputs(seed: int = 0) -> dict:
    streams_of = jax.random.split(jax.random.key(seed), 7)
    initial_starts = normal_values(streams_of[0], (SLICES, RADIAL, ANGLES), 1.0, 6.0, ((0, 16), (2, 16)), jnp.float32)
    source = normal_values(streams_of[1], (SLICES, RADIAL, ANGLES), 2.0, 12.0, ((0, 16), (2, 16)), jnp.float32)
    region = with_ends(jax.random.randint(streams_of[2], (RADIAL, ANGLES), 0, REGIONS), jax.random.fold_in(streams_of[2], 1), 0, REGIONS - 1).astype(jnp.int32)
    base_reluctivity = jnp.clip(jax.random.uniform(streams_of[3], (REGIONS,), jnp.float32, 0.4, 1.0), 0.4, 1.0)
    saturation = jnp.clip(jax.random.uniform(streams_of[4], (REGIONS,), jnp.float32, 0.2, 1.0), 0.2, 1.0)
    mobility = jnp.clip(jnp.exp(jax.random.uniform(streams_of[5], (REGIONS,), jnp.float32, math.log(0.01), math.log(0.12))), 0.01, 0.12)
    return {"initial_starts": initial_starts, "source": source, "region": region, "base_reluctivity": base_reluctivity, "saturation": saturation, "mobility": mobility}


def lookup(region, region_table):
    region_ids = jnp.arange(region_table.shape[0], dtype=jnp.int32)
    picked = jnp.where(region[None] == region_ids[:, None, None], region_table[:, None, None], jnp.float32(0.0))
    return jnp.sum(picked, axis=0)


def wrap_columns(values, margin):
    total = values.shape[1]
    return jnp.concatenate([values[:, total - margin:], values, values[:, :margin]], axis=1)


def advance(potential, base_nu, satur_rate, mobile, driver):
    padded = jnp.pad(potential, ((1, 1), (0, 0)))
    radial_b = (padded[2:, 1:-1] - padded[:-2, 1:-1]) * 0.5
    angle_b = (potential[:, 2:] - potential[:, :-2]) * 0.5
    flux_sq = radial_b * radial_b + angle_b * angle_b
    reluct = base_nu * (1.0 + satur_rate * flux_sq / (1.0 + flux_sq))
    reluct_pad = jnp.pad(reluct, ((1, 1), (0, 0)), mode="edge")
    reluct_mid = reluct[:, 1:-1]
    centre = potential[:, 2:-2]
    east_flux = 0.5 * (reluct_mid + reluct[:, 2:]) * (potential[:, 3:-1] - centre)
    west_flux = 0.5 * (reluct_mid + reluct[:, :-2]) * (potential[:, 1:-3] - centre)
    north_flux = 0.5 * (reluct_mid + reluct_pad[2:, 1:-1]) * (padded[2:, 2:-2] - centre)
    south_flux = 0.5 * (reluct_mid + reluct_pad[:-2, 1:-1]) * (padded[:-2, 2:-2] - centre)
    return centre + mobile * (east_flux + west_flux + north_flux + south_flux + driver)


def reference(initial_starts, source, region, base_reluctivity, saturation, mobility):
    base_nu = lookup(region, base_reluctivity)
    satur_rate = lookup(region, saturation)
    mobile = lookup(region, mobility)
    coarse_gain = 1.0 / (1.0 + 12.0 * mobile * base_nu)
    base_wide = wrap_columns(base_nu, 1)
    satur_wide = wrap_columns(satur_rate, 1)

    def run_slice(slice_pair):
        potential = slice_pair[0]
        for segment in range(STEPS):
            potential = advance(wrap_columns(potential, 2), base_wide, satur_wide, mobile, slice_pair[1])
        return potential

    starts = initial_starts
    fine_ends = initial_starts
    for iteration in range(ITERS):
        fine_ends = lax.map(run_slice, (starts, source))
        corrected = fine_ends - coarse_gain[None] * starts
        previous = fine_ends[SLICES - 1]
        collected = [previous]
        for slot in range(1, SLICES):
            previous = coarse_gain * previous + corrected[slot - 1]
            collected.append(previous)
        starts = jnp.stack(collected)
    return starts, fine_ends
```

```python
import jax
import jax.numpy as jnp
from jax import lax
from jax.experimental import pallas as pl
from jax.experimental.pallas import tpu as pltpu
from jax.sharding import PartitionSpec as P

MESH = pl.DeviceIdType.MESH
HALO = 6
HALF = 64
FRAME = HALF + 2 * HALO
OWN = HALF + HALO
ROWS = 8
F32 = jnp.float32


def rows(col, n):
    start = col * ROWS
    if not isinstance(start, int):
        start = pl.multiple_of(start, ROWS)
    return pl.ds(start, n * ROWS)


def kernel(
    base_ref, satur_ref, mob_ref, a_hbm, j_hbm, r_hbm, starts_hbm, ends_hbm,
    in_a, in_j, in_r, ta, tj, tr, starts, drive, regions, coef_a, coef_b, mobile, gain,
    work, ends, corr0, items, got, sums, out_e, out_s,
    in_sem, pair_send, pair_recv, edge_send, edge_recv, reg_send, reg_recv,
    there_send, there_recv, back_send, back_recv, halo_send, halo_recv, out_send, out_recv, out_sem,
):
    tm = lax.axis_index("tm")
    sp = lax.axis_index("space")
    core = lax.rem(tm, 2)
    other = 1 - core
    pair = tm - core
    chip = tm // 2
    right = lax.rem(sp + 1, 16)
    left = lax.rem(sp + 15, 16)
    outer = jnp.where(core == 0, left, right)
    ahead = jnp.where(core == 0, right, left)

    loads = []
    for n, (src, dst) in enumerate(((a_hbm, in_a), (r_hbm, in_r), (j_hbm, in_j))):
        cp = pltpu.make_async_copy(src, dst, in_sem.at[n])
        cp.start()
        loads.append(cp)

    barrier = pltpu.get_barrier_semaphore()
    pl.semaphore_signal(barrier, inc=1, device_id=(pair + other, sp), device_id_type=MESH)
    for d in range(1, 8):
        pl.semaphore_signal(
            barrier, inc=1, device_id=(2 * lax.rem(chip + d, 8) + core, sp), device_id_type=MESH
        )
    pl.semaphore_signal(barrier, inc=1, device_id=(pair, outer), device_id_type=MESH)
    pl.semaphore_signal(barrier, inc=1, device_id=(pair + 1, outer), device_id_type=MESH)

    def turn(src, dst):
        for s in range(8):
            dst[pl.ds(s, 128, stride=8), :] = src[pl.ds(128 * s, 128), :].T

    loads[0].wait()
    turn(in_a.at[0], ta)
    loads[1].wait()
    turn(in_r, tr)
    loads[2].wait()
    turn(in_j.at[0], tj)

    pl.semaphore_wait(barrier, 10)

    sends = []
    for n, (src, dst) in enumerate(((ta, starts.at[0]), (tj, drive))):
        cp = pltpu.make_async_remote_copy(
            src.at[rows(122, 6)], dst.at[core, rows(0, 6)],
            edge_send.at[n, 0], edge_recv.at[n, core], device_id=(pair, right), device_id_type=MESH,
        )
        cp.start()
        sends.append(cp)
        cp = pltpu.make_async_remote_copy(
            src.at[rows(0, 6)], dst.at[core, rows(OWN, 6)],
            edge_send.at[n, 1], edge_recv.at[n, core], device_id=(pair + 1, left), device_id_type=MESH,
        )
        cp.start()
        sends.append(cp)
    cp_reg = pltpu.make_async_remote_copy(
        tr.at[rows(122 * other, 6)], regions.at[rows(OWN * core, 6)],
        reg_send, reg_recv, device_id=(tm, ahead), device_id_type=MESH,
    )
    cp_reg.start()
    sends.append(cp_reg)
    pairs = []
    for n, (src, dst) in enumerate(((ta, starts.at[0]), (tj, drive))):
        cp = pltpu.make_async_remote_copy(
            src.at[rows(58 * other, OWN)], dst.at[core, rows(HALO * core, OWN)],
            pair_send.at[n], pair_recv.at[n], device_id=(pair + other, sp), device_id_type=MESH,
        )
        cp.start()
        pairs.append(cp)

    starts[0, core, rows(HALO * other, OWN), :] = ta[rows(58 * core, OWN), :]
    drive[core, rows(HALO * other, OWN), :] = tj[rows(58 * core, OWN), :]
    regions[rows(HALO * other, OWN), :] = tr[rows(58 * core, OWN), :]

    cp_reg.wait_recv()
    full = lambda x: jnp.full((8, 128), x, F32)
    base = [full(base_ref[k]) for k in range(8)]
    satur = [full(satur_ref[k]) for k in range(8)]
    mobs = [full(mob_ref[k]) for k in range(8)]
    tab_a = [0.5 * b * (1.0 + s) for b, s in zip(base, satur)]
    tab_b = [2.0 * b * s for b, s in zip(base, satur)]
    tab_c = [1.0 / (1.0 + 12.0 * m * b) for b, m in zip(base, mobs)]

    def lookup(t, _):
        r = regions[rows(t, 1), :]
        bits = [(r & 1) != 0, (r & 2) != 0, (r & 4) != 0]
        for tab, ref in ((tab_a, coef_a), (tab_b, coef_b), (mobs, mobile), (tab_c, gain)):
            level = tab
            for bit in bits:
                level = [jnp.where(bit, hi, lo) for lo, hi in zip(level[::2], level[1::2])]
            ref[rows(t, 1), :] = level[0]
        return 0

    lax.fori_loop(0, FRAME, lookup, 0)

    lane = lax.broadcasted_iota(jnp.int32, (8, 128), 1)
    sub = lax.broadcasted_iota(jnp.int32, (8, 128), 0)
    last_lane = lane == 127
    first_lane = lane == 0
    top = last_lane & (sub == 7)
    bottom = first_lane & (sub == 0)

    def up(x, end):
        r = pltpu.roll(x, 127, 1)
        return jnp.where(top, end, jnp.where(last_lane, pltpu.roll(r, 7, 0), r))

    def down(x, end):
        r = pltpu.roll(x, 1, 1)
        return jnp.where(bottom, end, jnp.where(first_lane, pltpu.roll(r, 1, 0), r))

    def fine(src, dst, lo, hi, shift):
        def column(before, here, after, t):
            north = up(here, 0.0)
            south = down(here, 0.0)
            br = north - south
            bt = after - before
            nu = coef_a[rows(t, 1), :] - coef_b[rows(t, 1), :] / (4.0 + (br * br + bt * bt))
            nu_n = up(nu, nu)
            nu_s = down(nu, nu)
            radial = (nu + nu_n) * (north - here) + (nu + nu_s) * (south - here)
            return nu, radial

        first = []
        for p in range(2):
            a = [src[p, rows(lo - 2 + k, 1), :] for k in range(4)]
            nu_w, _ = column(a[0], a[1], a[2], lo - 1)
            nu, radial = column(a[1], a[2], a[3], lo)
            west = (nu_w + nu) * (a[2] - a[1])
            first.append((a[2], a[3], nu, radial, west))

        def body(t, carry):
            out = []
            for p in range(2):
                here, after, nu, radial, west = carry[p]
                beyond = src[p, rows(t + 2, 1), :]
                nu_e, radial_e = column(here, after, beyond, t + 1)
                east = (nu + nu_e) * (after - here)
                total = (east - west) + radial + drive[p, rows(t, 1), :]
                dst[p, rows(t - shift, 1), :] = here + mobile[rows(t, 1), :] * total
                out.append((after, beyond, nu_e, radial_e, east))
            return tuple(out)

        def four(i, carry):
            for k in range(4):
                carry = body(lo + 4 * i + k, carry)
            return carry

        lax.fori_loop(0, (hi - lo) // 4, four, tuple(first))

    for cp in pairs:
        cp.wait_recv()
    for n in range(2):
        for p in range(2):
            pltpu.make_async_remote_copy(
                ta.at[rows(0, 6)], starts.at[0, 0, rows(0, 6)],
                edge_send.at[n, 0], edge_recv.at[n, p], device_id=(tm, right), device_id_type=MESH,
            ).wait_recv()

    for it in range(2):
        fine(starts.at[it], work, 2, FRAME - 2, 0)
        fine(work, work, 4, FRAME - 4, 0)
        fine(work, ends.at[it], 6, FRAME - 6, HALO)

        if it == 1:
            cp_e = pltpu.make_async_remote_copy(
                ends.at[1, other], out_e.at[rows(HALF * core, HALF)],
                out_send.at[0], out_recv.at[0], device_id=(pair + other, sp), device_id_type=MESH,
            )
            cp_e.start()
            sends.append(cp_e)

        def combine(t, _):
            c = gain[rows(t + HALO, 1), :]
            e0, e1 = ends[it, 0, rows(t, 1), :], ends[it, 1, rows(t, 1), :]
            k0 = e0 - c * starts[it, 0, rows(t + HALO, 1), :]
            k1 = e1 - c * starts[it, 1, rows(t + HALO, 1), :]
            corr0[rows(t, 1), :] = k0
            items[it, rows(t, 1), :] = jnp.where(chip == 7, e1, c * k0 + k1)
            return 0

        lax.fori_loop(0, HALF, combine, 0)

        there = []
        for d in range(1, 8):
            q = lax.rem(chip + d, 8)
            cp = pltpu.make_async_remote_copy(
                items.at[it, rows(8 * q, 8)], got.at[it, chip],
                there_send.at[it, d], there_recv.at[it, d], device_id=(2 * q + core, sp), device_id_type=MESH,
            )
            cp.start()
            there.append(cp)
        got[it, chip] = items[it, rows(8 * chip, 8), :]
        if it == 1:
            out_e[rows(HALF * core, HALF), :] = ends[1, core]
        for cp in there:
            cp.wait_recv()
        sends += there

        def recur(t, _):
            c = gain[rows(8 * chip + t + HALO, 1), :]
            c2 = c * c
            total = got[it, 7, rows(t, 1), :]
            sums[it, 0, rows(t, 1), :] = total
            for k in range(7):
                total = c2 * total + got[it, k, rows(t, 1), :]
                sums[it, k + 1, rows(t, 1), :] = total
            return 0

        lax.fori_loop(0, 8, recur, 0)

        back = []
        for d in range(1, 8):
            q = lax.rem(chip + d, 8)
            cp = pltpu.make_async_remote_copy(
                sums.at[it, q], starts.at[it + 1, 0, rows(8 * chip + HALO, 8)],
                back_send.at[it, d], back_recv.at[it, d], device_id=(2 * q + core, sp), device_id_type=MESH,
            )
            cp.start()
            back.append(cp)
        starts[it + 1, 0, rows(8 * chip + HALO, 8), :] = sums[it, chip]
        if it == 1:
            cp_e.wait_recv()
            for s in range(8):
                in_a[0, pl.ds(128 * s, 128), :] = out_e[pl.ds(s, 128, stride=8), :].T
            store_e = pltpu.make_async_copy(in_a, ends_hbm, out_sem.at[0])
            store_e.start()
        for cp in back:
            cp.wait_recv()
        sends += back

        def spread(t, _):
            c = gain[rows(t + HALO, 1), :]
            starts[it + 1, 1, rows(t + HALO, 1), :] = (
                c * starts[it + 1, 0, rows(t + HALO, 1), :] + corr0[rows(t, 1), :]
            )
            return 0

        lax.fori_loop(0, HALF, spread, 0)

        if it == 0:
            halos = []
            for n in range(2):
                if n == 0:
                    target = (jnp.where(core == 0, pair + 1, pair), jnp.where(core == 0, left, sp))
                    src, dst = rows(HALO, 6), rows(OWN, 6)
                else:
                    target = (jnp.where(core == 0, pair + 1, pair), jnp.where(core == 0, sp, right))
                    src, dst = rows(HALF, 6), rows(0, 6)
                cp = pltpu.make_async_remote_copy(
                    starts.at[1, :, src], starts.at[1, :, dst],
                    halo_send.at[n], halo_recv.at[n], device_id=target, device_id_type=MESH,
                )
                cp.start()
                halos.append(cp)
            for cp in halos:
                cp.wait_recv()
            sends += halos

    cp_s = pltpu.make_async_remote_copy(
        starts.at[2, other, rows(HALO, HALF)], out_s.at[rows(HALF * core, HALF)],
        out_send.at[1], out_recv.at[1], device_id=(pair + other, sp), device_id_type=MESH,
    )
    cp_s.start()
    sends.append(cp_s)
    out_s[rows(HALF * core, HALF), :] = starts[2, core, rows(HALO, HALF), :]
    cp_s.wait_recv()
    for s in range(8):
        in_j[0, pl.ds(128 * s, 128), :] = out_s[pl.ds(s, 128, stride=8), :].T
    store_s = pltpu.make_async_copy(in_j, starts_hbm, out_sem.at[1])
    store_s.start()
    for cp in sends + pairs:
        cp.wait_send()
    store_e.wait()
    store_s.wait()


def local(initial_starts, source, region, base_reluctivity, saturation, mobility):
    block = jax.ShapeDtypeStruct((1, 1024, 128), F32)
    smem = pl.BlockSpec(memory_space=pltpu.SMEM)
    hbm = pl.BlockSpec(memory_space=pl.ANY)
    big = lambda *lead: pltpu.VMEM(lead + (1024, 128), F32)
    frame = lambda *lead: pltpu.VMEM(lead + (FRAME * ROWS, 128), F32)
    half = lambda *lead: pltpu.VMEM(lead + (HALF * ROWS, 128), F32)
    sem = lambda *shape: pltpu.SemaphoreType.DMA(shape)
    return pl.pallas_call(
        kernel,
        out_shape=(block, block),
        in_specs=[smem] * 3 + [hbm] * 3,
        out_specs=(hbm, hbm),
        scratch_shapes=[
            big(1), big(1), pltpu.VMEM((1024, 128), jnp.int32), big(), big(), pltpu.VMEM((1024, 128), jnp.int32),
            frame(3, 2), frame(2), pltpu.VMEM((FRAME * ROWS, 128), jnp.int32),
            frame(), frame(), frame(), frame(),
            frame(2), half(2, 2), half(), half(2), pltpu.VMEM((2, 8, 64, 128), F32), pltpu.VMEM((2, 8, 64, 128), F32),
            big(), big(),
            sem(3), sem(2), sem(2), sem(2, 2), sem(2, 2), pltpu.SemaphoreType.DMA, pltpu.SemaphoreType.DMA,
            sem(2, 8), sem(2, 8), sem(2, 8), sem(2, 8), sem(2), sem(2), sem(2), sem(2), sem(2),
        ],
        compiler_params=pltpu.CompilerParams(
            collective_id=0, has_side_effects=True, vmem_limit_bytes=40 * 2**20
        ),
        name="parareal",
    )(base_reluctivity, saturation, mobility, initial_starts, source, region)


def solution(mesh):
    in_specs = (P("tm", None, "space"), P("tm", None, "space"), P(None, "space"), P(), P(), P())
    out_specs = (P("tm", None, "space"), P("tm", None, "space"))
    return jax.shard_map(local, mesh=mesh, in_specs=in_specs, out_specs=out_specs, check_vma=False)
```

```python
import jax
import jax.numpy as jnp
from jax import lax
from jax.experimental import pallas as pl
from jax.experimental.pallas import tpu as pltpu
from jax.sharding import PartitionSpec as P

MESH = pl.DeviceIdType.MESH
HALF = 64
OWN = 72
PAD = 8
MID = 16
ROWS = 96
F32 = jnp.float32
OFFSETS = ((1, 2), (1, 1), (1, 3), (0, 2), (1, 0), (0, 1), (0, 3))


def part(start, size):
    if not isinstance(start, int):
        start = pl.multiple_of(start, 8)
    return pl.ds(start, size)


def kernel(
    base_hbm, satur_hbm, mob_hbm, a_hbm, j_hbm, r_hbm, starts_hbm, ends_hbm,
    base_ref, satur_ref, mob_ref, in_a, in_j, in_r, ta, tj, tr, starts, drive, regions,
    coef_a, coef_b, mobile, gain, reluct, work, ends, corr0, items, got, sums, out_e, out_s,
    in_sem, pair_send, pair_recv, edge_send, edge_recv, reg_send, reg_recv,
    there_send, there_recv, back_send, back_recv, halo_send, halo_recv, out_send, out_recv, out_sem,
):
    tm = lax.axis_index("tm")
    sp = lax.axis_index("space")
    core = lax.rem(tm, 2)
    other = 1 - core
    pair = tm - core
    chip = tm // 2
    right = lax.rem(sp + 1, 16)
    left = lax.rem(sp + 15, 16)
    outer = jnp.where(core == 0, left, right)
    ahead = jnp.where(core == 0, right, left)

    def far(dy, dx):
        return 4 * lax.rem(chip // 4 + dy, 2) + lax.rem(lax.rem(chip, 4) + dx, 4)

    loads = []
    for n, (src, dst) in enumerate(
        ((r_hbm, in_r), (a_hbm, in_a), (j_hbm, in_j), (base_hbm, base_ref), (satur_hbm, satur_ref), (mob_hbm, mob_ref))
    ):
        cp = pltpu.make_async_copy(src, dst, in_sem.at[n])
        cp.start()
        loads.append(cp)

    barrier = pltpu.get_barrier_semaphore()
    for dy, dx in OFFSETS:
        pl.semaphore_signal(barrier, inc=1, device_id=(2 * far(dy, dx) + core, sp), device_id_type=MESH)
    pl.semaphore_signal(barrier, inc=1, device_id=(pair, outer), device_id_type=MESH)
    pl.semaphore_signal(barrier, inc=1, device_id=(pair + 1, outer), device_id_type=MESH)
    pl.semaphore_signal(barrier, inc=1, device_id=(pair + other, sp), device_id_type=MESH)

    def turn(src, dst):
        for t in range(8):
            dst[t] = src[pl.ds(t, 128, stride=8), :].T

    own = part(MID - PAD * core, OWN)
    mine = part((128 - OWN) * core, OWN)
    edge = part(jnp.where(core == 0, PAD, MID + HALF), 8)

    loads[0].wait()
    turn(in_r, tr)
    for cp in loads[3:]:
        cp.wait()
    base = [base_ref[k] for k in range(8)]
    satur = [satur_ref[k] for k in range(8)]
    full = lambda x: jnp.full((8, 128), x, F32)
    tab_a = [full(0.5 * b * (1.0 + s)) for b, s in zip(base, satur)]
    tab_b = [full(2.0 * b * s) for b, s in zip(base, satur)]
    tab_m = [full(mob_ref[k]) for k in range(8)]
    tab_c = [1.0 / (1.0 + 12.0 * m * full(b)) for b, m in zip(base, tab_m)]

    def look_up(src, first, at, size):
        for t in range(8):
            for k in range(size // 8):
                r = src[t, part(first + 8 * k, 8)]
                bits = [(r & 1) != 0, (r & 2) != 0, (r & 4) != 0]
                for tab, ref in ((tab_a, coef_a), (tab_b, coef_b), (tab_m, mobile), (tab_c, gain)):
                    level = tab
                    for bit in bits:
                        level = [jnp.where(bit, hi, lo) for lo, hi in zip(level[::2], level[1::2])]
                    ref[t, part(at + 8 * k, 8)] = level[0]

    look_up(tr, (128 - OWN) * core, MID - PAD * core, OWN)
    loads[1].wait()
    turn(in_a.at[0], ta)
    starts[0, core, :, own] = ta[:, mine]
    loads[2].wait()
    turn(in_j.at[0], tj)
    drive[core, :, own] = tj[:, mine]

    pl.semaphore_wait(barrier, 10)

    sends = []
    pairs = []
    for n, (src, dst) in enumerate(((ta, starts.at[0]), (tj, drive))):
        cp = pltpu.make_async_remote_copy(
            src.at[:, pl.ds(120, 8)], dst.at[core, :, pl.ds(PAD, 8)],
            edge_send.at[n, 0], edge_recv.at[n, core], device_id=(pair, right), device_id_type=MESH,
        )
        cp.start()
        sends.append(cp)
        cp = pltpu.make_async_remote_copy(
            src.at[:, pl.ds(0, 8)], dst.at[core, :, pl.ds(MID + HALF, 8)],
            edge_send.at[n, 1], edge_recv.at[n, core], device_id=(pair + 1, left), device_id_type=MESH,
        )
        cp.start()
        sends.append(cp)
        if n == 0:
            cp_reg = pltpu.make_async_remote_copy(
                tr.at[:, part(120 * other, 8)], regions.at[:, part(jnp.where(core == 0, 0, 8), 8)],
                reg_send, reg_recv, device_id=(tm, ahead), device_id_type=MESH,
            )
            cp_reg.start()
            sends.append(cp_reg)
        cp = pltpu.make_async_remote_copy(
            src.at[:, part((128 - OWN) * other, OWN)], dst.at[core, :, own_of(core)],
            pair_send.at[n], pair_recv.at[n], device_id=(pair + other, sp), device_id_type=MESH,
        )
        cp.start()
        pairs.append(cp)

    cp_reg.wait_recv()
    look_up(regions, jnp.where(core == 0, 0, 8), jnp.where(core == 0, PAD, MID + HALF), 8)

    lane = lambda size: lax.broadcasted_iota(jnp.int32, (size, 128), 1)

    def up(x, end):
        return jnp.where(lane(x.shape[0]) == 127, end, pltpu.roll(x, 127, 1))

    def down(x, end):
        return jnp.where(lane(x.shape[0]) == 0, end, pltpu.roll(x, 1, 1))

    def fine(src, dst, at, size, to):
        wide = pl.ds(PAD, 80)
        mid, east, west = pl.ds(at, size), pl.ds(at + 1, size), pl.ds(at - 1, size)
        out = pl.ds(to, size)
        for p in range(2):
            a = [src.at[p, t] for t in range(8)]
            for t in range(8):
                north = a[t + 1][wide] if t < 7 else up(a[0][wide], 0.0)
                south = a[t - 1][wide] if t > 0 else down(a[7][wide], 0.0)
                br = north - south
                bt = a[t][pl.ds(PAD + 1, 80)] - a[t][pl.ds(PAD - 1, 80)]
                reluct[t, wide] = coef_a[t, wide] - coef_b[t, wide] / (4.0 + (br * br + bt * bt))
            nu0, nu7, a0, a7 = reluct[0, mid], reluct[7, mid], a[0][mid], a[7][mid]
            top = (nu7 + up(nu0, nu7)) * (up(a0, 0.0) - a7)
            below = down(top, 2.0 * nu0 * a0)
            for t in range(8):
                nu, here = reluct[t, mid], a[t][mid]
                above = top if t == 7 else (nu + reluct[t + 1, mid]) * (a[t + 1][mid] - here)
                turned = (nu + reluct[t, east]) * (a[t][east] - here) + (nu + reluct[t, west]) * (a[t][west] - here)
                total = turned + (above - below) + drive[p, t, mid]
                dst[p, t, out] = here + mobile[t, mid] * total
                below = above

    for cp in pairs:
        cp.wait_recv()
    for n in range(2):
        for p in range(2):
            pltpu.make_async_remote_copy(
                ta.at[:, pl.ds(0, 8)], starts.at[0, 0, :, pl.ds(PAD, 8)],
                edge_send.at[n, 0], edge_recv.at[n, p], device_id=(tm, right), device_id_type=MESH,
            ).wait_recv()

    inner = pl.ds(MID, HALF)
    for it in range(2):
        fine(starts.at[it], work.at[0], PAD, 80, PAD)
        fine(work.at[0], work.at[1], PAD, 80, PAD)
        fine(work.at[1], ends.at[it], MID, HALF, 0)

        if it == 1:
            cp_e = pltpu.make_async_remote_copy(
                ends.at[1, other], out_e.at[:, part(HALF * core, HALF)],
                out_send.at[0], out_recv.at[0], device_id=(pair + other, sp), device_id_type=MESH,
            )
            cp_e.start()
            sends.append(cp_e)

        for t in range(8):
            c = gain[t, inner]
            e0, e1 = ends[it, 0, t], ends[it, 1, t]
            k0 = e0 - c * starts[it, 0, t, inner]
            k1 = e1 - c * starts[it, 1, t, inner]
            corr0[t] = k0
            items[it, t] = jnp.where(chip == 7, e1, c * k0 + k1)

        there = []
        for n, (dy, dx) in enumerate(OFFSETS):
            q = far(dy, dx)
            cp = pltpu.make_async_remote_copy(
                items.at[it, :, part(8 * q, 8)], got.at[it, chip],
                there_send.at[it, n], there_recv.at[it, n], device_id=(2 * q + core, sp), device_id_type=MESH,
            )
            cp.start()
            there.append(cp)
        got[it, chip] = items[it, :, part(8 * chip, 8)]
        c = gain[:, part(8 * chip + MID, 8)]
        c2 = c * c
        if it == 1:
            out_e[:, part(HALF * core, HALF)] = ends[1, core]
        for cp in there:
            cp.wait_recv()
        sends += there

        total = got[it, 7]
        sums[it, 0] = total
        for k in range(7):
            total = c2 * total + got[it, k]
            sums[it, k + 1] = total

        back = []
        for n, (dy, dx) in enumerate(OFFSETS):
            q = far(dy, dx)
            cp = pltpu.make_async_remote_copy(
                sums.at[it, q], starts.at[it + 1, 0, :, part(8 * chip + MID, 8)],
                back_send.at[it, n], back_recv.at[it, n], device_id=(2 * q + core, sp), device_id_type=MESH,
            )
            cp.start()
            back.append(cp)
        starts[it + 1, 0, :, part(8 * chip + MID, 8)] = sums[it, chip]
        if it == 1:
            cp_e.wait_recv()
            for t in range(8):
                in_a[0, pl.ds(t, 128, stride=8), :] = out_e[t].T
            store_e = pltpu.make_async_copy(in_a, ends_hbm, out_sem.at[0])
            store_e.start()
        for cp in back:
            cp.wait_recv()
        sends += back

        for t in range(8):
            starts[it + 1, 1, t, inner] = gain[t, inner] * starts[it + 1, 0, t, inner] + corr0[t]

        if it == 0:
            halos = []
            for n in range(2):
                if n == 0:
                    target = (jnp.where(core == 0, pair + 1, pair), jnp.where(core == 0, left, sp))
                    src, dst = pl.ds(MID, 8), pl.ds(MID + HALF, 8)
                else:
                    target = (jnp.where(core == 0, pair + 1, pair), jnp.where(core == 0, sp, right))
                    src, dst = pl.ds(MID + HALF - 8, 8), pl.ds(PAD, 8)
                cp = pltpu.make_async_remote_copy(
                    starts.at[1, :, :, src], starts.at[1, :, :, dst],
                    halo_send.at[n], halo_recv.at[n], device_id=target, device_id_type=MESH,
                )
                cp.start()
                halos.append(cp)
            for cp in halos:
                cp.wait_recv()
            sends += halos

    cp_s = pltpu.make_async_remote_copy(
        starts.at[2, other, :, inner], out_s.at[:, part(HALF * core, HALF)],
        out_send.at[1], out_recv.at[1], device_id=(pair + other, sp), device_id_type=MESH,
    )
    cp_s.start()
    sends.append(cp_s)
    out_s[:, part(HALF * core, HALF)] = starts[2, core, :, inner]
    cp_s.wait_recv()
    for t in range(8):
        in_j[0, pl.ds(t, 128, stride=8), :] = out_s[t].T
    store_s = pltpu.make_async_copy(in_j, starts_hbm, out_sem.at[1])
    store_s.start()
    for cp in sends + pairs:
        cp.wait_send()
    store_e.wait()
    store_s.wait()


def own_of(sender):
    return part(MID - PAD * (1 - sender), OWN)


def local(initial_starts, source, region, base_reluctivity, saturation, mobility):
    block = jax.ShapeDtypeStruct((1, 1024, 128), F32)
    hbm = pl.BlockSpec(memory_space=pltpu.HBM)
    vmem = lambda *shape: pltpu.VMEM(shape + (128,), F32)
    ints = lambda *shape: pltpu.VMEM(shape + (128,), jnp.int32)
    table = pltpu.SMEM((8,), F32)
    sem = lambda *shape: pltpu.SemaphoreType.DMA(shape)
    return pl.pallas_call(
        kernel,
        out_shape=(block, block),
        in_specs=[hbm] * 6,
        out_specs=(hbm, hbm),
        scratch_shapes=[
            table, table, table,
            vmem(1, 1024), vmem(1, 1024), ints(1024), vmem(8, 128), vmem(8, 128), ints(8, 128),
            vmem(3, 2, 8, ROWS), vmem(2, 8, ROWS), ints(8, 16),
            vmem(8, ROWS), vmem(8, ROWS), vmem(8, ROWS), vmem(8, ROWS), vmem(8, ROWS),
            vmem(2, 2, 8, ROWS), vmem(2, 2, 8, HALF), vmem(8, HALF), vmem(2, 8, HALF), vmem(2, 8, 8, 8), vmem(2, 8, 8, 8),
            vmem(8, 128), vmem(8, 128),
            sem(6), sem(2), sem(2), sem(2, 2), sem(2, 2), pltpu.SemaphoreType.DMA, pltpu.SemaphoreType.DMA,
            sem(2, 7), sem(2, 7), sem(2, 7), sem(2, 7), sem(2), sem(2), sem(2), sem(2), sem(2),
        ],
        compiler_params=pltpu.CompilerParams(
            collective_id=0, has_side_effects=True, vmem_limit_bytes=64 * 2**20
        ),
        name="parareal",
    )(base_reluctivity, saturation, mobility, initial_starts, source, region)


def solution(mesh):
    in_specs = (P("tm", None, "space"), P("tm", None, "space"), P(None, "space"), P(), P(), P())
    out_specs = (P("tm", None, "space"), P("tm", None, "space"))
    return jax.shard_map(local, mesh=mesh, in_specs=in_specs, out_specs=out_specs, check_vma=False)
```

```python
import jax
import jax.numpy as jnp
from jax import lax
from jax.experimental import pallas as pl
from jax.experimental.pallas import tpu as pltpu
from jax.sharding import PartitionSpec as P

MESH = pl.DeviceIdType.MESH
HALF = 64
OWN = 72
PAD = 8
MID = 16
ROWS = 96
EDGE = 40
F32 = jnp.float32
OFFSETS = ((1, 2), (1, 1), (1, 3), (0, 2), (1, 0), (0, 1), (0, 3))


def part(start, size):
    if not isinstance(start, int):
        start = pl.multiple_of(start, 8)
    return pl.ds(start, size)


def up(x, end):
    return jnp.where(lax.broadcasted_iota(jnp.int32, x.shape, 1) == 127, end, pltpu.roll(x, 127, 1))


def down(x, end):
    return jnp.where(lax.broadcasted_iota(jnp.int32, x.shape, 1) == 0, end, pltpu.roll(x, 1, 1))


def reluctivity(a, coef_a, coef_b, nu, at, size):
    rows = pl.ds(at, size)
    for t in range(8):
        north = a[t + 1][rows] if t < 7 else up(a[0][rows], 0.0)
        south = a[t - 1][rows] if t > 0 else down(a[7][rows], 0.0)
        br = north - south
        bt = a[t][pl.ds(at + 1, size)] - a[t][pl.ds(at - 1, size)]
        nu[t][rows] = coef_a[t, rows] - coef_b[t, rows] / (4.0 + (br * br + bt * bt))


def turning(a, nu, at, size):
    here, mid = a[pl.ds(at, size)], nu[pl.ds(at, size)]
    flux = (mid + nu[pl.ds(at + 1, size)]) * (a[pl.ds(at + 1, size)] - here)
    return flux + (mid + nu[pl.ds(at - 1, size)]) * (a[pl.ds(at - 1, size)] - here)


def update(a, nu, drive, mobile, at, size, put):
    rows = pl.ds(at, size)
    nu0, nu7, a0, a7 = nu[0][rows], nu[7][rows], a[0][rows], a[7][rows]
    top = (nu7 + up(nu0, nu7)) * (up(a0, 0.0) - a7)
    below = down(top, 2.0 * nu0 * a0)
    for t in range(8):
        here = a[t][rows]
        above = top if t == 7 else (nu[t][rows] + nu[t + 1][rows]) * (a[t + 1][rows] - here)
        total = turning(a[t], nu[t], at, size) + (above - below) + drive[t, rows]
        put(t, here + mobile[t, rows] * total)
        below = above


def kernel(
    base_hbm, satur_hbm, mob_hbm, a_hbm, j_hbm, r_hbm, out_s, out_e,
    base_ref, satur_ref, mob_ref, in_a, in_j, in_r, ta, tj, tr, starts, drive,
    coef_a, coef_b, mobile, gain, reluct, work, later,
    rim_r, rim, rim_drive, rim_a, rim_b, rim_mobile, rim_gain, rim_reluct, rim_work, rim_later, rim_items, rim_got,
    ends, corr0, items, got, sums,
    in_sem, pair_send, pair_recv, edge_send, edge_recv, reg_send, reg_recv,
    there_send, there_recv, back_send, back_recv, rim_send, rim_recv, halo_send, halo_recv,
    oute_send, oute_recv, outs_send, outs_recv,
):
    tm = lax.axis_index("tm")
    sp = lax.axis_index("space")
    core = lax.rem(tm, 2)
    other = 1 - core
    pair = tm - core
    chip = tm // 2
    right = lax.rem(sp + 1, 16)
    left = lax.rem(sp + 15, 16)
    outer = jnp.where(core == 0, left, right)
    partner = (pair + other, sp)
    beyond = (pair + other, outer)

    def far(dy, dx):
        return 4 * lax.rem(chip // 4 + dy, 2) + lax.rem(lax.rem(chip, 4) + dx, 4)

    def source(dy, dx):
        return far(dy, (4 - dx) % 4)

    def remote(src, dst, send, recv, target):
        return pltpu.make_async_remote_copy(src, dst, send, recv, device_id=target, device_id_type=MESH)

    loads = []
    for n, (src, dst) in enumerate(
        ((a_hbm, in_a), (j_hbm, in_j), (r_hbm, in_r), (base_hbm, base_ref), (satur_hbm, satur_ref), (mob_hbm, mob_ref))
    ):
        cp = pltpu.make_async_copy(src, dst, in_sem.at[n])
        cp.start()
        loads.append(cp)

    barrier = pltpu.get_barrier_semaphore()
    for dy, dx in OFFSETS:
        pl.semaphore_signal(barrier, inc=1, device_id=(2 * far(dy, dx) + core, sp), device_id_type=MESH)
    pl.semaphore_signal(barrier, inc=1, device_id=(pair, outer), device_id_type=MESH)
    pl.semaphore_signal(barrier, inc=1, device_id=(pair + 1, outer), device_id_type=MESH)
    pl.semaphore_signal(barrier, inc=1, device_id=partner, device_id_type=MESH)

    def turn(src, dst):
        for t in range(8):
            dst[t] = src[pl.ds(t, 128, stride=8), :].T

    sends = []

    def go(cp):
        cp.start()
        sends.append(cp)
        return cp

    own = part(MID - PAD * core, OWN)
    mine = part((128 - OWN) * core, OWN)
    theirs = part((128 - OWN) * other, OWN)
    theirs_at = part(MID - PAD * other, OWN)
    rim_halo = part(PAD + 16 * core, 8)
    rim_own = part(16 - 8 * core, 16)
    rim_from = part(MID + 48 * core, 16)
    far_halo = part(PAD + 72 * core, 8)
    rim_ends = part(56 * core, 8)

    loads[0].wait()
    turn(in_a.at[0], ta)
    pl.semaphore_wait(barrier, 10)

    def send_edges(n, src, dst):
        go(remote(src.at[:, pl.ds(120, 8)], dst.at[core, :, pl.ds(8, 8)], edge_send.at[n, 0], edge_recv.at[n, core], (pair, right)))
        go(remote(src.at[:, pl.ds(0, 8)], dst.at[core, :, pl.ds(24, 8)], edge_send.at[n, 1], edge_recv.at[n, core], (pair + 1, left)))

    send_edges(0, ta, rim)
    loads[1].wait()
    turn(in_j.at[0], tj)
    send_edges(1, tj, rim_drive)
    loads[2].wait()
    turn(in_r, tr)
    cp_reg = go(
        remote(tr.at[:, part(120 * other, 8)], rim_r.at[:, part(8 + 16 * core, 8)], reg_send, reg_recv, (tm, jnp.where(core == 0, right, left)))
    )
    pairs = [
        go(remote(src.at[:, theirs], dst.at[core, :, theirs_at], pair_send.at[n], pair_recv.at[n], partner))
        for n, (src, dst) in enumerate(((ta, starts.at[0]), (tj, drive)))
    ]

    for cp in loads[3:]:
        cp.wait()
    base = [base_ref[k] for k in range(8)]
    satur = [satur_ref[k] for k in range(8)]
    full = lambda x: jnp.full((8, 128), x, F32)
    tab_a = [full(0.5 * b * (1.0 + s)) for b, s in zip(base, satur)]
    tab_b = [full(2.0 * b * s) for b, s in zip(base, satur)]
    tab_m = [full(mob_ref[k]) for k in range(8)]
    tab_c = [1.0 / (1.0 + 12.0 * m * full(b)) for b, m in zip(base, tab_m)]

    def look_up(src, first, size, put):
        for t in range(8):
            for k in range(0, size, 8):
                r = src[t, part(first + k, 8)]
                bits = [(r & 1) != 0, (r & 2) != 0, (r & 4) != 0]
                for n, tab in enumerate((tab_a, tab_b, tab_m, tab_c)):
                    level = tab
                    for bit in bits:
                        level = [jnp.where(bit, hi, lo) for lo, hi in zip(level[::2], level[1::2])]
                    put(n, t, k, level[0])

    coefs = (coef_a, coef_b, mobile, gain)
    rim_coefs = (rim_a, rim_b, rim_mobile, rim_gain)

    def put_own(n, t, k, x):
        coefs[n][t, part(MID - PAD * core + k, 8)] = x

    def put_rim(n, t, k, x):
        rim_coefs[n][t, rim_halo] = x
        coefs[n][t, far_halo] = x

    look_up(tr, (128 - OWN) * core, OWN, put_own)
    starts[0, core, :, own] = ta[:, mine]
    drive[core, :, own] = tj[:, mine]

    inner = pl.ds(MID, HALF)
    chip7 = chip == 7

    def phases(ref):
        return [ref.at[t] for t in range(8)]

    nus = [reluct.at[t + 1] for t in range(8)]
    lates = [later.at[t + 1] for t in range(8)]

    def put_work(t, x):
        work[t, pl.ds(PAD, 80)] = x

    def put_later(t, x):
        later[t + 1, pl.ds(PAD, 80)] = x

    def two_steps(it, p):
        a = phases(starts.at[it, p])
        reluctivity(a, coef_a, coef_b, nus, PAD, 80)
        update(a, nus, drive.at[p], mobile, PAD, 80, put_work)
        a = phases(work)
        reluctivity(a, coef_a, coef_b, nus, PAD, 80)
        update(a, nus, drive.at[p], mobile, PAD, 80, put_later)
        reluctivity(lates, coef_a, coef_b, nus, PAD, 80)

    def last_step(p, t):
        here, mid = later[t + 1, inner], reluct[t + 1, inner]
        total = turning(later.at[t + 1], reluct.at[t + 1], MID, HALF) + drive[p, t, inner]
        total += (mid + reluct[t + 2, inner]) * (later[t + 2, inner] - here)
        total += (mid + reluct[t, inner]) * (later[t, inner] - here)
        return here + mobile[t, inner] * total

    for it in range(2):
        def put_ends(t, x):
            ends[it, core, t] = x
            if it == 1:
                out_e[t, part(HALF * core, HALF)] = x

        two_steps(it, core)
        update(lates, nus, drive.at[core], mobile, MID, HALF, put_ends)
        if it == 0:
            for cp in pairs:
                cp.wait_recv()
        two_steps(it, other)
        wide = pl.ds(PAD, 80)
        later[0, wide] = down(later[8, wide], 0.0)
        later[9, wide] = up(later[1, wide], 0.0)
        reluct[0, wide] = down(reluct[8, wide], reluct[1, wide])
        reluct[9, wide] = up(reluct[1, wide], reluct[8, wide])

        window = part(8 * other, 56) if it == 0 else pl.ds(0, HALF)
        frame_window = part(MID + 8 * other, 56) if it == 0 else inner

        def finish(t):
            theirs_end = last_step(other, t)
            ends[it, other, t] = theirs_end
            own_end = ends[it, core, t]
            c = gain[t, inner]
            own_corr = own_end - c * starts[it, core, t, inner]
            theirs_corr = theirs_end - c * starts[it, other, t, inner]
            first = jnp.where(core == 0, own_corr, theirs_corr)
            second = jnp.where(core == 0, theirs_corr, own_corr)
            corr0[it, t] = first
            items[it, t] = jnp.where(chip7, jnp.where(core == 0, theirs_end, own_end), c * first + second)

        there = []
        for n, (dy, dx) in enumerate(OFFSETS):
            q = far(dy, dx)
            finish(q)
            there.append(
                go(remote(items.at[it, q, window], got.at[it, chip, window], there_send.at[it, n], there_recv.at[it, n], (2 * q + core, sp)))
            )
        finish(chip)
        got[it, chip] = items[it, chip]

        if it == 1:
            cp_e = go(remote(ends.at[1, other], out_e.at[:, part(HALF * core, HALF)], oute_send, oute_recv, partner))
        else:
            cp_reg.wait_recv()
            look_up(rim_r, PAD + 16 * core, 8, put_rim)
            for ref, into in zip(coefs, rim_coefs):
                into[:, rim_own] = ref[:, rim_from]
            for n in range(2):
                for p in range(2):
                    remote(
                        ta.at[:, pl.ds(0, 8)], rim.at[0, :, pl.ds(8, 8)], edge_send.at[n, 0], edge_recv.at[n, p], partner
                    ).wait_recv()
            rim_nus = phases(rim_reluct)
            for p in range(2):
                rim[p, :, rim_own] = starts[0, p, :, rim_from]
                rim_drive[p, :, rim_own] = drive[p, :, rim_from]
                drive[p, :, far_halo] = rim_drive[p, :, rim_halo]

                def put_rim_work(t, x):
                    rim_work[t, pl.ds(8, 24)] = x

                def put_rim_later(t, x):
                    rim_later[t, pl.ds(8, 24)] = x

                def put_rim_ends(t, x):
                    ends[0, p, t, rim_ends] = x

                for a, put in ((rim.at[p], put_rim_work), (rim_work, put_rim_later)):
                    reluctivity(phases(a), rim_a, rim_b, rim_nus, 8, 24)
                    update(phases(a), rim_nus, rim_drive.at[p], rim_mobile, 8, 24, put)
                reluctivity(phases(rim_later), rim_a, rim_b, rim_nus, 8, 24)
                update(phases(rim_later), rim_nus, rim_drive.at[p], rim_mobile, 16, 8, put_rim_ends)
            rim_c = gain[:, part(MID + 56 * core, 8)]
            k0 = ends[0, 0, :, rim_ends] - rim_c * starts[0, 0, :, part(MID + 56 * core, 8)]
            k1 = ends[0, 1, :, rim_ends] - rim_c * starts[0, 1, :, part(MID + 56 * core, 8)]
            corr0[0, :, rim_ends] = k0
            rim_items[...] = jnp.where(chip7, ends[0, 1, :, rim_ends], rim_c * k0 + k1)
            rim_got[chip] = rim_items[...]

            def rim_copy(n):
                q = far(*OFFSETS[n])
                return remote(rim_items, rim_got.at[chip], rim_send.at[n], rim_recv.at[n], (2 * q + core, sp))

            for n, offset in enumerate(OFFSETS):
                @pl.when((far(*offset) > chip) | chip7)
                def _():
                    rim_copy(n).start()

        for cp in there:
            cp.wait_recv()
        c = gain[chip, frame_window]
        c2 = c * c
        total = got[it, 7, window]
        sums[it, 0, window] = total
        for k in range(7):
            total = c2 * total + got[it, k, window]
            sums[it, k + 1, window] = total
        back = []
        for n, (dy, dx) in enumerate(OFFSETS):
            q = far(dy, dx)
            back.append(
                go(remote(sums.at[it, q, window], starts.at[it + 1, 0, chip, frame_window], back_send.at[it, n], back_recv.at[it, n], (2 * q + core, sp)))
            )
        starts[it + 1, 0, chip, frame_window] = sums[it, chip, window]

        if it == 0:
            for n, (dy, dx) in enumerate(OFFSETS):
                @pl.when((source(dy, dx) < chip) | (source(dy, dx) == 7))
                def _():
                    rim_copy(n).wait_recv()
            rim_c2 = rim_c * rim_c
            total = rim_got[7]
            for k in range(7):
                total = jnp.where(k < chip, rim_c2 * total + rim_got[k], total)
            starts[1, 0, :, part(MID + 56 * core, 8)] = total
            starts[1, 1, :, part(MID + 56 * core, 8)] = rim_c * total + k0
            outer_halo = go(
                remote(starts.at[1, :, :, part(MID + 56 * core, 8)], starts.at[1, :, :, part(PAD + 72 * other, 8)], halo_send.at[0], halo_recv.at[0], beyond)
            )

        def spread(t):
            starts[it + 1, 1, t, frame_window] = gain[t, frame_window] * starts[it + 1, 0, t, frame_window] + corr0[it, t, window]

        if it == 0:
            spread(chip)
            for n in reversed(range(7)):
                back[n].wait_recv()
                spread(source(*OFFSETS[n]))
            inner_halo = go(
                remote(starts.at[1, :, :, part(MID + 56 * other, 8)], starts.at[1, :, :, part(PAD + 72 * core, 8)], halo_send.at[1], halo_recv.at[1], partner)
            )
            outer_halo.wait_recv()
            inner_halo.wait_recv()
        else:
            outs = []
            for n in reversed(range(8)):
                t = chip
                if n < 7:
                    back[n].wait_recv()
                    t = source(*OFFSETS[n])
                spread(t)
                outs.append(
                    go(remote(starts.at[2, other, t, inner], out_s.at[t, part(HALF * core, HALF)], outs_send.at[n], outs_recv.at[n], partner))
                )
                out_s[t, part(HALF * core, HALF)] = starts[2, core, t, inner]

    cp_e.wait_recv()
    for cp in outs:
        cp.wait_recv()
    for cp in sends:
        cp.wait_send()
    for n, offset in enumerate(OFFSETS):
        @pl.when((far(*offset) > chip) | chip7)
        def _():
            rim_copy(n).wait_send()


def hand_out(s_ref, e_ref, starts_hbm, ends_hbm, buf, sem):
    copies = []
    for n, (src, dst) in enumerate(((e_ref, ends_hbm), (s_ref, starts_hbm))):
        for t in range(8):
            buf[n, 0, pl.ds(t, 128, stride=8), :] = src[t].T
        cp = pltpu.make_async_copy(buf.at[n], dst, sem.at[n])
        cp.start()
        copies.append(cp)
    for cp in copies:
        cp.wait()


def local(initial_starts, source, region, base_reluctivity, saturation, mobility):
    held = jax.ShapeDtypeStruct((8, 128, 128), F32)
    block = jax.ShapeDtypeStruct((1, 1024, 128), F32)
    hbm = pl.BlockSpec(memory_space=pltpu.HBM)
    in_vmem = pl.BlockSpec(memory_space=pltpu.VMEM)
    vmem = lambda *shape: pltpu.VMEM(shape + (128,), F32)
    ints = lambda *shape: pltpu.VMEM(shape + (128,), jnp.int32)
    table = pltpu.SMEM((8,), F32)
    sem = lambda *shape: pltpu.SemaphoreType.DMA(shape)
    one = pltpu.SemaphoreType.DMA
    args = (base_reluctivity, saturation, mobility, initial_starts, source, region)
    kept = pl.pallas_call(
        kernel,
        out_shape=(held, held),
        in_specs=[hbm] * 6,
        out_specs=(in_vmem, in_vmem),
        scratch_shapes=[
            table, table, table,
            vmem(1, 1024), vmem(1, 1024), ints(1024), vmem(8, 128), vmem(8, 128), ints(8, 128),
            vmem(3, 2, 8, ROWS), vmem(2, 8, ROWS),
            vmem(8, ROWS), vmem(8, ROWS), vmem(8, ROWS), vmem(8, ROWS), vmem(10, ROWS), vmem(8, ROWS), vmem(10, ROWS),
            ints(8, EDGE), vmem(2, 8, EDGE), vmem(2, 8, EDGE), vmem(8, EDGE), vmem(8, EDGE), vmem(8, EDGE), vmem(8, EDGE),
            vmem(8, EDGE), vmem(8, EDGE), vmem(8, EDGE), vmem(8, 8), vmem(8, 8, 8),
            vmem(2, 2, 8, HALF), vmem(2, 8, HALF), vmem(2, 8, HALF), vmem(2, 8, HALF), vmem(2, 8, HALF),
            sem(6), sem(2), sem(2), sem(2, 2), sem(2, 2), one, one,
            sem(2, 7), sem(2, 7), sem(2, 7), sem(2, 7), sem(7), sem(7), sem(2), sem(2),
            one, one, sem(8), sem(8),
        ],
        compiler_params=pltpu.CompilerParams(
            collective_id=0, has_side_effects=True, vmem_limit_bytes=40 * 2**20
        ),
        name="parareal",
    )(*[pltpu.with_memory_space_constraint(x, pltpu.HBM) for x in args])
    return pl.pallas_call(
        hand_out,
        out_shape=(block, block),
        in_specs=[in_vmem] * 2,
        out_specs=(hbm, hbm),
        scratch_shapes=[vmem(2, 1, 1024), sem(2)],
        compiler_params=pltpu.CompilerParams(vmem_limit_bytes=16 * 2**20),
        name="hand_out",
    )(*kept)


def solution(mesh):
    in_specs = (P("tm", None, "space"), P("tm", None, "space"), P(None, "space"), P(), P(), P())
    out_specs = (P("tm", None, "space"), P("tm", None, "space"))
    return jax.shard_map(local, mesh=mesh, in_specs=in_specs, out_specs=out_specs, check_vma=False)
```

```python
import jax
import jax.numpy as jnp
from jax import lax
from jax.experimental import pallas as pl
from jax.experimental.pallas import tpu as pltpu
from jax.sharding import PartitionSpec as P

MESH = pl.DeviceIdType.MESH
HALF = 64
OWN = 80
PAD = 8
MID = 16
ROWS = 96
EDGE = 48
F32 = jnp.float32
OFFSETS = ((1, 2), (1, 1), (1, 3), (0, 2), (1, 0), (0, 1), (0, 3))


def part(start, size):
    if not isinstance(start, int):
        start = pl.multiple_of(start, 8)
    return pl.ds(start, size)


def up(x, end):
    return jnp.where(lax.broadcasted_iota(jnp.int32, x.shape, 1) == 127, end, pltpu.roll(x, 127, 1))


def down(x, end):
    return jnp.where(lax.broadcasted_iota(jnp.int32, x.shape, 1) == 0, end, pltpu.roll(x, 1, 1))


def reluctivity(a, coef_a, coef_b, nu, at, size):
    rows = pl.ds(at, size)
    for t in range(8):
        north = a[t + 1][rows] if t < 7 else up(a[0][rows], 0.0)
        south = a[t - 1][rows] if t > 0 else down(a[7][rows], 0.0)
        br = north - south
        bt = a[t][pl.ds(at + 1, size)] - a[t][pl.ds(at - 1, size)]
        nu[t][rows] = coef_a[t, rows] - coef_b[t, rows] / (4.0 + (br * br + bt * bt))


def turning(a, nu, at, size):
    here, mid = a[pl.ds(at, size)], nu[pl.ds(at, size)]
    flux = (mid + nu[pl.ds(at + 1, size)]) * (a[pl.ds(at + 1, size)] - here)
    return flux + (mid + nu[pl.ds(at - 1, size)]) * (a[pl.ds(at - 1, size)] - here)


def update(a, nu, drive, mobile, at, size, put):
    rows = pl.ds(at, size)
    nu0, nu7, a0, a7 = nu[0][rows], nu[7][rows], a[0][rows], a[7][rows]
    top = (nu7 + up(nu0, nu7)) * (up(a0, 0.0) - a7)
    below = down(top, 2.0 * nu0 * a0)
    for t in range(8):
        here = a[t][rows]
        above = top if t == 7 else (nu[t][rows] + nu[t + 1][rows]) * (a[t + 1][rows] - here)
        total = turning(a[t], nu[t], at, size) + (above - below) + drive[t, rows]
        put(t, here + mobile[t, rows] * total)
        below = above


def kernel(
    base_hbm, satur_hbm, mob_hbm, a_hbm, j_hbm, r_hbm, out_s, out_e,
    base_ref, satur_ref, mob_ref, in_a, in_j, in_r, ta, tj, tr, starts, drive,
    coef_a, coef_b, mobile, gain, reluct, work, later,
    rim_r, rim, rim_drive, rim_a, rim_b, rim_mobile, rim_gain, rim_reluct, rim_work, rim_later, rim_ends, rim_corr0, rim_items, rim_got,
    ends, corr0, items, got, sums,
    in_sem, pair_send, pair_recv, edge_send, edge_recv, reg_send, reg_recv,
    there_send, there_recv, back_send, back_recv, rim_send, rim_recv,
    oute_send, oute_recv, outs_send, outs_recv,
):
    tm = lax.axis_index("tm")
    sp = lax.axis_index("space")
    core = lax.rem(tm, 2)
    other = 1 - core
    pair = tm - core
    chip = tm // 2
    right = lax.rem(sp + 1, 16)
    left = lax.rem(sp + 15, 16)
    outer = jnp.where(core == 0, left, right)
    partner = (pair + other, sp)

    def far(dy, dx):
        return 4 * lax.rem(chip // 4 + dy, 2) + lax.rem(lax.rem(chip, 4) + dx, 4)

    def source(dy, dx):
        return far(dy, (4 - dx) % 4)

    def remote(src, dst, send, recv, target):
        return pltpu.make_async_remote_copy(src, dst, send, recv, device_id=target, device_id_type=MESH)

    loads = []
    for n, (src, dst) in enumerate(
        ((a_hbm, in_a), (j_hbm, in_j), (r_hbm, in_r), (base_hbm, base_ref), (satur_hbm, satur_ref), (mob_hbm, mob_ref))
    ):
        cp = pltpu.make_async_copy(src, dst, in_sem.at[n])
        cp.start()
        loads.append(cp)

    barrier = pltpu.get_barrier_semaphore()
    for dy, dx in OFFSETS:
        pl.semaphore_signal(barrier, inc=1, device_id=(2 * far(dy, dx) + core, sp), device_id_type=MESH)
    pl.semaphore_signal(barrier, inc=1, device_id=(pair, outer), device_id_type=MESH)
    pl.semaphore_signal(barrier, inc=1, device_id=(pair + 1, outer), device_id_type=MESH)
    pl.semaphore_signal(barrier, inc=1, device_id=partner, device_id_type=MESH)

    def turn(src, dst):
        for t in range(8):
            dst[t] = src[pl.ds(t, 128, stride=8), :].T

    sends = []

    def go(cp):
        cp.start()
        sends.append(cp)
        return cp

    wide = pl.ds(PAD, OWN)
    inner = pl.ds(MID, HALF)
    mine = part((128 - OWN) * core, OWN)
    theirs = part((128 - OWN) * other, OWN)
    rim_halo = part(8 + 16 * core, 16)
    rim_own = part(8 + 16 * other, 16)
    rim_from = part(PAD + 64 * core, 16)
    rim_out = pl.ds(16, 16)
    kept, kept_at = part(PAD + 8 * core, 72), part(PAD + 8 * other, 72)
    beyond, beyond_at = part(16 + 8 * core, 8), part(PAD + 72 * core, 8)
    back_at = part(PAD + 16 * other, 64)
    rim_at = part(PAD + 64 * core, 16)
    own_half = part(HALF * core, HALF)

    loads[0].wait()
    turn(in_a.at[0], ta)
    pl.semaphore_wait(barrier, 10)

    def send_edges(n, src, dst):
        go(remote(src.at[:, pl.ds(112, 16)], dst.at[core, :, pl.ds(8, 16)], edge_send.at[n, 0], edge_recv.at[n, core], (pair, right)))
        go(remote(src.at[:, pl.ds(0, 16)], dst.at[core, :, pl.ds(24, 16)], edge_send.at[n, 1], edge_recv.at[n, core], (pair + 1, left)))

    def send_pair(n, src, dst):
        return go(remote(src.at[:, theirs], dst.at[core, :, wide], pair_send.at[n], pair_recv.at[n], partner))

    send_edges(0, ta, rim)
    loads[1].wait()
    turn(in_j.at[0], tj)
    send_edges(1, tj, rim_drive)
    pairs = [send_pair(0, ta, starts.at[0]), send_pair(1, tj, drive.at[0])]
    loads[2].wait()
    turn(in_r, tr)
    cp_reg = go(
        remote(tr.at[:, part(112 * other, 16)], rim_r.at[:, rim_halo], reg_send, reg_recv, (tm, jnp.where(core == 0, right, left)))
    )

    for cp in loads[3:]:
        cp.wait()
    base = [base_ref[k] for k in range(8)]
    satur = [satur_ref[k] for k in range(8)]
    full = lambda x: jnp.full((8, 128), x, F32)
    tab_a = [full(0.5 * b * (1.0 + s)) for b, s in zip(base, satur)]
    tab_b = [full(2.0 * b * s) for b, s in zip(base, satur)]
    tab_m = [full(mob_ref[k]) for k in range(8)]
    tab_c = [1.0 / (1.0 + 12.0 * m * full(b)) for b, m in zip(base, tab_m)]

    def look_up(src, first, size, put):
        for t in range(8):
            for k in range(0, size, 8):
                r = src[t, part(first + k, 8)]
                bits = [(r & 1) != 0, (r & 2) != 0, (r & 4) != 0]
                for n, tab in enumerate((tab_a, tab_b, tab_m, tab_c)):
                    level = tab
                    for bit in bits:
                        level = [jnp.where(bit, hi, lo) for lo, hi in zip(level[::2], level[1::2])]
                    put(n, t, k, level[0])

    coefs = (coef_a, coef_b, mobile, gain)
    rim_coefs = (rim_a, rim_b, rim_mobile, rim_gain)

    def put_own(n, t, k, x):
        coefs[n][0, t, pl.ds(PAD + k, 8)] = x

    def put_rim(n, t, k, x):
        rim_coefs[n][t, part(8 + 16 * core + k, 8)] = x

    look_up(tr, (128 - OWN) * core, OWN, put_own)
    starts[0, core, :, wide] = ta[:, mine]
    drive[0, core, :, wide] = tj[:, mine]

    chip7 = chip == 7

    def phases(ref):
        return [ref.at[t] for t in range(8)]

    nus = [reluct.at[t + 1] for t in range(8)]
    lates = [later.at[t + 1] for t in range(8)]

    def put_work(t, x):
        work[t, wide] = x

    def put_later(t, x):
        later[t + 1, wide] = x

    def two_steps(it, p):
        ca, cb, cm, force = coef_a.at[it], coef_b.at[it], mobile.at[it], drive.at[it, p]
        a = phases(starts.at[it, p])
        reluctivity(a, ca, cb, nus, PAD, OWN)
        update(a, nus, force, cm, PAD, OWN, put_work)
        a = phases(work)
        reluctivity(a, ca, cb, nus, PAD, OWN)
        update(a, nus, force, cm, PAD, OWN, put_later)
        reluctivity(lates, ca, cb, nus, PAD, OWN)

    def last_step(it, p, t):
        here, mid = later[t + 1, inner], reluct[t + 1, inner]
        total = turning(later.at[t + 1], reluct.at[t + 1], MID, HALF) + drive[it, p, t, inner]
        total += (mid + reluct[t + 2, inner]) * (later[t + 2, inner] - here)
        total += (mid + reluct[t, inner]) * (later[t, inner] - here)
        return here + mobile[it, t, inner] * total

    for it in range(2):
        def put_ends(t, x):
            ends[it, core, t] = x
            if it == 1:
                out_e[t, own_half] = x

        two_steps(it, core)
        update(lates, nus, drive.at[it, core], mobile.at[it], MID, HALF, put_ends)
        if it == 0:
            for cp in pairs:
                cp.wait_recv()
        two_steps(it, other)
        later[0, wide] = down(later[8, wide], 0.0)
        later[9, wide] = up(later[1, wide], 0.0)
        reluct[0, wide] = down(reluct[8, wide], reluct[1, wide])
        reluct[9, wide] = up(reluct[1, wide], reluct[8, wide])

        def finish(t):
            theirs_end = last_step(it, other, t)
            ends[it, other, t] = theirs_end
            own_end = ends[it, core, t]
            c = gain[it, t, inner]
            own_corr = own_end - c * starts[it, core, t, inner]
            theirs_corr = theirs_end - c * starts[it, other, t, inner]
            first = jnp.where(core == 0, own_corr, theirs_corr)
            second = jnp.where(core == 0, theirs_corr, own_corr)
            corr0[it, t] = first
            items[it, t] = jnp.where(chip7, jnp.where(core == 0, theirs_end, own_end), c * first + second)

        there = []
        for n, (dy, dx) in enumerate(OFFSETS):
            q = far(dy, dx)
            finish(q)
            there.append(
                go(remote(items.at[it, q], got.at[it, chip], there_send.at[it, n], there_recv.at[it, n], (2 * q + core, sp)))
            )
        finish(chip)
        got[it, chip] = items[it, chip]

        if it == 1:
            cp_e = go(remote(ends.at[1, other], out_e.at[:, own_half], oute_send, oute_recv, partner))
        else:
            cp_reg.wait_recv()
            look_up(rim_r, 8 + 16 * core, 16, put_rim)
            for ref, into in zip(coefs, rim_coefs):
                into[:, rim_own] = ref[0, :, rim_from]
            for n in range(2):
                for p in range(2):
                    remote(
                        ta.at[:, pl.ds(0, 16)], rim.at[0, :, pl.ds(8, 16)], edge_send.at[n, 0], edge_recv.at[n, p], partner
                    ).wait_recv()
            rim_nus = phases(rim_reluct)
            for p in range(2):
                rim[p, :, rim_own] = starts[0, p, :, rim_from]
                rim_drive[p, :, rim_own] = drive[0, p, :, rim_from]

                def put_rim_work(t, x):
                    rim_work[t, pl.ds(8, 32)] = x

                def put_rim_later(t, x):
                    rim_later[t, pl.ds(8, 32)] = x

                def put_rim_ends(t, x):
                    rim_ends[p, t] = x

                for a, put in ((rim.at[p], put_rim_work), (rim_work, put_rim_later)):
                    reluctivity(phases(a), rim_a, rim_b, rim_nus, 8, 32)
                    update(phases(a), rim_nus, rim_drive.at[p], rim_mobile, 8, 32, put)
                reluctivity(phases(rim_later), rim_a, rim_b, rim_nus, 8, 32)
                update(phases(rim_later), rim_nus, rim_drive.at[p], rim_mobile, 16, 16, put_rim_ends)
            rim_c = rim_gain[:, rim_out]
            k0 = rim_ends[0] - rim_c * rim[0, :, rim_out]
            k1 = rim_ends[1] - rim_c * rim[1, :, rim_out]
            rim_corr0[...] = k0
            rim_items[...] = jnp.where(chip7, rim_ends[1], rim_c * k0 + k1)
            rim_got[chip] = rim_items[...]

            def rim_copy(n):
                q = far(*OFFSETS[n])
                return remote(rim_items, rim_got.at[chip], rim_send.at[n], rim_recv.at[n], (2 * q + core, sp))

            for n, offset in enumerate(OFFSETS):
                @pl.when((far(*offset) > chip) | chip7)
                def _():
                    rim_copy(n).start()

            for ref, edge in zip(coefs, rim_coefs):
                ref[1, :, kept_at] = ref[0, :, kept]
                ref[1, :, beyond_at] = edge[:, beyond]
            drive[1, :, :, kept_at] = drive[0, :, :, kept]
            drive[1, :, :, beyond_at] = rim_drive[:, :, beyond]

        for cp in there:
            cp.wait_recv()
        c = gain[it, chip, inner]
        c2 = c * c
        total = got[it, 7]
        sums[it, 0] = total
        for k in range(7):
            total = c2 * total + got[it, k]
            sums[it, k + 1] = total
        land = back_at if it == 0 else inner
        back = []
        for n, (dy, dx) in enumerate(OFFSETS):
            q = far(dy, dx)
            back.append(
                go(remote(sums.at[it, q], starts.at[it + 1, 0, chip, land], back_send.at[it, n], back_recv.at[it, n], (2 * q + core, sp)))
            )
        starts[it + 1, 0, chip, land] = sums[it, chip]

        if it == 0:
            for n, (dy, dx) in enumerate(OFFSETS):
                @pl.when((source(dy, dx) < chip) | (source(dy, dx) == 7))
                def _():
                    rim_copy(n).wait_recv()
            rim_c = rim_gain[:, rim_out]
            rim_c2 = rim_c * rim_c
            total = rim_got[7]
            for k in range(7):
                total = jnp.where(k < chip, rim_c2 * total + rim_got[k], total)
            starts[1, 0, :, rim_at] = total
            starts[1, 1, :, rim_at] = rim_c * total + rim_corr0[...]

        def spread(t):
            starts[it + 1, 1, t, land] = gain[it, t, inner] * starts[it + 1, 0, t, land] + corr0[it, t]

        if it == 0:
            spread(chip)
            for n in reversed(range(7)):
                back[n].wait_recv()
                spread(source(*OFFSETS[n]))
        else:
            outs = []
            for n in reversed(range(8)):
                t = chip
                if n < 7:
                    back[n].wait_recv()
                    t = source(*OFFSETS[n])
                spread(t)
                outs.append(
                    go(remote(starts.at[2, other, t, inner], out_s.at[t, own_half], outs_send.at[n], outs_recv.at[n], partner))
                )
                out_s[t, own_half] = starts[2, core, t, inner]

    cp_e.wait_recv()
    for cp in outs:
        cp.wait_recv()
    for cp in sends:
        cp.wait_send()
    for n, offset in enumerate(OFFSETS):
        @pl.when((far(*offset) > chip) | chip7)
        def _():
            rim_copy(n).wait_send()


def hand_out(s_ref, e_ref, starts_hbm, ends_hbm, buf, sem):
    copies = []
    for n, (src, dst) in enumerate(((e_ref, ends_hbm), (s_ref, starts_hbm))):
        for t in range(8):
            buf[n, 0, pl.ds(t, 128, stride=8), :] = src[t].T
        cp = pltpu.make_async_copy(buf.at[n], dst, sem.at[n])
        cp.start()
        copies.append(cp)
    for cp in copies:
        cp.wait()


def local(initial_starts, source, region, base_reluctivity, saturation, mobility):
    held = jax.ShapeDtypeStruct((8, 128, 128), F32)
    block = jax.ShapeDtypeStruct((1, 1024, 128), F32)
    hbm = pl.BlockSpec(memory_space=pltpu.HBM)
    in_vmem = pl.BlockSpec(memory_space=pltpu.VMEM)
    vmem = lambda *shape: pltpu.VMEM(shape + (128,), F32)
    ints = lambda *shape: pltpu.VMEM(shape + (128,), jnp.int32)
    table = pltpu.SMEM((8,), F32)
    sem = lambda *shape: pltpu.SemaphoreType.DMA(shape)
    one = pltpu.SemaphoreType.DMA
    args = (base_reluctivity, saturation, mobility, initial_starts, source, region)
    kept = pl.pallas_call(
        kernel,
        out_shape=(held, held),
        in_specs=[hbm] * 6,
        out_specs=(in_vmem, in_vmem),
        scratch_shapes=[
            table, table, table,
            vmem(1, 1024), vmem(1, 1024), ints(1024), vmem(8, 128), vmem(8, 128), ints(8, 128),
            vmem(3, 2, 8, ROWS), vmem(2, 2, 8, ROWS),
            vmem(2, 8, ROWS), vmem(2, 8, ROWS), vmem(2, 8, ROWS), vmem(2, 8, ROWS), vmem(10, ROWS), vmem(8, ROWS), vmem(10, ROWS),
            ints(8, EDGE), vmem(2, 8, EDGE), vmem(2, 8, EDGE), vmem(8, EDGE), vmem(8, EDGE), vmem(8, EDGE), vmem(8, EDGE),
            vmem(8, EDGE), vmem(8, EDGE), vmem(8, EDGE), vmem(2, 8, 16), vmem(8, 16), vmem(8, 16), vmem(8, 8, 16),
            vmem(2, 2, 8, HALF), vmem(2, 8, HALF), vmem(2, 8, HALF), vmem(2, 8, HALF), vmem(2, 8, HALF),
            sem(6), sem(2), sem(2), sem(2, 2), sem(2, 2), one, one,
            sem(2, 7), sem(2, 7), sem(2, 7), sem(2, 7), sem(7), sem(7),
            one, one, sem(8), sem(8),
        ],
        compiler_params=pltpu.CompilerParams(
            collective_id=0, has_side_effects=True, vmem_limit_bytes=40 * 2**20
        ),
        name="parareal",
    )(*[pltpu.with_memory_space_constraint(x, pltpu.HBM) for x in args])
    return pl.pallas_call(
        hand_out,
        out_shape=(block, block),
        in_specs=[in_vmem] * 2,
        out_specs=(hbm, hbm),
        scratch_shapes=[vmem(2, 1, 1024), sem(2)],
        compiler_params=pltpu.CompilerParams(vmem_limit_bytes=16 * 2**20),
        name="hand_out",
    )(*kept)


def solution(mesh):
    in_specs = (P("tm", None, "space"), P("tm", None, "space"), P(None, "space"), P(), P(), P())
    out_specs = (P("tm", None, "space"), P("tm", None, "space"))
    return jax.shard_map(local, mesh=mesh, in_specs=in_specs, out_specs=out_specs, check_vma=False)
```

```python
import jax
import jax.numpy as jnp
from jax import lax
from jax.experimental import pallas as pl
from jax.experimental.pallas import tpu as pltpu
from jax.sharding import PartitionSpec as P

MESH = pl.DeviceIdType.MESH
HALF = 64
OWN = 80
PAD = 8
MID = 16
ROWS = 96
EDGE = 40
F32 = jnp.float32
OFFSETS = ((1, 2), (1, 1), (1, 3), (0, 2), (1, 0), (0, 1), (0, 3))


def part(start, size):
    if not isinstance(start, int):
        start = pl.multiple_of(start, 8)
    return pl.ds(start, size)


def up(x, end):
    return jnp.where(lax.broadcasted_iota(jnp.int32, x.shape, 1) == 127, end, pltpu.roll(x, 127, 1))


def down(x, end):
    return jnp.where(lax.broadcasted_iota(jnp.int32, x.shape, 1) == 0, end, pltpu.roll(x, 1, 1))


def reluctivity(a, coef_a, coef_b, nu, at, size):
    rows = pl.ds(at, size)
    for t in range(8):
        north = a[t + 1][rows] if t < 7 else up(a[0][rows], 0.0)
        south = a[t - 1][rows] if t > 0 else down(a[7][rows], 0.0)
        br = north - south
        bt = a[t][pl.ds(at + 1, size)] - a[t][pl.ds(at - 1, size)]
        nu[t][rows] = coef_a[t, rows] - coef_b[t, rows] / (4.0 + (br * br + bt * bt))


def turning(a, nu, at, size):
    here, mid = a[pl.ds(at, size)], nu[pl.ds(at, size)]
    flux = (mid + nu[pl.ds(at + 1, size)]) * (a[pl.ds(at + 1, size)] - here)
    return flux + (mid + nu[pl.ds(at - 1, size)]) * (a[pl.ds(at - 1, size)] - here)


def update(a, nu, drive, mobile, at, size, put):
    rows = pl.ds(at, size)
    nu0, nu7, a0, a7 = nu[0][rows], nu[7][rows], a[0][rows], a[7][rows]
    top = (nu7 + up(nu0, nu7)) * (up(a0, 0.0) - a7)
    below = down(top, 2.0 * nu0 * a0)
    for t in range(8):
        here = a[t][rows]
        above = top if t == 7 else (nu[t][rows] + nu[t + 1][rows]) * (a[t + 1][rows] - here)
        total = turning(a[t], nu[t], at, size) + (above - below) + drive[t, rows]
        put(t, here + mobile[t, rows] * total)
        below = above


def kernel(
    base_hbm, satur_hbm, mob_hbm, a_hbm, j_hbm, r_hbm, out_s, out_e,
    base_ref, satur_ref, mob_ref, in_a, in_j, in_r, ta, tj, tr, starts, drive,
    coef_a, coef_b, mobile, gain, carry_gain, reluct, work, later,
    rim_r, rim, rim_drive, rim_a, rim_b, rim_mobile, rim_gain, rim_reluct, rim_work, rim_later, rim_ends, rim_corr0, rim_items, rim_got,
    ends, corr0, items, got, sums,
    in_sem, pair_send, pair_recv, edge_send, edge_recv, reg_send, reg_recv,
    there_send, there_recv, back_send, back_recv, rim_send, rim_recv, halo_send, halo_recv,
    oute_send, oute_recv, outs_send, outs_recv,
):
    tm = lax.axis_index("tm")
    sp = lax.axis_index("space")
    core = lax.rem(tm, 2)
    other = 1 - core
    pair = tm - core
    chip = tm // 2
    right = lax.rem(sp + 1, 16)
    left = lax.rem(sp + 15, 16)
    outer = jnp.where(core == 0, left, right)
    partner = (pair + other, sp)

    def far(dy, dx):
        return 4 * lax.rem(chip // 4 + dy, 2) + lax.rem(lax.rem(chip, 4) + dx, 4)

    def source(dy, dx):
        return far(dy, (4 - dx) % 4)

    def remote(src, dst, send, recv, target):
        return pltpu.make_async_remote_copy(src, dst, send, recv, device_id=target, device_id_type=MESH)

    loads = []
    for n, (src, dst, pieces) in enumerate(((a_hbm.at[0], in_a.at[0], 4), (j_hbm.at[0], in_j.at[0], 4), (r_hbm, in_r, 4))):
        size = 1024 // pieces
        loads.append([])
        for k in range(pieces):
            cp = pltpu.make_async_copy(src.at[pl.ds(size * k, size)], dst.at[pl.ds(size * k, size)], in_sem.at[n, k])
            cp.start()
            loads[-1].append(cp)
    tables = []
    for n, (src, dst) in enumerate(((base_hbm, base_ref), (satur_hbm, satur_ref), (mob_hbm, mob_ref))):
        cp = pltpu.make_async_copy(src, dst, in_sem.at[3, n])
        cp.start()
        tables.append(cp)

    def arrived(copies):
        for cp in copies:
            cp.wait()

    barrier = pltpu.get_barrier_semaphore()
    for dy, dx in OFFSETS:
        pl.semaphore_signal(barrier, inc=1, device_id=(2 * far(dy, dx) + core, sp), device_id_type=MESH)
        pl.semaphore_signal(barrier, inc=1, device_id=(2 * far(dy, dx) + other, sp), device_id_type=MESH)
    pl.semaphore_signal(barrier, inc=1, device_id=(pair, outer), device_id_type=MESH)
    pl.semaphore_signal(barrier, inc=1, device_id=(pair + 1, outer), device_id_type=MESH)
    pl.semaphore_signal(barrier, inc=1, device_id=partner, device_id_type=MESH)

    def turn(src, dst):
        for t in range(8):
            dst[t] = src[pl.ds(t, 128, stride=8), :].T

    sends = []

    def go(cp):
        cp.start()
        sends.append(cp)
        return cp

    wide = pl.ds(PAD, OWN)
    inner = pl.ds(MID, HALF)
    mine = part((128 - OWN) * core, OWN)
    theirs = part((128 - OWN) * other, OWN)
    rim_halo = part(8 + 16 * core, 8)
    rim_own = part(8 + 8 * other, 16)
    rim_from = part(PAD + 64 * core, 16)
    rim_out = pl.ds(16, 8)
    kept, kept_at = part(PAD + 8 * core, 72), part(PAD + 8 * other, 72)
    beyond_at = part(PAD + 72 * core, 8)
    rim_at = part(MID + 56 * core, 8)
    own_half = part(HALF * core, HALF)
    own_half = part(HALF * core, HALF)

    arrived(loads[0])
    turn(in_a.at[0], ta)
    pl.semaphore_wait(barrier, 17)

    def send_edges(n, src, dst):
        go(remote(src.at[:, pl.ds(120, 8)], dst.at[core, :, pl.ds(8, 8)], edge_send.at[n, 0], edge_recv.at[n, core], (pair, right)))
        go(remote(src.at[:, pl.ds(0, 8)], dst.at[core, :, pl.ds(24, 8)], edge_send.at[n, 1], edge_recv.at[n, core], (pair + 1, left)))

    def send_pair(n, src, dst):
        return go(remote(src.at[:, theirs], dst.at[core, :, wide], pair_send.at[n], pair_recv.at[n], partner))

    send_edges(0, ta, rim)
    arrived(loads[1])
    turn(in_j.at[0], tj)
    send_edges(1, tj, rim_drive)
    arrived(loads[2])
    turn(in_r, tr)
    cp_reg = go(
        remote(tr.at[:, part(120 * other, 8)], rim_r.at[:, rim_halo], reg_send, reg_recv, (tm, jnp.where(core == 0, right, left)))
    )
    pairs = [send_pair(0, ta, starts.at[0]), send_pair(1, tj, drive.at[0])]

    arrived(tables)
    base = [base_ref[k] for k in range(8)]
    satur = [satur_ref[k] for k in range(8)]
    full = lambda x: jnp.full((8, 128), x, F32)
    tab_a = [full(0.5 * b * (1.0 + s)) for b, s in zip(base, satur)]
    tab_b = [full(2.0 * b * s) for b, s in zip(base, satur)]
    tab_m = [full(mob_ref[k]) for k in range(8)]
    tab_c = [1.0 / (1.0 + 12.0 * m * full(b)) for b, m in zip(base, tab_m)]

    def look_up(src, first, size, put):
        for t in range(8):
            for k in range(0, size, 8):
                r = src[t, part(first + k, 8)]
                bits = [(r & 1) != 0, (r & 2) != 0, (r & 4) != 0]
                for n, tab in enumerate((tab_a, tab_b, tab_m, tab_c)):
                    level = tab
                    for bit in bits:
                        level = [jnp.where(bit, hi, lo) for lo, hi in zip(level[::2], level[1::2])]
                    put(n, t, k, level[0])

    coefs = (coef_a, coef_b, mobile, gain)
    rim_coefs = (rim_a, rim_b, rim_mobile, rim_gain)

    def put_own(n, t, k, x):
        coefs[n][0, t, pl.ds(PAD + k, 8)] = x

    def put_rim(n, t, k, x):
        rim_coefs[n][t, rim_halo] = x

    look_up(tr, (128 - OWN) * core, OWN, put_own)
    for it, first in enumerate((8 + 48 * other, HALF * other)):
        for k in range(0, HALF, 8):
            r = tr[chip, part(first + k, 8)]
            level = tab_c
            for bit in ((r & 1) != 0, (r & 2) != 0, (r & 4) != 0):
                level = [jnp.where(bit, hi, lo) for lo, hi in zip(level[::2], level[1::2])]
            carry_gain[it, pl.ds(k, 8)] = level[0]
    starts[0, core, :, wide] = ta[:, mine]
    drive[0, core, :, wide] = tj[:, mine]

    chip7 = chip == 7

    def phases(ref):
        return [ref.at[t] for t in range(8)]

    nus = [reluct.at[t + 1] for t in range(8)]
    lates = [later.at[t + 1] for t in range(8)]

    def put_work(t, x):
        work[t, wide] = x

    def put_later(t, x):
        later[t + 1, wide] = x

    def two_steps(it, p):
        ca, cb, cm, force = coef_a.at[it], coef_b.at[it], mobile.at[it], drive.at[it, p]
        a = phases(starts.at[it, p])
        reluctivity(a, ca, cb, nus, PAD, OWN)
        update(a, nus, force, cm, PAD, OWN, put_work)
        a = phases(work)
        reluctivity(a, ca, cb, nus, PAD, OWN)
        update(a, nus, force, cm, PAD, OWN, put_later)
        reluctivity(lates, ca, cb, nus, PAD, OWN)

    def last_step(it, p, t):
        here, mid = later[t + 1, inner], reluct[t + 1, inner]
        total = turning(later.at[t + 1], reluct.at[t + 1], MID, HALF) + drive[it, p, t, inner]
        total += (mid + reluct[t + 2, inner]) * (later[t + 2, inner] - here)
        total += (mid + reluct[t, inner]) * (later[t, inner] - here)
        return here + mobile[it, t, inner] * total

    for it in range(2):
        def put_ends(t, x):
            ends[it, core, t] = x
            if it == 1:
                out_e[t, own_half] = x

        two_steps(it, core)
        update(lates, nus, drive.at[it, core], mobile.at[it], MID, HALF, put_ends)
        if it == 0:
            for cp in pairs:
                cp.wait_recv()
        two_steps(it, other)
        later[0, wide] = down(later[8, wide], 0.0)
        later[9, wide] = up(later[1, wide], 0.0)
        reluct[0, wide] = down(reluct[8, wide], reluct[1, wide])
        reluct[9, wide] = up(reluct[1, wide], reluct[8, wide])

        def finish(t):
            theirs_end = last_step(it, other, t)
            ends[it, other, t] = theirs_end
            own_end = ends[it, core, t]
            c = gain[it, t, inner]
            own_corr = own_end - c * starts[it, core, t, inner]
            theirs_corr = theirs_end - c * starts[it, other, t, inner]
            first = jnp.where(core == 0, own_corr, theirs_corr)
            second = jnp.where(core == 0, theirs_corr, own_corr)
            corr0[it, t] = first
            items[it, t] = jnp.where(chip7, jnp.where(core == 0, theirs_end, own_end), c * first + second)

        there = []
        for n, (dy, dx) in enumerate(OFFSETS):
            q = far(dy, dx)
            finish(q)
            there.append(
                go(remote(items.at[it, q], got.at[it, chip], there_send.at[it, n], there_recv.at[it, n], (2 * q + other, sp)))
            )
        finish(chip)
        there.append(go(remote(items.at[it, chip], got.at[it, chip], there_send.at[it, 7], there_recv.at[it, 7], partner)))

        if it == 1:
            cp_e = go(remote(ends.at[1, other], out_e.at[:, own_half], oute_send, oute_recv, partner))
        else:
            cp_reg.wait_recv()
            look_up(rim_r, 8 + 16 * core, 8, put_rim)
            for ref, into in zip(coefs, rim_coefs):
                into[:, rim_own] = ref[0, :, rim_from]
            for n in range(2):
                for p in range(2):
                    remote(
                        ta.at[:, pl.ds(0, 8)], rim.at[0, :, pl.ds(8, 8)], edge_send.at[n, 0], edge_recv.at[n, p], partner
                    ).wait_recv()
            rim_nus = phases(rim_reluct)
            for p in range(2):
                rim[p, :, rim_own] = starts[0, p, :, rim_from]
                rim_drive[p, :, rim_own] = drive[0, p, :, rim_from]

                def put_rim_work(t, x):
                    rim_work[t, pl.ds(8, 24)] = x

                def put_rim_later(t, x):
                    rim_later[t, pl.ds(8, 24)] = x

                def put_rim_ends(t, x):
                    rim_ends[p, t] = x

                for a, put in ((rim.at[p], put_rim_work), (rim_work, put_rim_later)):
                    reluctivity(phases(a), rim_a, rim_b, rim_nus, 8, 24)
                    update(phases(a), rim_nus, rim_drive.at[p], rim_mobile, 8, 24, put)
                reluctivity(phases(rim_later), rim_a, rim_b, rim_nus, 8, 24)
                update(phases(rim_later), rim_nus, rim_drive.at[p], rim_mobile, 16, 8, put_rim_ends)
            rim_c = rim_gain[:, rim_out]
            k0 = rim_ends[0] - rim_c * rim[0, :, rim_out]
            k1 = rim_ends[1] - rim_c * rim[1, :, rim_out]
            rim_corr0[...] = k0
            rim_items[...] = jnp.where(chip7, rim_ends[1], rim_c * k0 + k1)
            rim_got[chip] = rim_items[...]

            def rim_copy(n):
                q = far(*OFFSETS[n])
                return remote(rim_items, rim_got.at[chip], rim_send.at[n], rim_recv.at[n], (2 * q + core, sp))

            for n, offset in enumerate(OFFSETS):
                @pl.when((far(*offset) > chip) | chip7)
                def _():
                    rim_copy(n).start()

            for ref, edge in zip(coefs, rim_coefs):
                ref[1, :, kept_at] = ref[0, :, kept]
                ref[1, :, beyond_at] = edge[:, rim_halo]
            drive[1, :, :, kept_at] = drive[0, :, :, kept]
            drive[1, :, :, beyond_at] = rim_drive[:, :, rim_halo]

        for cp in there:
            cp.wait_recv()
        c = carry_gain[it]
        c2 = c * c
        total = got[it, 7]
        sums[it, 0] = total
        for k in range(7):
            total = c2 * total + got[it, k]
            sums[it, k + 1] = total
        land = part(PAD + 16 * other, HALF) if it == 0 else inner
        their_land = part(PAD + 16 * core, HALF) if it == 0 else inner
        back = []
        for n, (dy, dx) in enumerate(OFFSETS):
            q = far(dy, dx)
            back.append(
                go(remote(sums.at[it, q], starts.at[it + 1, 0, chip, their_land], back_send.at[it, n], back_recv.at[it, n], (2 * q + other, sp)))
            )
        back.append(go(remote(sums.at[it, chip], starts.at[it + 1, 0, chip, their_land], back_send.at[it, 7], back_recv.at[it, 7], partner)))

        if it == 0:
            for n, (dy, dx) in enumerate(OFFSETS):
                @pl.when((source(dy, dx) < chip) | (source(dy, dx) == 7))
                def _():
                    rim_copy(n).wait_recv()
            rim_c = rim_gain[:, rim_out]
            rim_c2 = rim_c * rim_c
            total = rim_got[7]
            for k in range(7):
                total = jnp.where(k < chip, rim_c2 * total + rim_got[k], total)
            starts[1, 0, :, rim_at] = total
            starts[1, 1, :, rim_at] = rim_c * total + rim_corr0[...]
            outer_halo = go(
                remote(starts.at[1, :, :, rim_at], starts.at[1, :, :, part(PAD + 72 * other, 8)], halo_send, halo_recv, (pair + other, outer))
            )

        def spread(t):
            starts[it + 1, 1, t, land] = gain[it, t, inner] * starts[it + 1, 0, t, land] + corr0[it, t]

        if it == 0:
            for n in reversed(range(8)):
                back[n].wait_recv()
                spread(source(*OFFSETS[n]) if n < 7 else chip)
            outer_halo.wait_recv()
        else:
            outs = []
            for n in reversed(range(8)):
                back[n].wait_recv()
                t = source(*OFFSETS[n]) if n < 7 else chip
                spread(t)
                outs.append(
                    go(remote(starts.at[2, other, t, inner], out_s.at[t, own_half], outs_send.at[n], outs_recv.at[n], partner))
                )
                out_s[t, own_half] = starts[2, core, t, inner]

    cp_e.wait_recv()
    for cp in outs:
        cp.wait_recv()
    for cp in sends:
        cp.wait_send()
    for n, offset in enumerate(OFFSETS):
        @pl.when((far(*offset) > chip) | chip7)
        def _():
            rim_copy(n).wait_send()


def hand_out(s_ref, e_ref, starts_hbm, ends_hbm, buf, sem):
    copies = []
    for n, (src, dst) in enumerate(((e_ref, ends_hbm), (s_ref, starts_hbm))):
        for t in range(8):
            buf[n, 0, pl.ds(t, 128, stride=8), :] = src[t].T
        cp = pltpu.make_async_copy(buf.at[n], dst, sem.at[n])
        cp.start()
        copies.append(cp)
    for cp in copies:
        cp.wait()


def local(initial_starts, source, region, base_reluctivity, saturation, mobility):
    held = jax.ShapeDtypeStruct((8, 128, 128), F32)
    block = jax.ShapeDtypeStruct((1, 1024, 128), F32)
    hbm = pl.BlockSpec(memory_space=pltpu.HBM)
    in_vmem = pl.BlockSpec(memory_space=pltpu.VMEM)
    vmem = lambda *shape: pltpu.VMEM(shape + (128,), F32)
    ints = lambda *shape: pltpu.VMEM(shape + (128,), jnp.int32)
    table = pltpu.SMEM((8,), F32)
    sem = lambda *shape: pltpu.SemaphoreType.DMA(shape)
    one = pltpu.SemaphoreType.DMA
    args = (base_reluctivity, saturation, mobility, initial_starts, source, region)
    kept = pl.pallas_call(
        kernel,
        out_shape=(held, held),
        in_specs=[hbm] * 6,
        out_specs=(in_vmem, in_vmem),
        scratch_shapes=[
            table, table, table,
            vmem(1, 1024), vmem(1, 1024), ints(1024), vmem(8, 128), vmem(8, 128), ints(8, 128),
            vmem(3, 2, 8, ROWS), vmem(2, 2, 8, ROWS),
            vmem(2, 8, ROWS), vmem(2, 8, ROWS), vmem(2, 8, ROWS), vmem(2, 8, ROWS), vmem(2, HALF), vmem(10, ROWS), vmem(8, ROWS), vmem(10, ROWS),
            ints(8, EDGE), vmem(2, 8, EDGE), vmem(2, 8, EDGE), vmem(8, EDGE), vmem(8, EDGE), vmem(8, EDGE), vmem(8, EDGE),
            vmem(8, EDGE), vmem(8, EDGE), vmem(8, EDGE), vmem(2, 8, 8), vmem(8, 8), vmem(8, 8), vmem(8, 8, 8),
            vmem(2, 2, 8, HALF), vmem(2, 8, HALF), vmem(2, 8, HALF), vmem(2, 8, HALF), vmem(2, 8, HALF),
            sem(4, 4), sem(2), sem(2), sem(2, 2), sem(2, 2), one, one,
            sem(2, 8), sem(2, 8), sem(2, 8), sem(2, 8), sem(7), sem(7), one, one,
            one, one, sem(8), sem(8),
        ],
        compiler_params=pltpu.CompilerParams(
            collective_id=0, has_side_effects=True, vmem_limit_bytes=40 * 2**20
        ),
        name="parareal",
    )(*[pltpu.with_memory_space_constraint(x, pltpu.HBM) for x in args])
    return pl.pallas_call(
        hand_out,
        out_shape=(block, block),
        in_specs=[in_vmem] * 2,
        out_specs=(hbm, hbm),
        scratch_shapes=[vmem(2, 1, 1024), sem(2)],
        compiler_params=pltpu.CompilerParams(vmem_limit_bytes=16 * 2**20),
        name="hand_out",
    )(*kept)


def solution(mesh):
    in_specs = (P("tm", None, "space"), P("tm", None, "space"), P(None, "space"), P(), P(), P())
    out_specs = (P("tm", None, "space"), P("tm", None, "space"))
    return jax.shard_map(local, mesh=mesh, in_specs=in_specs, out_specs=out_specs, check_vma=False)
```

```python
import jax
import jax.numpy as jnp
from jax import lax
from jax.experimental import pallas as pl
from jax.experimental.pallas import tpu as pltpu
from jax.sharding import PartitionSpec as P

MESH = pl.DeviceIdType.MESH
HALF = 64
OWN = 80
PAD = 8
MID = 16
ROWS = 96
EDGE = 40
F32 = jnp.float32
OFFSETS = ((1, 2), (1, 1), (1, 3), (0, 2), (1, 0), (0, 1), (0, 3))


def part(start, size):
    if not isinstance(start, int):
        start = pl.multiple_of(start, 8)
    return pl.ds(start, size)


def up(x, end):
    return jnp.where(lax.broadcasted_iota(jnp.int32, x.shape, 1) == 127, end, pltpu.roll(x, 127, 1))


def down(x, end):
    return jnp.where(lax.broadcasted_iota(jnp.int32, x.shape, 1) == 0, end, pltpu.roll(x, 1, 1))


def reluctivity(a, coef_a, coef_b, nu, at, size):
    rows = pl.ds(at, size)
    for t in range(8):
        north = a[t + 1][rows] if t < 7 else up(a[0][rows], 0.0)
        south = a[t - 1][rows] if t > 0 else down(a[7][rows], 0.0)
        br = north - south
        bt = a[t][pl.ds(at + 1, size)] - a[t][pl.ds(at - 1, size)]
        nu[t][rows] = coef_a[t, rows] - coef_b[t, rows] / (4.0 + (br * br + bt * bt))


def turning(a, nu, at, size):
    here, mid = a[pl.ds(at, size)], nu[pl.ds(at, size)]
    flux = (mid + nu[pl.ds(at + 1, size)]) * (a[pl.ds(at + 1, size)] - here)
    return flux + (mid + nu[pl.ds(at - 1, size)]) * (a[pl.ds(at - 1, size)] - here)


def update(a, nu, drive, mobile, at, size, put):
    rows = pl.ds(at, size)
    nu0, nu7, a0, a7 = nu[0][rows], nu[7][rows], a[0][rows], a[7][rows]
    top = (nu7 + up(nu0, nu7)) * (up(a0, 0.0) - a7)
    below = down(top, 2.0 * nu0 * a0)
    for t in range(8):
        here = a[t][rows]
        above = top if t == 7 else (nu[t][rows] + nu[t + 1][rows]) * (a[t + 1][rows] - here)
        total = turning(a[t], nu[t], at, size) + (above - below) + drive[t, rows]
        put(t, here + mobile[t, rows] * total)
        below = above


def kernel(
    base_hbm, satur_hbm, mob_hbm, a_hbm, j_hbm, r_hbm, out_s, out_e,
    base_ref, satur_ref, mob_ref, in_a, in_j, in_r, ta, tj, tr, starts, drive,
    coef_a, coef_b, mobile, gain, carry_gain, reluct, work, later,
    rim_r, rim, rim_drive, rim_a, rim_b, rim_mobile, rim_gain, rim_reluct, rim_work, rim_later, rim_ends, rim_corr0, rim_items, rim_got,
    ends, corr0, items, got, sums,
    word, in_sem, pair_send, pair_recv, edge_send, edge_recv, reg_send, reg_recv,
    there_send, there_recv, back_send, back_recv, rim_send, rim_recv, halo_send, halo_recv,
    oute_send, oute_recv, outs_send, outs_recv,
):
    tm = lax.axis_index("tm")
    sp = lax.axis_index("space")
    core = lax.rem(tm, 2)
    other = 1 - core
    pair = tm - core
    chip = tm // 2
    right = lax.rem(sp + 1, 16)
    left = lax.rem(sp + 15, 16)
    outer = jnp.where(core == 0, left, right)
    partner = (pair + other, sp)

    def far(dy, dx):
        return 4 * lax.rem(chip // 4 + dy, 2) + lax.rem(lax.rem(chip, 4) + dx, 4)

    def source(dy, dx):
        return far(dy, (4 - dx) % 4)

    def remote(src, dst, send, recv, target):
        return pltpu.make_async_remote_copy(src, dst, send, recv, device_id=target, device_id_type=MESH)

    barrier = pltpu.get_barrier_semaphore()
    across = (2 * far(1, 0) + core, sp)
    near = [(2 * far(0, dx) + core, sp) for dx in (1, 3, 2)] + [across, (pair, outer), (pair + 1, outer), partner]
    for device in near:
        pl.semaphore_signal(barrier, inc=1, device_id=device, device_id_type=MESH)

    loads = []
    for n, (src, dst, pieces) in enumerate(((a_hbm.at[0], in_a.at[0], 4), (j_hbm.at[0], in_j.at[0], 4), (r_hbm, in_r, 4))):
        size = 1024 // pieces
        loads.append([])
        for k in range(pieces):
            cp = pltpu.make_async_copy(src.at[pl.ds(size * k, size)], dst.at[pl.ds(size * k, size)], in_sem.at[n, k])
            cp.start()
            loads[-1].append(cp)
    tables = []
    for n, (src, dst) in enumerate(((base_hbm, base_ref), (satur_hbm, satur_ref), (mob_hbm, mob_ref))):
        cp = pltpu.make_async_copy(src, dst, in_sem.at[3, n])
        cp.start()
        tables.append(cp)

    def arrived(copies):
        for cp in copies:
            cp.wait()

    def turn(src, dst):
        for t in range(8):
            dst[t] = src[pl.ds(t, 128, stride=8), :].T

    sends = []

    def go(cp):
        cp.start()
        sends.append(cp)
        return cp

    wide = pl.ds(PAD, OWN)
    inner = pl.ds(MID, HALF)
    mine = part((128 - OWN) * core, OWN)
    theirs = part((128 - OWN) * other, OWN)
    rim_halo = part(8 + 16 * core, 8)
    rim_own = part(8 + 8 * other, 16)
    rim_from = part(PAD + 64 * core, 16)
    rim_out = pl.ds(16, 8)
    kept, kept_at = part(PAD + 8 * core, 72), part(PAD + 8 * other, 72)
    beyond_at = part(PAD + 72 * core, 8)
    rim_at = part(MID + 56 * core, 8)
    own_half = part(HALF * core, HALF)
    own_half = part(HALF * core, HALF)

    arrived(loads[0])
    turn(in_a.at[0], ta)

    arrived(loads[1])
    turn(in_j.at[0], tj)
    arrived(loads[2])
    turn(in_r, tr)
    arrived(tables)
    base = [base_ref[k] for k in range(8)]
    satur = [satur_ref[k] for k in range(8)]
    full = lambda x: jnp.full((8, 128), x, F32)
    tab_a = [full(0.5 * b * (1.0 + s)) for b, s in zip(base, satur)]
    tab_b = [full(2.0 * b * s) for b, s in zip(base, satur)]
    tab_m = [full(mob_ref[k]) for k in range(8)]
    tab_c = [1.0 / (1.0 + 12.0 * m * full(b)) for b, m in zip(base, tab_m)]

    def look_up(src, first, size, put):
        for t in range(8):
            for k in range(0, size, 8):
                r = src[t, part(first + k, 8)]
                bits = [(r & 1) != 0, (r & 2) != 0, (r & 4) != 0]
                for n, tab in enumerate((tab_a, tab_b, tab_m, tab_c)):
                    level = tab
                    for bit in bits:
                        level = [jnp.where(bit, hi, lo) for lo, hi in zip(level[::2], level[1::2])]
                    put(n, t, k, level[0])

    coefs = (coef_a, coef_b, mobile, gain)
    rim_coefs = (rim_a, rim_b, rim_mobile, rim_gain)

    def put_own(n, t, k, x):
        coefs[n][0, t, pl.ds(PAD + k, 8)] = x

    def put_rim(n, t, k, x):
        rim_coefs[n][t, rim_halo] = x

    look_up(tr, (128 - OWN) * core, OWN, put_own)
    for it, first in enumerate((8 + 48 * other, HALF * other)):
        for k in range(0, HALF, 8):
            r = tr[chip, part(first + k, 8)]
            level = tab_c
            for bit in ((r & 1) != 0, (r & 2) != 0, (r & 4) != 0):
                level = [jnp.where(bit, hi, lo) for lo, hi in zip(level[::2], level[1::2])]
            carry_gain[it, pl.ds(k, 8)] = level[0]
    starts[0, core, :, wide] = ta[:, mine]
    drive[0, core, :, wide] = tj[:, mine]

    pl.semaphore_wait(barrier, len(near))
    pl.semaphore_signal(word.at[0], inc=1, device_id=across, device_id_type=MESH)

    def send_edges(n, src, dst):
        go(remote(src.at[:, pl.ds(120, 8)], dst.at[core, :, pl.ds(8, 8)], edge_send.at[n, 0], edge_recv.at[n, core], (pair, right)))
        go(remote(src.at[:, pl.ds(0, 8)], dst.at[core, :, pl.ds(24, 8)], edge_send.at[n, 1], edge_recv.at[n, core], (pair + 1, left)))

    def send_pair(n, src, dst):
        return go(remote(src.at[:, theirs], dst.at[core, :, wide], pair_send.at[n], pair_recv.at[n], partner))

    send_edges(0, ta, rim)
    send_edges(1, tj, rim_drive)
    cp_reg = go(
        remote(tr.at[:, part(120 * other, 8)], rim_r.at[:, rim_halo], reg_send, reg_recv, (tm, jnp.where(core == 0, right, left)))
    )
    pairs = [send_pair(0, ta, starts.at[0]), send_pair(1, tj, drive.at[0])]


    chip7 = chip == 7

    def phases(ref):
        return [ref.at[t] for t in range(8)]

    nus = [reluct.at[t + 1] for t in range(8)]
    lates = [later.at[t + 1] for t in range(8)]

    def put_work(t, x):
        work[t, wide] = x

    def put_later(t, x):
        later[t + 1, wide] = x

    def two_steps(it, p):
        ca, cb, cm, force = coef_a.at[it], coef_b.at[it], mobile.at[it], drive.at[it, p]
        a = phases(starts.at[it, p])
        reluctivity(a, ca, cb, nus, PAD, OWN)
        update(a, nus, force, cm, PAD, OWN, put_work)
        a = phases(work)
        reluctivity(a, ca, cb, nus, PAD, OWN)
        update(a, nus, force, cm, PAD, OWN, put_later)
        reluctivity(lates, ca, cb, nus, PAD, OWN)

    def last_step(it, p, t):
        here, mid = later[t + 1, inner], reluct[t + 1, inner]
        total = turning(later.at[t + 1], reluct.at[t + 1], MID, HALF) + drive[it, p, t, inner]
        total += (mid + reluct[t + 2, inner]) * (later[t + 2, inner] - here)
        total += (mid + reluct[t, inner]) * (later[t, inner] - here)
        return here + mobile[it, t, inner] * total

    for it in range(2):
        def put_ends(t, x):
            ends[it, core, t] = x
            if it == 1:
                out_e[t, own_half] = x

        two_steps(it, core)
        update(lates, nus, drive.at[it, core], mobile.at[it], MID, HALF, put_ends)
        if it == 0:
            pl.semaphore_wait(word.at[0], 1)
            pl.semaphore_signal(word.at[1], inc=1, device_id=partner, device_id_type=MESH)
            for cp in pairs:
                cp.wait_recv()
        two_steps(it, other)
        later[0, wide] = down(later[8, wide], 0.0)
        later[9, wide] = up(later[1, wide], 0.0)
        reluct[0, wide] = down(reluct[8, wide], reluct[1, wide])
        reluct[9, wide] = up(reluct[1, wide], reluct[8, wide])

        def finish(t):
            theirs_end = last_step(it, other, t)
            ends[it, other, t] = theirs_end
            own_end = ends[it, core, t]
            c = gain[it, t, inner]
            own_corr = own_end - c * starts[it, core, t, inner]
            theirs_corr = theirs_end - c * starts[it, other, t, inner]
            first = jnp.where(core == 0, own_corr, theirs_corr)
            second = jnp.where(core == 0, theirs_corr, own_corr)
            corr0[it, t] = first
            items[it, t] = jnp.where(chip7, jnp.where(core == 0, theirs_end, own_end), c * first + second)

        if it == 0:
            pl.semaphore_wait(word.at[1], 1)
        there = []
        for n, (dy, dx) in enumerate(OFFSETS):
            q = far(dy, dx)
            finish(q)
            there.append(
                go(remote(items.at[it, q], got.at[it, chip], there_send.at[it, n], there_recv.at[it, n], (2 * q + other, sp)))
            )
        finish(chip)
        there.append(go(remote(items.at[it, chip], got.at[it, chip], there_send.at[it, 7], there_recv.at[it, 7], partner)))

        if it == 1:
            cp_e = go(remote(ends.at[1, other], out_e.at[:, own_half], oute_send, oute_recv, partner))
        else:
            cp_reg.wait_recv()
            look_up(rim_r, 8 + 16 * core, 8, put_rim)
            for ref, into in zip(coefs, rim_coefs):
                into[:, rim_own] = ref[0, :, rim_from]
            for n in range(2):
                for p in range(2):
                    remote(
                        ta.at[:, pl.ds(0, 8)], rim.at[0, :, pl.ds(8, 8)], edge_send.at[n, 0], edge_recv.at[n, p], partner
                    ).wait_recv()
            rim_nus = phases(rim_reluct)
            for p in range(2):
                rim[p, :, rim_own] = starts[0, p, :, rim_from]
                rim_drive[p, :, rim_own] = drive[0, p, :, rim_from]

                def put_rim_work(t, x):
                    rim_work[t, pl.ds(8, 24)] = x

                def put_rim_later(t, x):
                    rim_later[t, pl.ds(8, 24)] = x

                def put_rim_ends(t, x):
                    rim_ends[p, t] = x

                for a, put in ((rim.at[p], put_rim_work), (rim_work, put_rim_later)):
                    reluctivity(phases(a), rim_a, rim_b, rim_nus, 8, 24)
                    update(phases(a), rim_nus, rim_drive.at[p], rim_mobile, 8, 24, put)
                reluctivity(phases(rim_later), rim_a, rim_b, rim_nus, 8, 24)
                update(phases(rim_later), rim_nus, rim_drive.at[p], rim_mobile, 16, 8, put_rim_ends)
            rim_c = rim_gain[:, rim_out]
            k0 = rim_ends[0] - rim_c * rim[0, :, rim_out]
            k1 = rim_ends[1] - rim_c * rim[1, :, rim_out]
            rim_corr0[...] = k0
            rim_items[...] = jnp.where(chip7, rim_ends[1], rim_c * k0 + k1)
            rim_got[chip] = rim_items[...]

            def rim_copy(n):
                q = far(*OFFSETS[n])
                return remote(rim_items, rim_got.at[chip], rim_send.at[n], rim_recv.at[n], (2 * q + core, sp))

            for n, offset in enumerate(OFFSETS):
                @pl.when((far(*offset) > chip) | chip7)
                def _():
                    rim_copy(n).start()

            for ref, edge in zip(coefs, rim_coefs):
                ref[1, :, kept_at] = ref[0, :, kept]
                ref[1, :, beyond_at] = edge[:, rim_halo]
            drive[1, :, :, kept_at] = drive[0, :, :, kept]
            drive[1, :, :, beyond_at] = rim_drive[:, :, rim_halo]

        for cp in there:
            cp.wait_recv()
        c = carry_gain[it]
        c2 = c * c
        total = got[it, 7]
        sums[it, 0] = total
        for k in range(7):
            total = c2 * total + got[it, k]
            sums[it, k + 1] = total
        land = part(PAD + 16 * other, HALF) if it == 0 else inner
        their_land = part(PAD + 16 * core, HALF) if it == 0 else inner
        back = []
        for n, (dy, dx) in enumerate(OFFSETS):
            q = far(dy, dx)
            back.append(
                go(remote(sums.at[it, q], starts.at[it + 1, 0, chip, their_land], back_send.at[it, n], back_recv.at[it, n], (2 * q + other, sp)))
            )
        back.append(go(remote(sums.at[it, chip], starts.at[it + 1, 0, chip, their_land], back_send.at[it, 7], back_recv.at[it, 7], partner)))

        if it == 0:
            for n, (dy, dx) in enumerate(OFFSETS):
                @pl.when((source(dy, dx) < chip) | (source(dy, dx) == 7))
                def _():
                    rim_copy(n).wait_recv()
            rim_c = rim_gain[:, rim_out]
            rim_c2 = rim_c * rim_c
            total = rim_got[7]
            for k in range(7):
                total = jnp.where(k < chip, rim_c2 * total + rim_got[k], total)
            starts[1, 0, :, rim_at] = total
            starts[1, 1, :, rim_at] = rim_c * total + rim_corr0[...]
            outer_halo = go(
                remote(starts.at[1, :, :, rim_at], starts.at[1, :, :, part(PAD + 72 * other, 8)], halo_send, halo_recv, (pair + other, outer))
            )

        def spread(t):
            starts[it + 1, 1, t, land] = gain[it, t, inner] * starts[it + 1, 0, t, land] + corr0[it, t]

        if it == 0:
            for n in reversed(range(8)):
                back[n].wait_recv()
                spread(source(*OFFSETS[n]) if n < 7 else chip)
            outer_halo.wait_recv()
        else:
            outs = []
            for n in reversed(range(8)):
                back[n].wait_recv()
                t = source(*OFFSETS[n]) if n < 7 else chip
                spread(t)
                outs.append(
                    go(remote(starts.at[2, other, t, inner], out_s.at[t, own_half], outs_send.at[n], outs_recv.at[n], partner))
                )
                out_s[t, own_half] = starts[2, core, t, inner]

    cp_e.wait_recv()
    for cp in outs:
        cp.wait_recv()
    for cp in sends:
        cp.wait_send()
    for n, offset in enumerate(OFFSETS):
        @pl.when((far(*offset) > chip) | chip7)
        def _():
            rim_copy(n).wait_send()


def hand_out(s_ref, e_ref, starts_hbm, ends_hbm, buf, sem):
    copies = []
    for n, (src, dst) in enumerate(((e_ref, ends_hbm), (s_ref, starts_hbm))):
        for t in range(8):
            buf[n, 0, pl.ds(t, 128, stride=8), :] = src[t].T
        cp = pltpu.make_async_copy(buf.at[n], dst, sem.at[n])
        cp.start()
        copies.append(cp)
    for cp in copies:
        cp.wait()


def local(initial_starts, source, region, base_reluctivity, saturation, mobility):
    held = jax.ShapeDtypeStruct((8, 128, 128), F32)
    block = jax.ShapeDtypeStruct((1, 1024, 128), F32)
    hbm = pl.BlockSpec(memory_space=pltpu.HBM)
    in_vmem = pl.BlockSpec(memory_space=pltpu.VMEM)
    vmem = lambda *shape: pltpu.VMEM(shape + (128,), F32)
    ints = lambda *shape: pltpu.VMEM(shape + (128,), jnp.int32)
    table = pltpu.SMEM((8,), F32)
    sem = lambda *shape: pltpu.SemaphoreType.DMA(shape)
    one = pltpu.SemaphoreType.DMA
    args = (base_reluctivity, saturation, mobility, initial_starts, source, region)
    kept = pl.pallas_call(
        kernel,
        out_shape=(held, held),
        in_specs=[hbm] * 6,
        out_specs=(in_vmem, in_vmem),
        scratch_shapes=[
            table, table, table,
            vmem(1, 1024), vmem(1, 1024), ints(1024), vmem(8, 128), vmem(8, 128), ints(8, 128),
            vmem(3, 2, 8, ROWS), vmem(2, 2, 8, ROWS),
            vmem(2, 8, ROWS), vmem(2, 8, ROWS), vmem(2, 8, ROWS), vmem(2, 8, ROWS), vmem(2, HALF), vmem(10, ROWS), vmem(8, ROWS), vmem(10, ROWS),
            ints(8, EDGE), vmem(2, 8, EDGE), vmem(2, 8, EDGE), vmem(8, EDGE), vmem(8, EDGE), vmem(8, EDGE), vmem(8, EDGE),
            vmem(8, EDGE), vmem(8, EDGE), vmem(8, EDGE), vmem(2, 8, 8), vmem(8, 8), vmem(8, 8), vmem(8, 8, 8),
            vmem(2, 2, 8, HALF), vmem(2, 8, HALF), vmem(2, 8, HALF), vmem(2, 8, HALF), vmem(2, 8, HALF),
            pltpu.SemaphoreType.REGULAR((2,)), sem(4, 4), sem(2), sem(2), sem(2, 2), sem(2, 2), one, one,
            sem(2, 8), sem(2, 8), sem(2, 8), sem(2, 8), sem(7), sem(7), one, one,
            one, one, sem(8), sem(8),
        ],
        compiler_params=pltpu.CompilerParams(
            collective_id=0, has_side_effects=True, vmem_limit_bytes=40 * 2**20
        ),
        name="parareal",
    )(*[pltpu.with_memory_space_constraint(x, pltpu.HBM) for x in args])
    return pl.pallas_call(
        hand_out,
        out_shape=(block, block),
        in_specs=[in_vmem] * 2,
        out_specs=(hbm, hbm),
        scratch_shapes=[vmem(2, 1, 1024), sem(2)],
        compiler_params=pltpu.CompilerParams(vmem_limit_bytes=16 * 2**20),
        name="hand_out",
    )(*kept)


def solution(mesh):
    in_specs = (P("tm", None, "space"), P("tm", None, "space"), P(None, "space"), P(), P(), P())
    out_specs = (P("tm", None, "space"), P("tm", None, "space"))
    return jax.shard_map(local, mesh=mesh, in_specs=in_specs, out_specs=out_specs, check_vma=False)
```

```python
import jax
import jax.numpy as jnp
from jax import lax
from jax.experimental import pallas as pl
from jax.experimental.pallas import tpu as pltpu
from jax.sharding import PartitionSpec as P

MESH = pl.DeviceIdType.MESH
HALF = 64
OWN = 80
PAD = 8
MID = 16
ROWS = 96
EDGE = 40
F32 = jnp.float32
OFFSETS = ((1, 2), (1, 1), (1, 3), (0, 2), (1, 0), (0, 1), (0, 3))


def part(start, size):
    if not isinstance(start, int):
        start = pl.multiple_of(start, 8)
    return pl.ds(start, size)


def up(x, end):
    return jnp.where(lax.broadcasted_iota(jnp.int32, x.shape, 1) == 127, end, pltpu.roll(x, 127, 1))


def down(x, end):
    return jnp.where(lax.broadcasted_iota(jnp.int32, x.shape, 1) == 0, end, pltpu.roll(x, 1, 1))


def blocks(at, size):
    step = size // 2 if size >= 64 else size
    return [(at + k, step) for k in range(0, size, step)]


def reluctivity(a, coef_a, coef_b, nu, at, size):
    for start, step in blocks(at, size):
        rows = pl.ds(start, step)
        here = [x[rows] for x in a]
        for t in range(8):
            north = here[t + 1] if t < 7 else up(here[0], 0.0)
            south = here[t - 1] if t > 0 else down(here[7], 0.0)
            br = north - south
            bt = a[t][pl.ds(start + 1, step)] - a[t][pl.ds(start - 1, step)]
            nu[t][rows] = coef_a[t, rows] - coef_b[t, rows] / (4.0 + (br * br + bt * bt))


def turning(a, nu, here, mid, at, size):
    flux = (mid + nu[pl.ds(at + 1, size)]) * (a[pl.ds(at + 1, size)] - here)
    return flux + (mid + nu[pl.ds(at - 1, size)]) * (a[pl.ds(at - 1, size)] - here)


def update(a, nu, drive, mobile, at, size, put):
    for start, step in blocks(at, size):
        rows = pl.ds(start, step)
        mid, nu7, here, a7 = nu[0][rows], nu[7][rows], a[0][rows], a[7][rows]
        top = (nu7 + up(mid, nu7)) * (up(here, 0.0) - a7)
        below = down(top, 2.0 * mid * here)
        for t in range(8):
            if t < 7:
                following, next_nu = a[t + 1][rows], nu[t + 1][rows]
                above = (mid + next_nu) * (following - here)
            else:
                above = top
            total = turning(a[t], nu[t], here, mid, start, step) + (above - below) + drive[t, rows]
            put(t, pl.ds(start - at, step), here + mobile[t, rows] * total)
            below, here, mid = above, following, next_nu


def kernel(
    base_hbm, satur_hbm, mob_hbm, a_hbm, j_hbm, r_hbm, out_s, out_e,
    base_ref, satur_ref, mob_ref, in_a, in_j, in_r, ta, tj, tr, starts, drive,
    coef_a, coef_b, mobile, gain, carry_gain, reluct, work, later,
    rim_r, rim, rim_drive, rim_a, rim_b, rim_mobile, rim_gain, rim_reluct, rim_work, rim_later, rim_ends, rim_corr0, rim_items, rim_got,
    ends, corr0, items, got, sums,
    word, in_sem, pair_send, pair_recv, edge_send, edge_recv, reg_send, reg_recv,
    there_send, there_recv, back_send, back_recv, rim_send, rim_recv, halo_send, halo_recv,
    oute_send, oute_recv, outs_send, outs_recv,
):
    tm = lax.axis_index("tm")
    sp = lax.axis_index("space")
    core = lax.rem(tm, 2)
    other = 1 - core
    pair = tm - core
    chip = tm // 2
    right = lax.rem(sp + 1, 16)
    left = lax.rem(sp + 15, 16)
    outer = jnp.where(core == 0, left, right)
    partner = (pair + other, sp)

    def far(dy, dx):
        return 4 * lax.rem(chip // 4 + dy, 2) + lax.rem(lax.rem(chip, 4) + dx, 4)

    def source(dy, dx):
        return far(dy, (4 - dx) % 4)

    def remote(src, dst, send, recv, target):
        return pltpu.make_async_remote_copy(src, dst, send, recv, device_id=target, device_id_type=MESH)

    barrier = pltpu.get_barrier_semaphore()
    tellers = [(2 * far(1, 0) + core, sp), (2 * far(1, 0) + other, sp), partner]
    near = [(2 * far(0, dx) + core, sp) for dx in (1, 3, 2)] + tellers
    for device in near:
        pl.semaphore_signal(barrier, inc=1, device_id=device, device_id_type=MESH)

    loads = []
    for n, (src, dst, pieces) in enumerate(((a_hbm.at[0], in_a.at[0], 4), (j_hbm.at[0], in_j.at[0], 4), (r_hbm, in_r, 4))):
        size = 1024 // pieces
        loads.append([])
        for k in range(pieces):
            cp = pltpu.make_async_copy(src.at[pl.ds(size * k, size)], dst.at[pl.ds(size * k, size)], in_sem.at[n, k])
            cp.start()
            loads[-1].append(cp)
    tables = []
    for n, (src, dst) in enumerate(((base_hbm, base_ref), (satur_hbm, satur_ref), (mob_hbm, mob_ref))):
        cp = pltpu.make_async_copy(src, dst, in_sem.at[3, n])
        cp.start()
        tables.append(cp)

    def arrived(copies):
        for cp in copies:
            cp.wait()

    def turn(src, dst):
        for t in range(8):
            dst[t] = src[pl.ds(t, 128, stride=8), :].T

    sends = []

    def go(cp):
        cp.start()
        sends.append(cp)
        return cp

    wide = pl.ds(PAD, OWN)
    inner = pl.ds(MID, HALF)
    mine = part((128 - OWN) * core, OWN)
    theirs = part((128 - OWN) * other, OWN)
    rim_halo = part(8 + 16 * core, 8)
    rim_own = part(8 + 8 * other, 16)
    rim_from = part(PAD + 64 * core, 16)
    rim_out = pl.ds(16, 8)
    kept, kept_at = part(PAD + 8 * core, 72), part(PAD + 8 * other, 72)
    window, their_window = part(8 * other, 56), part(8 * core, 56)
    rim_at = part(MID + 56 * core, 8)
    own_half = part(HALF * core, HALF)

    arrived(loads[0])
    turn(in_a.at[0], ta)

    arrived(loads[1])
    turn(in_j.at[0], tj)
    arrived(loads[2])
    turn(in_r, tr)
    arrived(tables)
    base = [base_ref[k] for k in range(8)]
    satur = [satur_ref[k] for k in range(8)]
    full = lambda x: jnp.full((8, 128), x, F32)
    tab_a = [full(0.5 * b * (1.0 + s)) for b, s in zip(base, satur)]
    tab_b = [full(2.0 * b * s) for b, s in zip(base, satur)]
    tab_m = [full(mob_ref[k]) for k in range(8)]
    tab_c = [1.0 / (1.0 + 12.0 * m * full(b)) for b, m in zip(base, tab_m)]

    def look_up(src, first, size, put):
        for t in range(8):
            for k in range(0, size, 8):
                r = src[t, part(first + k, 8)]
                bits = [(r & 1) != 0, (r & 2) != 0, (r & 4) != 0]
                for n, tab in enumerate((tab_a, tab_b, tab_m, tab_c)):
                    level = tab
                    for bit in bits:
                        level = [jnp.where(bit, hi, lo) for lo, hi in zip(level[::2], level[1::2])]
                    put(n, t, k, level[0])

    coefs = (coef_a, coef_b, mobile, gain)
    rim_coefs = (rim_a, rim_b, rim_mobile, rim_gain)

    def put_own(n, t, k, x):
        coefs[n][0, t, pl.ds(PAD + k, 8)] = x

    def put_rim(n, t, k, x):
        rim_coefs[n][t, rim_halo] = x

    look_up(tr, (128 - OWN) * core, OWN, put_own)
    for it, first in enumerate((8 + 48 * other, HALF * other)):
        for k in range(0, HALF, 8):
            r = tr[chip, part(first + k, 8)]
            level = tab_c
            for bit in ((r & 1) != 0, (r & 2) != 0, (r & 4) != 0):
                level = [jnp.where(bit, hi, lo) for lo, hi in zip(level[::2], level[1::2])]
            carry_gain[it, pl.ds(k, 8)] = level[0]
    starts[0, core, :, wide] = ta[:, mine]
    drive[0, core, :, wide] = tj[:, mine]

    even = lax.rem(sp, 2) == 0
    edge_sources = [(pair, outer), (pair + 1, outer)]

    def greet(devices):
        for device in devices:
            pl.semaphore_signal(barrier, inc=1, device_id=device, device_id_type=MESH)

    @pl.when(even)
    def _():
        pl.semaphore_wait(barrier, len(near))
        greet(edge_sources + [(tm, jnp.where(core == 0, right, left))])

    @pl.when(jnp.logical_not(even))
    def _():
        pl.semaphore_wait(barrier, len(near) + 3)
        greet(edge_sources)

    for device in tellers:
        pl.semaphore_signal(word, inc=1, device_id=device, device_id_type=MESH)

    def edge_copies():
        copies = []
        for n, (src, dst) in enumerate(((ta, rim.at[0]), (tj, rim_drive))):
            copies.append(
                remote(src.at[:, pl.ds(120, 8)], dst.at[core, :, pl.ds(8, 8)], edge_send.at[n, 0], edge_recv.at[n, core], (pair, right))
            )
            copies.append(
                remote(src.at[:, pl.ds(0, 8)], dst.at[core, :, pl.ds(24, 8)], edge_send.at[n, 1], edge_recv.at[n, core], (pair + 1, left))
            )
        ahead = (tm, jnp.where(core == 0, right, left))
        copies.append(remote(tr.at[:, part(120 * other, 8)], rim_r.at[:, rim_halo], reg_send, reg_recv, ahead))
        return copies

    def send_pair(n, src, dst):
        return go(remote(src.at[:, theirs], dst.at[core, :, wide], pair_send.at[n], pair_recv.at[n], partner))

    @pl.when(jnp.logical_not(even))
    def _():
        for cp in edge_copies():
            cp.start()

    pairs = [send_pair(0, ta, starts.at[0]), send_pair(1, tj, drive.at[0])]

    chip7 = chip == 7

    def phases(ref):
        return [ref.at[t] for t in range(8)]

    nus = [reluct.at[t + 1] for t in range(8)]
    lates = [later.at[t + 1] for t in range(8)]

    def put_work(t, rows, x):
        work[t, pl.ds(PAD + rows.start, rows.size)] = x

    def put_later(t, rows, x):
        later[t + 1, pl.ds(PAD + rows.start, rows.size)] = x

    def two_steps(it, p):
        ca, cb, cm, force = coef_a.at[it], coef_b.at[it], mobile.at[it], drive.at[it, p]
        a = phases(starts.at[it, p])
        reluctivity(a, ca, cb, nus, PAD, OWN)
        update(a, nus, force, cm, PAD, OWN, put_work)
        a = phases(work)
        reluctivity(a, ca, cb, nus, PAD, OWN)
        update(a, nus, force, cm, PAD, OWN, put_later)
        reluctivity(lates, ca, cb, nus, PAD, OWN)

    def last_step(it, p, t):
        here, mid = later[t + 1, inner], reluct[t + 1, inner]
        total = turning(later.at[t + 1], reluct.at[t + 1], here, mid, MID, HALF) + drive[it, p, t, inner]
        total += (mid + reluct[t + 2, inner]) * (later[t + 2, inner] - here)
        total += (mid + reluct[t, inner]) * (later[t, inner] - here)
        return here + mobile[it, t, inner] * total

    for it in range(2):
        def put_ends(t, rows, x):
            ends[it, core, t, rows] = x
            if it == 1:
                out_e[t, part(HALF * core + rows.start, rows.size)] = x

        two_steps(it, core)
        update(lates, nus, drive.at[it, core], mobile.at[it], MID, HALF, put_ends)
        if it == 0:
            for cp in pairs:
                cp.wait_recv()
        two_steps(it, other)
        later[0, wide] = down(later[8, wide], 0.0)
        later[9, wide] = up(later[1, wide], 0.0)
        reluct[0, wide] = down(reluct[8, wide], reluct[1, wide])
        reluct[9, wide] = up(reluct[1, wide], reluct[8, wide])

        def finish(t):
            theirs_end = last_step(it, other, t)
            ends[it, other, t] = theirs_end
            own_end = ends[it, core, t]
            c = gain[it, t, inner]
            own_corr = own_end - c * starts[it, core, t, inner]
            theirs_corr = theirs_end - c * starts[it, other, t, inner]
            first = jnp.where(core == 0, own_corr, theirs_corr)
            second = jnp.where(core == 0, theirs_corr, own_corr)
            corr0[it, t] = first
            items[it, t] = jnp.where(chip7, jnp.where(core == 0, theirs_end, own_end), c * first + second)

        if it == 0:
            pl.semaphore_wait(word, len(tellers))
        there = []
        for n, (dy, dx) in enumerate(OFFSETS):
            q = far(dy, dx)
            finish(q)
            mine_out = items.at[it, q] if it == 0 else items.at[it, q, window]
            there.append(
                go(remote(mine_out, got.at[it, chip] if it == 0 else got.at[it, chip, window], there_send.at[it, n], there_recv.at[it, n], (2 * q + other, sp)))
            )
        finish(chip)
        mine_out = items.at[it, chip] if it == 0 else items.at[it, chip, window]
        land = got.at[it, chip] if it == 0 else got.at[it, chip, window]
        there.append(go(remote(mine_out, land, there_send.at[it, 7], there_recv.at[it, 7], partner)))

        if it == 0:
            @pl.when(even)
            def _():
                pl.semaphore_wait(barrier, 2)
                for cp in edge_copies():
                    cp.start()

            edge_copies()[-1].wait_recv()
            look_up(rim_r, 8 + 16 * core, 8, put_rim)
            for ref, into in zip(coefs, rim_coefs):
                into[:, rim_own] = ref[0, :, rim_from]
            for n in range(2):
                for p in range(2):
                    remote(
                        ta.at[:, pl.ds(0, 8)], rim.at[0, 0, :, pl.ds(8, 8)], edge_send.at[n, 0], edge_recv.at[n, p], partner
                    ).wait_recv()
            rim_drive[:, :, rim_own] = drive[0, :, :, rim_from]
            rim[0, :, :, rim_own] = starts[0, :, :, rim_from]
        else:
            outer_halo.wait_recv()
            rim[1, :, :, rim_own] = starts[1, :, :, part(MID + 48 * core, 16)]
        rim_nus = phases(rim_reluct)
        for p in range(2):
            def put_rim_work(t, rows, x):
                rim_work[t, pl.ds(8, 24)] = x

            def put_rim_later(t, rows, x):
                rim_later[t, pl.ds(8, 24)] = x

            def put_rim_ends(t, rows, x):
                rim_ends[p, t] = x

            for a, put in ((rim.at[it, p], put_rim_work), (rim_work, put_rim_later)):
                reluctivity(phases(a), rim_a, rim_b, rim_nus, 8, 24)
                update(phases(a), rim_nus, rim_drive.at[p], rim_mobile, 8, 24, put)
            reluctivity(phases(rim_later), rim_a, rim_b, rim_nus, 8, 24)
            update(phases(rim_later), rim_nus, rim_drive.at[p], rim_mobile, 16, 8, put_rim_ends)
        rim_c = rim_gain[:, rim_out]
        k0 = rim_ends[0] - rim_c * rim[it, 0, :, rim_out]
        k1 = rim_ends[1] - rim_c * rim[it, 1, :, rim_out]
        rim_corr0[...] = k0
        rim_items[it] = jnp.where(chip7, rim_ends[1], rim_c * k0 + k1)
        rim_got[it, chip] = rim_items[it]

        def rim_copy(it, n):
            q = far(*OFFSETS[n])
            return remote(rim_items.at[it], rim_got.at[it, chip], rim_send.at[it, n], rim_recv.at[it, n], (2 * q + core, sp))

        for n, offset in enumerate(OFFSETS):
            @pl.when((far(*offset) > chip) | chip7)
            def _():
                rim_copy(it, n).start()

        if it == 1:
            ends[1, other, :, part(56 * core, 8)] = rim_ends[other]
            out_e[:, part(120 * core, 8)] = rim_ends[core]
            cp_e = go(remote(ends.at[1, other], out_e.at[:, own_half], oute_send, oute_recv, partner))
        else:
            for ref in coefs:
                ref[1, :, kept_at] = ref[0, :, kept]
            drive[1, :, :, kept_at] = drive[0, :, :, kept]

        for cp in there:
            cp.wait_recv()
        c = carry_gain[it]
        c2 = c * c
        total = got[it, 7]
        sums[it, 0] = total
        for k in range(7):
            total = c2 * total + got[it, k]
            sums[it, k + 1] = total
        rows = pl.ds(0, HALF) if it == 0 else window
        their_rows = pl.ds(0, HALF) if it == 0 else their_window
        frame_rows = inner if it == 0 else part(MID + 8 * other, 56)
        land = part(PAD + 16 * other, HALF) if it == 0 else frame_rows
        their_land = part(PAD + 16 * core, HALF) if it == 0 else part(MID + 8 * core, 56)
        back = []
        for n, (dy, dx) in enumerate(OFFSETS):
            q = far(dy, dx)
            back.append(
                go(remote(sums.at[it, q, their_rows], starts.at[it + 1, 0, chip, their_land], back_send.at[it, n], back_recv.at[it, n], (2 * q + other, sp)))
            )
        back.append(go(remote(sums.at[it, chip, their_rows], starts.at[it + 1, 0, chip, their_land], back_send.at[it, 7], back_recv.at[it, 7], partner)))

        for n, (dy, dx) in enumerate(OFFSETS):
            @pl.when((source(dy, dx) < chip) | (source(dy, dx) == 7))
            def _():
                rim_copy(it, n).wait_recv()
        rim_c = rim_gain[:, rim_out]
        rim_c2 = rim_c * rim_c
        total = rim_got[it, 7]
        for k in range(7):
            total = jnp.where(k < chip, rim_c2 * total + rim_got[it, k], total)
        starts[it + 1, 0, :, rim_at] = total
        starts[it + 1, 1, :, rim_at] = rim_c * total + rim_corr0[...]
        if it == 0:
            outer_halo = go(
                remote(starts.at[1, :, :, rim_at], rim.at[1, :, :, part(8 + 16 * other, 8)], halo_send, halo_recv, (pair + other, outer))
            )
        else:
            outs = [
                go(remote(starts.at[2, other, :, rim_at], out_s.at[:, part(120 * core, 8)], outs_send.at[8], outs_recv.at[8], partner))
            ]
            out_s[:, part(120 * core, 8)] = starts[2, core, :, rim_at]

        def spread(t):
            starts[it + 1, 1, t, land] = gain[it, t, frame_rows] * starts[it + 1, 0, t, land] + corr0[it, t, rows]

        if it == 0:
            for n in reversed(range(8)):
                back[n].wait_recv()
                spread(source(*OFFSETS[n]) if n < 7 else chip)
        else:
            out_rows = part(HALF * core + 8 * other, 56)
            for n in reversed(range(8)):
                back[n].wait_recv()
                t = source(*OFFSETS[n]) if n < 7 else chip
                spread(t)
                outs.append(
                    go(remote(starts.at[2, other, t, land], out_s.at[t, out_rows], outs_send.at[n], outs_recv.at[n], partner))
                )
                out_s[t, out_rows] = starts[2, core, t, land]

    for cp in edge_copies():
        cp.wait_send()
    cp_e.wait_recv()
    for cp in outs:
        cp.wait_recv()
    for cp in sends:
        cp.wait_send()
    for n, offset in enumerate(OFFSETS):
        @pl.when((far(*offset) > chip) | chip7)
        def _():
            for it in range(2):
                rim_copy(it, n).wait_send()


def hand_out(s_ref, e_ref, starts_hbm, ends_hbm, buf, sem):
    copies = []
    for n, (src, dst) in enumerate(((e_ref, ends_hbm), (s_ref, starts_hbm))):
        for t in range(8):
            buf[n, 0, pl.ds(t, 128, stride=8), :] = src[t].T
        cp = pltpu.make_async_copy(buf.at[n], dst, sem.at[n])
        cp.start()
        copies.append(cp)
    for cp in copies:
        cp.wait()


def local(initial_starts, source, region, base_reluctivity, saturation, mobility):
    held = jax.ShapeDtypeStruct((8, 128, 128), F32)
    block = jax.ShapeDtypeStruct((1, 1024, 128), F32)
    hbm = pl.BlockSpec(memory_space=pltpu.HBM)
    in_vmem = pl.BlockSpec(memory_space=pltpu.VMEM)
    vmem = lambda *shape: pltpu.VMEM(shape + (128,), F32)
    ints = lambda *shape: pltpu.VMEM(shape + (128,), jnp.int32)
    table = pltpu.SMEM((8,), F32)
    sem = lambda *shape: pltpu.SemaphoreType.DMA(shape)
    one = pltpu.SemaphoreType.DMA
    args = (base_reluctivity, saturation, mobility, initial_starts, source, region)
    kept = pl.pallas_call(
        kernel,
        out_shape=(held, held),
        in_specs=[hbm] * 6,
        out_specs=(in_vmem, in_vmem),
        scratch_shapes=[
            table, table, table,
            vmem(1, 1024), vmem(1, 1024), ints(1024), vmem(8, 128), vmem(8, 128), ints(8, 128),
            vmem(3, 2, 8, ROWS), vmem(2, 2, 8, ROWS),
            vmem(2, 8, ROWS), vmem(2, 8, ROWS), vmem(2, 8, ROWS), vmem(2, 8, ROWS), vmem(2, HALF), vmem(10, ROWS), vmem(8, ROWS), vmem(10, ROWS),
            ints(8, EDGE), vmem(2, 2, 8, EDGE), vmem(2, 8, EDGE), vmem(8, EDGE), vmem(8, EDGE), vmem(8, EDGE), vmem(8, EDGE),
            vmem(8, EDGE), vmem(8, EDGE), vmem(8, EDGE), vmem(2, 8, 8), vmem(8, 8), vmem(2, 8, 8), vmem(2, 8, 8, 8),
            vmem(2, 2, 8, HALF), vmem(2, 8, HALF), vmem(2, 8, HALF), vmem(2, 8, HALF), vmem(2, 8, HALF),
            pltpu.SemaphoreType.REGULAR, sem(4, 4), sem(2), sem(2), sem(2, 2), sem(2, 2), one, one,
            sem(2, 8), sem(2, 8), sem(2, 8), sem(2, 8), sem(2, 7), sem(2, 7), one, one,
            one, one, sem(9), sem(9),
        ],
        compiler_params=pltpu.CompilerParams(
            collective_id=0, has_side_effects=True, vmem_limit_bytes=40 * 2**20
        ),
        name="parareal",
    )(*[pltpu.with_memory_space_constraint(x, pltpu.HBM) for x in args])
    return pl.pallas_call(
        hand_out,
        out_shape=(block, block),
        in_specs=[in_vmem] * 2,
        out_specs=(hbm, hbm),
        scratch_shapes=[vmem(2, 1, 1024), sem(2)],
        compiler_params=pltpu.CompilerParams(vmem_limit_bytes=16 * 2**20),
        name="hand_out",
    )(*kept)


def solution(mesh):
    in_specs = (P("tm", None, "space"), P("tm", None, "space"), P(None, "space"), P(), P(), P())
    out_specs = (P("tm", None, "space"), P("tm", None, "space"))
    return jax.shard_map(local, mesh=mesh, in_specs=in_specs, out_specs=out_specs, check_vma=False)
```

```python
import jax
import jax.numpy as jnp
from jax import lax
from jax.experimental import pallas as pl
from jax.experimental.pallas import tpu as pltpu
from jax.sharding import PartitionSpec as P

MESH = pl.DeviceIdType.MESH
HALF = 64
OWN = 80
PAD = 8
MID = 16
ROWS = 96
EDGE = 40
F32 = jnp.float32
OFFSETS = ((1, 2), (1, 1), (1, 3), (0, 2), (1, 0), (0, 1), (0, 3))


def part(start, size):
    if not isinstance(start, int):
        start = pl.multiple_of(start, 8)
    return pl.ds(start, size)


def up(x, end):
    return jnp.where(lax.broadcasted_iota(jnp.int32, x.shape, 1) == 127, end, pltpu.roll(x, 127, 1))


def down(x, end):
    return jnp.where(lax.broadcasted_iota(jnp.int32, x.shape, 1) == 0, end, pltpu.roll(x, 1, 1))


def blocks(at, size):
    step = size // 2 if size >= 64 else size
    return [(at + k, step) for k in range(0, size, step)]


def reluctivity(a, coef_a, coef_b, nu, at, size):
    for start, step in blocks(at, size):
        rows = pl.ds(start, step)
        here = [x[rows] for x in a]
        for t in range(8):
            north = here[t + 1] if t < 7 else up(here[0], 0.0)
            south = here[t - 1] if t > 0 else down(here[7], 0.0)
            br = north - south
            bt = a[t][pl.ds(start + 1, step)] - a[t][pl.ds(start - 1, step)]
            nu[t][rows] = coef_a[t, rows] - coef_b[t, rows] / (4.0 + (br * br + bt * bt))


def turning(a, nu, here, mid, at, size):
    flux = (mid + nu[pl.ds(at + 1, size)]) * (a[pl.ds(at + 1, size)] - here)
    return flux + (mid + nu[pl.ds(at - 1, size)]) * (a[pl.ds(at - 1, size)] - here)


def update(a, nu, drive, mobile, at, size, put):
    for start, step in blocks(at, size):
        rows = pl.ds(start, step)
        mid, nu7, here, a7 = nu[0][rows], nu[7][rows], a[0][rows], a[7][rows]
        top = (nu7 + up(mid, nu7)) * (up(here, 0.0) - a7)
        below = down(top, 2.0 * mid * here)
        for t in range(8):
            if t < 7:
                following, next_nu = a[t + 1][rows], nu[t + 1][rows]
                above = (mid + next_nu) * (following - here)
            else:
                above = top
            total = turning(a[t], nu[t], here, mid, start, step) + (above - below) + drive[t, rows]
            put(t, pl.ds(start - at, step), here + mobile[t, rows] * total)
            below, here, mid = above, following, next_nu


def kernel(
    base_hbm, satur_hbm, mob_hbm, a_hbm, j_hbm, r_hbm, out_s, out_e,
    base_ref, satur_ref, mob_ref, in_a, in_j, in_r, ta, tj, tr, starts, drive,
    coef_a, coef_b, mobile, gain, carry_gain, reluct, work, later,
    rim_r, rim, rim_drive, rim_a, rim_b, rim_mobile, rim_gain, rim_reluct, rim_work, rim_later, rim_ends, rim_corr0, rim_items, rim_got,
    ends, corr0, items, got, sums,
    word, in_sem, pair_send, pair_recv, edge_send, edge_recv, reg_send, reg_recv,
    there_send, there_recv, back_send, back_recv, rim_send, rim_recv, halo_send, halo_recv,
    oute_send, oute_recv, outs_send, outs_recv,
):
    tm = lax.axis_index("tm")
    sp = lax.axis_index("space")
    core = lax.rem(tm, 2)
    other = 1 - core
    pair = tm - core
    chip = tm // 2
    right = lax.rem(sp + 1, 16)
    left = lax.rem(sp + 15, 16)
    outer = jnp.where(core == 0, left, right)
    partner = (pair + other, sp)

    def far(dy, dx):
        return 4 * lax.rem(chip // 4 + dy, 2) + lax.rem(lax.rem(chip, 4) + dx, 4)

    def source(dy, dx):
        return far(dy, (4 - dx) % 4)

    def remote(src, dst, send, recv, target):
        return pltpu.make_async_remote_copy(src, dst, send, recv, device_id=target, device_id_type=MESH)

    barrier = pltpu.get_barrier_semaphore()
    tellers = [(2 * far(1, 0) + core, sp), (2 * far(1, 0) + other, sp), partner]
    near = [(2 * far(0, dx) + core, sp) for dx in (1, 3, 2)] + tellers
    plane = lax.rem(sp, 8)
    is_first, is_last = plane == 0, plane == 7
    edge_sources = [(pair, outer), (pair + 1, outer)]

    def greet(devices):
        for device in devices:
            pl.semaphore_signal(barrier, inc=1, device_id=device, device_id_type=MESH)

    greet(near)
    later_greeting = (is_first & (core == 0)) | (is_last & (core == 1))

    @pl.when(jnp.logical_not(later_greeting))
    def _():
        greet(edge_sources)

    loads = []
    for n, (src, dst, pieces) in enumerate(((a_hbm.at[0], in_a.at[0], 4), (j_hbm.at[0], in_j.at[0], 4), (r_hbm, in_r, 4))):
        size = 1024 // pieces
        loads.append([])
        for k in range(pieces):
            cp = pltpu.make_async_copy(src.at[pl.ds(size * k, size)], dst.at[pl.ds(size * k, size)], in_sem.at[n, k])
            cp.start()
            loads[-1].append(cp)
    tables = []
    for n, (src, dst) in enumerate(((base_hbm, base_ref), (satur_hbm, satur_ref), (mob_hbm, mob_ref))):
        cp = pltpu.make_async_copy(src, dst, in_sem.at[3, n])
        cp.start()
        tables.append(cp)

    def arrived(copies):
        for cp in copies:
            cp.wait()

    def turn(src, dst):
        for t in range(8):
            dst[t] = src[pl.ds(t, 128, stride=8), :].T

    sends = []

    def go(cp):
        cp.start()
        sends.append(cp)
        return cp

    wide = pl.ds(PAD, OWN)
    inner = pl.ds(MID, HALF)
    mine = part((128 - OWN) * core, OWN)
    theirs = part((128 - OWN) * other, OWN)
    rim_halo = part(8 + 16 * core, 8)
    rim_own = part(8 + 8 * other, 16)
    rim_from = part(PAD + 64 * core, 16)
    rim_out = pl.ds(16, 8)
    kept, kept_at = part(PAD + 8 * core, 72), part(PAD + 8 * other, 72)
    window, their_window = part(8 * other, 56), part(8 * core, 56)
    rim_at = part(MID + 56 * core, 8)
    own_half = part(HALF * core, HALF)

    arrived(loads[0])
    turn(in_a.at[0], ta)

    arrived(loads[1])
    turn(in_j.at[0], tj)
    arrived(loads[2])
    turn(in_r, tr)
    arrived(tables)
    base = [base_ref[k] for k in range(8)]
    satur = [satur_ref[k] for k in range(8)]
    full = lambda x: jnp.full((8, 128), x, F32)
    tab_a = [full(0.5 * b * (1.0 + s)) for b, s in zip(base, satur)]
    tab_b = [full(2.0 * b * s) for b, s in zip(base, satur)]
    tab_m = [full(mob_ref[k]) for k in range(8)]
    tab_c = [1.0 / (1.0 + 12.0 * m * full(b)) for b, m in zip(base, tab_m)]

    def look_up(src, first, size, put):
        for t in range(8):
            for k in range(0, size, 8):
                r = src[t, part(first + k, 8)]
                bits = [(r & 1) != 0, (r & 2) != 0, (r & 4) != 0]
                for n, tab in enumerate((tab_a, tab_b, tab_m, tab_c)):
                    level = tab
                    for bit in bits:
                        level = [jnp.where(bit, hi, lo) for lo, hi in zip(level[::2], level[1::2])]
                    put(n, t, k, level[0])

    coefs = (coef_a, coef_b, mobile, gain)
    rim_coefs = (rim_a, rim_b, rim_mobile, rim_gain)

    def put_own(n, t, k, x):
        coefs[n][0, t, pl.ds(PAD + k, 8)] = x

    def put_rim(n, t, k, x):
        rim_coefs[n][t, rim_halo] = x

    look_up(tr, (128 - OWN) * core, OWN, put_own)
    for it, first in enumerate((8 + 48 * other, HALF * other)):
        for k in range(0, HALF, 8):
            r = tr[chip, part(first + k, 8)]
            level = tab_c
            for bit in ((r & 1) != 0, (r & 2) != 0, (r & 4) != 0):
                level = [jnp.where(bit, hi, lo) for lo, hi in zip(level[::2], level[1::2])]
            carry_gain[it, pl.ds(k, 8)] = level[0]
    starts[0, core, :, wide] = ta[:, mine]
    drive[0, core, :, wide] = tj[:, mine]

    @pl.when(is_first)
    def _():
        pl.semaphore_wait(barrier, len(near) + 1)
        greet([(pair + 1, left)])

        @pl.when(core == 0)
        def _():
            greet([(pair, left)])

    @pl.when(is_last & (core == 1))
    def _():
        pl.semaphore_wait(barrier, len(near) + 3)
        greet(edge_sources)

    @pl.when(jnp.logical_not(is_first | (is_last & (core == 1))))
    def _():
        pl.semaphore_wait(barrier, len(near) + 2)

    for device in tellers:
        pl.semaphore_signal(word, inc=1, device_id=device, device_id_type=MESH)

    def right_edge(n, src, dst):
        return remote(src.at[:, pl.ds(120, 8)], dst.at[core, :, pl.ds(8, 8)], edge_send.at[n, 0], edge_recv.at[n, core], (pair, right))

    def left_edge(n, src, dst):
        return remote(src.at[:, pl.ds(0, 8)], dst.at[core, :, pl.ds(24, 8)], edge_send.at[n, 1], edge_recv.at[n, core], (pair + 1, left))

    def region_edge():
        ahead = (tm, jnp.where(core == 0, right, left))
        return remote(tr.at[:, part(120 * other, 8)], rim_r.at[:, rim_halo], reg_send, reg_recv, ahead)

    edges = ((0, ta, rim.at[0]), (1, tj, rim_drive))

    def send_pair(n, src, dst):
        return go(remote(src.at[:, theirs], dst.at[core, :, wide], pair_send.at[n], pair_recv.at[n], partner))

    for edge in edges:
        right_edge(*edge).start()

        @pl.when(jnp.logical_not(is_first))
        def _():
            left_edge(*edge).start()

    @pl.when(jnp.logical_not(is_first & (core == 1)))
    def _():
        region_edge().start()

    pairs = [send_pair(0, ta, starts.at[0]), send_pair(1, tj, drive.at[0])]

    chip7 = chip == 7

    def phases(ref):
        return [ref.at[t] for t in range(8)]

    nus = [reluct.at[t + 1] for t in range(8)]
    lates = [later.at[t + 1] for t in range(8)]

    def put_work(t, rows, x):
        work[t, pl.ds(PAD + rows.start, rows.size)] = x

    def put_later(t, rows, x):
        later[t + 1, pl.ds(PAD + rows.start, rows.size)] = x

    def two_steps(it, p):
        ca, cb, cm, force = coef_a.at[it], coef_b.at[it], mobile.at[it], drive.at[it, p]
        a = phases(starts.at[it, p])
        reluctivity(a, ca, cb, nus, PAD, OWN)
        update(a, nus, force, cm, PAD, OWN, put_work)
        a = phases(work)
        reluctivity(a, ca, cb, nus, PAD, OWN)
        update(a, nus, force, cm, PAD, OWN, put_later)
        reluctivity(lates, ca, cb, nus, PAD, OWN)

    def last_step(it, p, t):
        here, mid = later[t + 1, inner], reluct[t + 1, inner]
        total = turning(later.at[t + 1], reluct.at[t + 1], here, mid, MID, HALF) + drive[it, p, t, inner]
        total += (mid + reluct[t + 2, inner]) * (later[t + 2, inner] - here)
        total += (mid + reluct[t, inner]) * (later[t, inner] - here)
        return here + mobile[it, t, inner] * total

    for it in range(2):
        def put_ends(t, rows, x):
            ends[it, core, t, rows] = x
            if it == 1:
                out_e[t, part(HALF * core + rows.start, rows.size)] = x

        two_steps(it, core)
        update(lates, nus, drive.at[it, core], mobile.at[it], MID, HALF, put_ends)
        if it == 0:
            for cp in pairs:
                cp.wait_recv()
        two_steps(it, other)
        later[0, wide] = down(later[8, wide], 0.0)
        later[9, wide] = up(later[1, wide], 0.0)
        reluct[0, wide] = down(reluct[8, wide], reluct[1, wide])
        reluct[9, wide] = up(reluct[1, wide], reluct[8, wide])

        def finish(t):
            theirs_end = last_step(it, other, t)
            ends[it, other, t] = theirs_end
            own_end = ends[it, core, t]
            c = gain[it, t, inner]
            own_corr = own_end - c * starts[it, core, t, inner]
            theirs_corr = theirs_end - c * starts[it, other, t, inner]
            first = jnp.where(core == 0, own_corr, theirs_corr)
            second = jnp.where(core == 0, theirs_corr, own_corr)
            corr0[it, t] = first
            items[it, t] = jnp.where(chip7, jnp.where(core == 0, theirs_end, own_end), c * first + second)

        if it == 0:
            pl.semaphore_wait(word, len(tellers))
        there = []
        for n, (dy, dx) in enumerate(OFFSETS):
            q = far(dy, dx)
            finish(q)
            mine_out = items.at[it, q] if it == 0 else items.at[it, q, window]
            there.append(
                go(remote(mine_out, got.at[it, chip] if it == 0 else got.at[it, chip, window], there_send.at[it, n], there_recv.at[it, n], (2 * q + other, sp)))
            )
        finish(chip)
        mine_out = items.at[it, chip] if it == 0 else items.at[it, chip, window]
        land = got.at[it, chip] if it == 0 else got.at[it, chip, window]
        there.append(go(remote(mine_out, land, there_send.at[it, 7], there_recv.at[it, 7], partner)))

        if it == 0:
            @pl.when(is_first)
            def _():
                pl.semaphore_wait(barrier, 1)
                for edge in edges:
                    left_edge(*edge).start()

                @pl.when(core == 1)
                def _():
                    region_edge().start()

            region_edge().wait_recv()
            look_up(rim_r, 8 + 16 * core, 8, put_rim)
            for ref, into in zip(coefs, rim_coefs):
                into[:, rim_own] = ref[0, :, rim_from]
            for n in range(2):
                for p in range(2):
                    remote(
                        ta.at[:, pl.ds(0, 8)], rim.at[0, 0, :, pl.ds(8, 8)], edge_send.at[n, 0], edge_recv.at[n, p], partner
                    ).wait_recv()
            rim_drive[:, :, rim_own] = drive[0, :, :, rim_from]
            rim[0, :, :, rim_own] = starts[0, :, :, rim_from]
        else:
            outer_halo.wait_recv()
            rim[1, :, :, rim_own] = starts[1, :, :, part(MID + 48 * core, 16)]
        rim_nus = phases(rim_reluct)
        for p in range(2):
            def put_rim_work(t, rows, x):
                rim_work[t, pl.ds(8, 24)] = x

            def put_rim_later(t, rows, x):
                rim_later[t, pl.ds(8, 24)] = x

            def put_rim_ends(t, rows, x):
                rim_ends[p, t] = x

            for a, put in ((rim.at[it, p], put_rim_work), (rim_work, put_rim_later)):
                reluctivity(phases(a), rim_a, rim_b, rim_nus, 8, 24)
                update(phases(a), rim_nus, rim_drive.at[p], rim_mobile, 8, 24, put)
            reluctivity(phases(rim_later), rim_a, rim_b, rim_nus, 8, 24)
            update(phases(rim_later), rim_nus, rim_drive.at[p], rim_mobile, 16, 8, put_rim_ends)
        rim_c = rim_gain[:, rim_out]
        k0 = rim_ends[0] - rim_c * rim[it, 0, :, rim_out]
        k1 = rim_ends[1] - rim_c * rim[it, 1, :, rim_out]
        rim_corr0[...] = k0
        rim_items[it] = jnp.where(chip7, rim_ends[1], rim_c * k0 + k1)
        rim_got[it, chip] = rim_items[it]

        def rim_copy(it, n):
            q = far(*OFFSETS[n])
            return remote(rim_items.at[it], rim_got.at[it, chip], rim_send.at[it, n], rim_recv.at[it, n], (2 * q + core, sp))

        for n, offset in enumerate(OFFSETS):
            @pl.when((far(*offset) > chip) | chip7)
            def _():
                rim_copy(it, n).start()

        if it == 1:
            ends[1, other, :, part(56 * core, 8)] = rim_ends[other]
            out_e[:, part(120 * core, 8)] = rim_ends[core]
            cp_e = go(remote(ends.at[1, other], out_e.at[:, own_half], oute_send, oute_recv, partner))
        else:
            for ref in coefs:
                ref[1, :, kept_at] = ref[0, :, kept]
            drive[1, :, :, kept_at] = drive[0, :, :, kept]

        for cp in there:
            cp.wait_recv()
        c = carry_gain[it]
        c2 = c * c
        total = got[it, 7]
        sums[it, 0] = total
        for k in range(7):
            total = c2 * total + got[it, k]
            sums[it, k + 1] = total
        rows = pl.ds(0, HALF) if it == 0 else window
        their_rows = pl.ds(0, HALF) if it == 0 else their_window
        frame_rows = inner if it == 0 else part(MID + 8 * other, 56)
        land = part(PAD + 16 * other, HALF) if it == 0 else frame_rows
        their_land = part(PAD + 16 * core, HALF) if it == 0 else part(MID + 8 * core, 56)
        back = []
        for n, (dy, dx) in enumerate(OFFSETS):
            q = far(dy, dx)
            back.append(
                go(remote(sums.at[it, q, their_rows], starts.at[it + 1, 0, chip, their_land], back_send.at[it, n], back_recv.at[it, n], (2 * q + other, sp)))
            )
        back.append(go(remote(sums.at[it, chip, their_rows], starts.at[it + 1, 0, chip, their_land], back_send.at[it, 7], back_recv.at[it, 7], partner)))

        for n, (dy, dx) in enumerate(OFFSETS):
            @pl.when((source(dy, dx) < chip) | (source(dy, dx) == 7))
            def _():
                rim_copy(it, n).wait_recv()
        rim_c = rim_gain[:, rim_out]
        rim_c2 = rim_c * rim_c
        total = rim_got[it, 7]
        for k in range(7):
            total = jnp.where(k < chip, rim_c2 * total + rim_got[it, k], total)
        starts[it + 1, 0, :, rim_at] = total
        starts[it + 1, 1, :, rim_at] = rim_c * total + rim_corr0[...]
        if it == 0:
            outer_halo = go(
                remote(starts.at[1, :, :, rim_at], rim.at[1, :, :, part(8 + 16 * other, 8)], halo_send, halo_recv, (pair + other, outer))
            )
        else:
            outs = [
                go(remote(starts.at[2, other, :, rim_at], out_s.at[:, part(120 * core, 8)], outs_send.at[8], outs_recv.at[8], partner))
            ]
            out_s[:, part(120 * core, 8)] = starts[2, core, :, rim_at]

        def spread(t):
            starts[it + 1, 1, t, land] = gain[it, t, frame_rows] * starts[it + 1, 0, t, land] + corr0[it, t, rows]

        if it == 0:
            for n in reversed(range(8)):
                back[n].wait_recv()
                spread(source(*OFFSETS[n]) if n < 7 else chip)
        else:
            out_rows = part(HALF * core + 8 * other, 56)
            for n in reversed(range(8)):
                back[n].wait_recv()
                t = source(*OFFSETS[n]) if n < 7 else chip
                spread(t)
                outs.append(
                    go(remote(starts.at[2, other, t, land], out_s.at[t, out_rows], outs_send.at[n], outs_recv.at[n], partner))
                )
                out_s[t, out_rows] = starts[2, core, t, land]

    for edge in edges:
        right_edge(*edge).wait_send()
        left_edge(*edge).wait_send()
    region_edge().wait_send()
    cp_e.wait_recv()
    for cp in outs:
        cp.wait_recv()
    for cp in sends:
        cp.wait_send()
    for n, offset in enumerate(OFFSETS):
        @pl.when((far(*offset) > chip) | chip7)
        def _():
            for it in range(2):
                rim_copy(it, n).wait_send()


def hand_out(s_ref, e_ref, starts_hbm, ends_hbm, buf, sem):
    copies = []
    for n, (src, dst) in enumerate(((e_ref, ends_hbm), (s_ref, starts_hbm))):
        for t in range(8):
            buf[n, 0, pl.ds(t, 128, stride=8), :] = src[t].T
        cp = pltpu.make_async_copy(buf.at[n], dst, sem.at[n])
        cp.start()
        copies.append(cp)
    for cp in copies:
        cp.wait()


def local(initial_starts, source, region, base_reluctivity, saturation, mobility):
    held = jax.ShapeDtypeStruct((8, 128, 128), F32)
    block = jax.ShapeDtypeStruct((1, 1024, 128), F32)
    hbm = pl.BlockSpec(memory_space=pltpu.HBM)
    in_vmem = pl.BlockSpec(memory_space=pltpu.VMEM)
    vmem = lambda *shape: pltpu.VMEM(shape + (128,), F32)
    ints = lambda *shape: pltpu.VMEM(shape + (128,), jnp.int32)
    table = pltpu.SMEM((8,), F32)
    sem = lambda *shape: pltpu.SemaphoreType.DMA(shape)
    one = pltpu.SemaphoreType.DMA
    args = (base_reluctivity, saturation, mobility, initial_starts, source, region)
    kept = pl.pallas_call(
        kernel,
        out_shape=(held, held),
        in_specs=[hbm] * 6,
        out_specs=(in_vmem, in_vmem),
        scratch_shapes=[
            table, table, table,
            vmem(1, 1024), vmem(1, 1024), ints(1024), vmem(8, 128), vmem(8, 128), ints(8, 128),
            vmem(3, 2, 8, ROWS), vmem(2, 2, 8, ROWS),
            vmem(2, 8, ROWS), vmem(2, 8, ROWS), vmem(2, 8, ROWS), vmem(2, 8, ROWS), vmem(2, HALF), vmem(10, ROWS), vmem(8, ROWS), vmem(10, ROWS),
            ints(8, EDGE), vmem(2, 2, 8, EDGE), vmem(2, 8, EDGE), vmem(8, EDGE), vmem(8, EDGE), vmem(8, EDGE), vmem(8, EDGE),
            vmem(8, EDGE), vmem(8, EDGE), vmem(8, EDGE), vmem(2, 8, 8), vmem(8, 8), vmem(2, 8, 8), vmem(2, 8, 8, 8),
            vmem(2, 2, 8, HALF), vmem(2, 8, HALF), vmem(2, 8, HALF), vmem(2, 8, HALF), vmem(2, 8, HALF),
            pltpu.SemaphoreType.REGULAR, sem(4, 4), sem(2), sem(2), sem(2, 2), sem(2, 2), one, one,
            sem(2, 8), sem(2, 8), sem(2, 8), sem(2, 8), sem(2, 7), sem(2, 7), one, one,
            one, one, sem(9), sem(9),
        ],
        compiler_params=pltpu.CompilerParams(
            collective_id=0, has_side_effects=True, vmem_limit_bytes=40 * 2**20
        ),
        name="parareal",
    )(*[pltpu.with_memory_space_constraint(x, pltpu.HBM) for x in args])
    return pl.pallas_call(
        hand_out,
        out_shape=(block, block),
        in_specs=[in_vmem] * 2,
        out_specs=(hbm, hbm),
        scratch_shapes=[vmem(2, 1, 1024), sem(2)],
        compiler_params=pltpu.CompilerParams(vmem_limit_bytes=16 * 2**20),
        name="hand_out",
    )(*kept)


def solution(mesh):
    in_specs = (P("tm", None, "space"), P("tm", None, "space"), P(None, "space"), P(), P(), P())
    out_specs = (P("tm", None, "space"), P("tm", None, "space"))
    return jax.shard_map(local, mesh=mesh, in_specs=in_specs, out_specs=out_specs, check_vma=False)
```

```python
import jax
import jax.numpy as jnp
from jax import lax
from jax.experimental import pallas as pl
from jax.experimental.pallas import tpu as pltpu
from jax.sharding import PartitionSpec as P

MESH = pl.DeviceIdType.MESH
HALF = 64
OWN = 80
PAD = 8
MID = 16
ROWS = 96
EDGE = 40
F32 = jnp.float32
OFFSETS = ((1, 2), (1, 1), (0, 2), (1, 3), (0, 1), (1, 0), (0, 3))


def part(start, size):
    if not isinstance(start, int):
        start = pl.multiple_of(start, 8)
    return pl.ds(start, size)


def up(x, end):
    return jnp.where(lax.broadcasted_iota(jnp.int32, x.shape, 1) == 127, end, pltpu.roll(x, 127, 1))


def down(x, end):
    return jnp.where(lax.broadcasted_iota(jnp.int32, x.shape, 1) == 0, end, pltpu.roll(x, 1, 1))


def blocks(at, size):
    step = size // 2 if size >= 64 else size
    return [(at + k, step) for k in range(0, size, step)]


def reluctivity(a, coef_a, coef_b, nu, at, size):
    for start, step in blocks(at, size):
        rows = pl.ds(start, step)
        here = [x[rows] for x in a]
        for t in range(8):
            north = here[t + 1] if t < 7 else up(here[0], 0.0)
            south = here[t - 1] if t > 0 else down(here[7], 0.0)
            br = north - south
            bt = a[t][pl.ds(start + 1, step)] - a[t][pl.ds(start - 1, step)]
            nu[t][rows] = coef_a[t, rows] - coef_b[t, rows] / (4.0 + (br * br + bt * bt))


def turning(a, nu, here, mid, at, size):
    flux = (mid + nu[pl.ds(at + 1, size)]) * (a[pl.ds(at + 1, size)] - here)
    return flux + (mid + nu[pl.ds(at - 1, size)]) * (a[pl.ds(at - 1, size)] - here)


def update(a, nu, drive, mobile, at, size, put):
    for start, step in blocks(at, size):
        rows = pl.ds(start, step)
        mid, nu7, here, a7 = nu[0][rows], nu[7][rows], a[0][rows], a[7][rows]
        top = (nu7 + up(mid, nu7)) * (up(here, 0.0) - a7)
        below = down(top, 2.0 * mid * here)
        for t in range(8):
            if t < 7:
                following, next_nu = a[t + 1][rows], nu[t + 1][rows]
                above = (mid + next_nu) * (following - here)
            else:
                above = top
            total = turning(a[t], nu[t], here, mid, start, step) + (above - below) + drive[t, rows]
            put(t, pl.ds(start - at, step), here + mobile[t, rows] * total)
            below, here, mid = above, following, next_nu


def kernel(
    base_hbm, satur_hbm, mob_hbm, a_hbm, j_hbm, r_hbm, out_s, out_e,
    base_ref, satur_ref, mob_ref, in_a, in_j, in_r, ta, tj, tr, starts, drive,
    coef_a, coef_b, mobile, gain, carry_gain, reluct, work, later,
    rim_r, rim, rim_drive, rim_a, rim_b, rim_mobile, rim_gain, rim_reluct, rim_work, rim_later, rim_ends, rim_corr0, rim_items, rim_got,
    ends, corr0, items, got, sums,
    word, in_sem, pair_send, pair_recv, edge_send, edge_recv, reg_send, reg_recv,
    there_send, there_recv, back_send, back_recv, rim_send, rim_recv, halo_send, halo_recv,
    oute_send, oute_recv, outs_send, outs_recv,
):
    tm = lax.axis_index("tm")
    sp = lax.axis_index("space")
    core = lax.rem(tm, 2)
    other = 1 - core
    pair = tm - core
    chip = tm // 2
    right = lax.rem(sp + 1, 16)
    left = lax.rem(sp + 15, 16)
    outer = jnp.where(core == 0, left, right)
    partner = (pair + other, sp)

    def far(dy, dx):
        return 4 * lax.rem(chip // 4 + dy, 2) + lax.rem(lax.rem(chip, 4) + dx, 4)

    def source(dy, dx):
        return far(dy, (4 - dx) % 4)

    def remote(src, dst, send, recv, target):
        return pltpu.make_async_remote_copy(src, dst, send, recv, device_id=target, device_id_type=MESH)

    barrier = pltpu.get_barrier_semaphore()
    tellers = [(2 * far(1, 0) + core, sp), (2 * far(1, 0) + other, sp), partner]
    near = [(2 * far(0, dx) + core, sp) for dx in (1, 3, 2)] + tellers
    plane = lax.rem(sp, 8)
    is_first, is_last = plane == 0, plane == 7
    edge_sources = [(pair, outer), (pair + 1, outer)]

    def greet(devices):
        for device in devices:
            pl.semaphore_signal(barrier, inc=1, device_id=device, device_id_type=MESH)

    greet(near)
    later_greeting = (is_first & (core == 0)) | (is_last & (core == 1))

    @pl.when(jnp.logical_not(later_greeting))
    def _():
        greet(edge_sources)

    loads = []
    for n, (src, dst, pieces) in enumerate(((a_hbm.at[0], in_a.at[0], 4), (j_hbm.at[0], in_j.at[0], 4), (r_hbm, in_r, 4))):
        size = 1024 // pieces
        loads.append([])
        for k in range(pieces):
            cp = pltpu.make_async_copy(src.at[pl.ds(size * k, size)], dst.at[pl.ds(size * k, size)], in_sem.at[n, k])
            cp.start()
            loads[-1].append(cp)
    tables = []
    for n, (src, dst) in enumerate(((base_hbm, base_ref), (satur_hbm, satur_ref), (mob_hbm, mob_ref))):
        cp = pltpu.make_async_copy(src, dst, in_sem.at[3, n])
        cp.start()
        tables.append(cp)

    def arrived(copies):
        for cp in copies:
            cp.wait()

    def turn(src, dst):
        for t in range(8):
            dst[t] = src[pl.ds(t, 128, stride=8), :].T

    sends = []

    def go(cp):
        cp.start()
        sends.append(cp)
        return cp

    wide = pl.ds(PAD, OWN)
    inner = pl.ds(MID, HALF)
    mine = part((128 - OWN) * core, OWN)
    theirs = part((128 - OWN) * other, OWN)
    rim_halo = part(8 + 16 * core, 8)
    rim_own = part(8 + 8 * other, 16)
    rim_from = part(PAD + 64 * core, 16)
    rim_out = pl.ds(16, 8)
    kept, kept_at = part(PAD + 8 * core, 72), part(PAD + 8 * other, 72)
    window, their_window = part(8 * other, 56), part(8 * core, 56)
    rim_at = part(MID + 56 * core, 8)
    own_half = part(HALF * core, HALF)

    arrived(loads[0])
    turn(in_a.at[0], ta)

    arrived(loads[1])
    turn(in_j.at[0], tj)
    arrived(loads[2])
    turn(in_r, tr)
    arrived(tables)
    base = [base_ref[k] for k in range(8)]
    satur = [satur_ref[k] for k in range(8)]
    full = lambda x: jnp.full((8, 128), x, F32)
    tab_a = [full(0.5 * b * (1.0 + s)) for b, s in zip(base, satur)]
    tab_b = [full(2.0 * b * s) for b, s in zip(base, satur)]
    tab_m = [full(mob_ref[k]) for k in range(8)]
    tab_c = [1.0 / (1.0 + 12.0 * m * full(b)) for b, m in zip(base, tab_m)]

    def look_up(src, first, size, put):
        for t in range(8):
            for k in range(0, size, 8):
                r = src[t, part(first + k, 8)]
                bits = [(r & 1) != 0, (r & 2) != 0, (r & 4) != 0]
                for n, tab in enumerate((tab_a, tab_b, tab_m, tab_c)):
                    level = tab
                    for bit in bits:
                        level = [jnp.where(bit, hi, lo) for lo, hi in zip(level[::2], level[1::2])]
                    put(n, t, k, level[0])

    coefs = (coef_a, coef_b, mobile, gain)
    rim_coefs = (rim_a, rim_b, rim_mobile, rim_gain)

    def put_own(n, t, k, x):
        coefs[n][0, t, pl.ds(PAD + k, 8)] = x

    def put_rim(n, t, k, x):
        rim_coefs[n][t, rim_halo] = x

    look_up(tr, (128 - OWN) * core, OWN, put_own)
    for it, first in enumerate((8 + 48 * other, HALF * other)):
        for k in range(0, HALF, 8):
            r = tr[chip, part(first + k, 8)]
            level = tab_c
            for bit in ((r & 1) != 0, (r & 2) != 0, (r & 4) != 0):
                level = [jnp.where(bit, hi, lo) for lo, hi in zip(level[::2], level[1::2])]
            carry_gain[it, pl.ds(k, 8)] = level[0]
    starts[0, core, :, wide] = ta[:, mine]
    drive[0, core, :, wide] = tj[:, mine]

    @pl.when(is_first)
    def _():
        pl.semaphore_wait(barrier, len(near) + 1)
        greet([(pair + 1, left)])

        @pl.when(core == 0)
        def _():
            greet([(pair, left)])

    @pl.when(is_last & (core == 1))
    def _():
        pl.semaphore_wait(barrier, len(near) + 3)
        greet(edge_sources)

    @pl.when(jnp.logical_not(is_first | (is_last & (core == 1))))
    def _():
        pl.semaphore_wait(barrier, len(near) + 2)

    for device in tellers:
        pl.semaphore_signal(word, inc=1, device_id=device, device_id_type=MESH)

    def right_edge(n, src, dst):
        return remote(src.at[:, pl.ds(120, 8)], dst.at[core, :, pl.ds(8, 8)], edge_send.at[n, 0], edge_recv.at[n, core], (pair, right))

    def left_edge(n, src, dst):
        return remote(src.at[:, pl.ds(0, 8)], dst.at[core, :, pl.ds(24, 8)], edge_send.at[n, 1], edge_recv.at[n, core], (pair + 1, left))

    def region_edge():
        ahead = (tm, jnp.where(core == 0, right, left))
        return remote(tr.at[:, part(120 * other, 8)], rim_r.at[:, rim_halo], reg_send, reg_recv, ahead)

    edges = ((0, ta, rim.at[0]), (1, tj, rim_drive))

    def send_pair(n, src, dst):
        return go(remote(src.at[:, theirs], dst.at[core, :, wide], pair_send.at[n], pair_recv.at[n], partner))

    for edge in edges:
        right_edge(*edge).start()

        @pl.when(jnp.logical_not(is_first))
        def _():
            left_edge(*edge).start()

    @pl.when(jnp.logical_not(is_first & (core == 1)))
    def _():
        region_edge().start()

    pairs = [send_pair(0, ta, starts.at[0]), send_pair(1, tj, drive.at[0])]

    chip7 = chip == 7

    def phases(ref):
        return [ref.at[t] for t in range(8)]

    nus = [reluct.at[t + 1] for t in range(8)]
    lates = [later.at[t + 1] for t in range(8)]

    def put_work(t, rows, x):
        work[t, pl.ds(PAD + rows.start, rows.size)] = x

    def put_later(t, rows, x):
        later[t + 1, pl.ds(PAD + rows.start, rows.size)] = x

    def two_steps(it, p):
        ca, cb, cm, force = coef_a.at[it], coef_b.at[it], mobile.at[it], drive.at[it, p]
        a = phases(starts.at[it, p])
        reluctivity(a, ca, cb, nus, PAD, OWN)
        update(a, nus, force, cm, PAD, OWN, put_work)
        a = phases(work)
        reluctivity(a, ca, cb, nus, PAD, OWN)
        update(a, nus, force, cm, PAD, OWN, put_later)
        reluctivity(lates, ca, cb, nus, PAD, OWN)

    def last_step(it, p, t):
        here, mid = later[t + 1, inner], reluct[t + 1, inner]
        total = turning(later.at[t + 1], reluct.at[t + 1], here, mid, MID, HALF) + drive[it, p, t, inner]
        total += (mid + reluct[t + 2, inner]) * (later[t + 2, inner] - here)
        total += (mid + reluct[t, inner]) * (later[t, inner] - here)
        return here + mobile[it, t, inner] * total

    for it in range(2):
        def put_ends(t, rows, x):
            ends[it, core, t, rows] = x
            if it == 1:
                out_e[t, part(HALF * core + rows.start, rows.size)] = x

        two_steps(it, core)
        update(lates, nus, drive.at[it, core], mobile.at[it], MID, HALF, put_ends)
        if it == 0:
            for cp in pairs:
                cp.wait_recv()
        two_steps(it, other)
        later[0, wide] = down(later[8, wide], 0.0)
        later[9, wide] = up(later[1, wide], 0.0)
        reluct[0, wide] = down(reluct[8, wide], reluct[1, wide])
        reluct[9, wide] = up(reluct[1, wide], reluct[8, wide])

        def finish(t):
            theirs_end = last_step(it, other, t)
            ends[it, other, t] = theirs_end
            own_end = ends[it, core, t]
            c = gain[it, t, inner]
            own_corr = own_end - c * starts[it, core, t, inner]
            theirs_corr = theirs_end - c * starts[it, other, t, inner]
            first = jnp.where(core == 0, own_corr, theirs_corr)
            second = jnp.where(core == 0, theirs_corr, own_corr)
            corr0[it, t] = first
            items[it, t] = jnp.where(chip7, jnp.where(core == 0, theirs_end, own_end), c * first + second)

        if it == 0:
            pl.semaphore_wait(word, len(tellers))
        there = []
        for n, (dy, dx) in enumerate(OFFSETS):
            q = far(dy, dx)
            finish(q)
            mine_out = items.at[it, q] if it == 0 else items.at[it, q, window]
            there.append(
                go(remote(mine_out, got.at[it, chip] if it == 0 else got.at[it, chip, window], there_send.at[it, n], there_recv.at[it, n], (2 * q + other, sp)))
            )
        finish(chip)
        mine_out = items.at[it, chip] if it == 0 else items.at[it, chip, window]
        land = got.at[it, chip] if it == 0 else got.at[it, chip, window]
        there.append(go(remote(mine_out, land, there_send.at[it, 7], there_recv.at[it, 7], partner)))

        if it == 0:
            @pl.when(is_first)
            def _():
                pl.semaphore_wait(barrier, 1)
                for edge in edges:
                    left_edge(*edge).start()

                @pl.when(core == 1)
                def _():
                    region_edge().start()

            region_edge().wait_recv()
            look_up(rim_r, 8 + 16 * core, 8, put_rim)
            for ref, into in zip(coefs, rim_coefs):
                into[:, rim_own] = ref[0, :, rim_from]
            for n in range(2):
                for p in range(2):
                    remote(
                        ta.at[:, pl.ds(0, 8)], rim.at[0, 0, :, pl.ds(8, 8)], edge_send.at[n, 0], edge_recv.at[n, p], partner
                    ).wait_recv()
            rim_drive[:, :, rim_own] = drive[0, :, :, rim_from]
            rim[0, :, :, rim_own] = starts[0, :, :, rim_from]
        else:
            outer_halo.wait_recv()
            rim[1, :, :, rim_own] = starts[1, :, :, part(MID + 48 * core, 16)]
        rim_nus = phases(rim_reluct)
        for p in range(2):
            def put_rim_work(t, rows, x):
                rim_work[t, pl.ds(8, 24)] = x

            def put_rim_later(t, rows, x):
                rim_later[t, pl.ds(8, 24)] = x

            def put_rim_ends(t, rows, x):
                rim_ends[p, t] = x

            for a, put in ((rim.at[it, p], put_rim_work), (rim_work, put_rim_later)):
                reluctivity(phases(a), rim_a, rim_b, rim_nus, 8, 24)
                update(phases(a), rim_nus, rim_drive.at[p], rim_mobile, 8, 24, put)
            reluctivity(phases(rim_later), rim_a, rim_b, rim_nus, 8, 24)
            update(phases(rim_later), rim_nus, rim_drive.at[p], rim_mobile, 16, 8, put_rim_ends)
        rim_c = rim_gain[:, rim_out]
        k0 = rim_ends[0] - rim_c * rim[it, 0, :, rim_out]
        k1 = rim_ends[1] - rim_c * rim[it, 1, :, rim_out]
        rim_corr0[...] = k0
        rim_items[it] = jnp.where(chip7, rim_ends[1], rim_c * k0 + k1)
        rim_got[it, chip] = rim_items[it]

        def rim_copy(it, n):
            q = far(*OFFSETS[n])
            return remote(rim_items.at[it], rim_got.at[it, chip], rim_send.at[it, n], rim_recv.at[it, n], (2 * q + core, sp))

        for n, offset in enumerate(OFFSETS):
            @pl.when((far(*offset) > chip) | chip7)
            def _():
                rim_copy(it, n).start()

        if it == 1:
            ends[1, other, :, part(56 * core, 8)] = rim_ends[other]
            out_e[:, part(120 * core, 8)] = rim_ends[core]
            cp_e = go(remote(ends.at[1, other], out_e.at[:, own_half], oute_send, oute_recv, partner))
        else:
            for ref in coefs:
                ref[1, :, kept_at] = ref[0, :, kept]
            drive[1, :, :, kept_at] = drive[0, :, :, kept]

        for cp in there:
            cp.wait_recv()
        c = carry_gain[it]
        c2 = c * c
        total = got[it, 7]
        sums[it, 0] = total
        for k in range(7):
            total = c2 * total + got[it, k]
            sums[it, k + 1] = total
        rows = pl.ds(0, HALF) if it == 0 else window
        their_rows = pl.ds(0, HALF) if it == 0 else their_window
        frame_rows = inner if it == 0 else part(MID + 8 * other, 56)
        land = part(PAD + 16 * other, HALF) if it == 0 else frame_rows
        their_land = part(PAD + 16 * core, HALF) if it == 0 else part(MID + 8 * core, 56)
        back = []
        for n, (dy, dx) in enumerate(OFFSETS):
            q = far(dy, dx)
            back.append(
                go(remote(sums.at[it, q, their_rows], starts.at[it + 1, 0, chip, their_land], back_send.at[it, n], back_recv.at[it, n], (2 * q + other, sp)))
            )
        back.append(go(remote(sums.at[it, chip, their_rows], starts.at[it + 1, 0, chip, their_land], back_send.at[it, 7], back_recv.at[it, 7], partner)))

        for n, (dy, dx) in enumerate(OFFSETS):
            @pl.when((source(dy, dx) < chip) | (source(dy, dx) == 7))
            def _():
                rim_copy(it, n).wait_recv()
        rim_c = rim_gain[:, rim_out]
        rim_c2 = rim_c * rim_c
        total = rim_got[it, 7]
        for k in range(7):
            total = jnp.where(k < chip, rim_c2 * total + rim_got[it, k], total)
        starts[it + 1, 0, :, rim_at] = total
        starts[it + 1, 1, :, rim_at] = rim_c * total + rim_corr0[...]
        if it == 0:
            outer_halo = go(
                remote(starts.at[1, :, :, rim_at], rim.at[1, :, :, part(8 + 16 * other, 8)], halo_send, halo_recv, (pair + other, outer))
            )
        else:
            outs = [
                go(remote(starts.at[2, other, :, rim_at], out_s.at[:, part(120 * core, 8)], outs_send.at[8], outs_recv.at[8], partner))
            ]
            out_s[:, part(120 * core, 8)] = starts[2, core, :, rim_at]

        def spread(t):
            starts[it + 1, 1, t, land] = gain[it, t, frame_rows] * starts[it + 1, 0, t, land] + corr0[it, t, rows]

        if it == 0:
            for n in reversed(range(8)):
                back[n].wait_recv()
                spread(source(*OFFSETS[n]) if n < 7 else chip)
        else:
            out_rows = part(HALF * core + 8 * other, 56)
            for n in reversed(range(8)):
                back[n].wait_recv()
                t = source(*OFFSETS[n]) if n < 7 else chip
                spread(t)
                outs.append(
                    go(remote(starts.at[2, other, t, land], out_s.at[t, out_rows], outs_send.at[n], outs_recv.at[n], partner))
                )
                out_s[t, out_rows] = starts[2, core, t, land]

    for edge in edges:
        right_edge(*edge).wait_send()
        left_edge(*edge).wait_send()
    region_edge().wait_send()
    cp_e.wait_recv()
    for cp in outs:
        cp.wait_recv()
    for cp in sends:
        cp.wait_send()
    for n, offset in enumerate(OFFSETS):
        @pl.when((far(*offset) > chip) | chip7)
        def _():
            for it in range(2):
                rim_copy(it, n).wait_send()


def hand_out(s_ref, e_ref, starts_hbm, ends_hbm, buf, sem):
    copies = []
    for n, (src, dst) in enumerate(((e_ref, ends_hbm), (s_ref, starts_hbm))):
        for t in range(8):
            buf[n, 0, pl.ds(t, 128, stride=8), :] = src[t].T
        cp = pltpu.make_async_copy(buf.at[n], dst, sem.at[n])
        cp.start()
        copies.append(cp)
    for cp in copies:
        cp.wait()


def local(initial_starts, source, region, base_reluctivity, saturation, mobility):
    held = jax.ShapeDtypeStruct((8, 128, 128), F32)
    block = jax.ShapeDtypeStruct((1, 1024, 128), F32)
    hbm = pl.BlockSpec(memory_space=pltpu.HBM)
    in_vmem = pl.BlockSpec(memory_space=pltpu.VMEM)
    vmem = lambda *shape: pltpu.VMEM(shape + (128,), F32)
    ints = lambda *shape: pltpu.VMEM(shape + (128,), jnp.int32)
    table = pltpu.SMEM((8,), F32)
    sem = lambda *shape: pltpu.SemaphoreType.DMA(shape)
    one = pltpu.SemaphoreType.DMA
    args = (base_reluctivity, saturation, mobility, initial_starts, source, region)
    kept = pl.pallas_call(
        kernel,
        out_shape=(held, held),
        in_specs=[hbm] * 6,
        out_specs=(in_vmem, in_vmem),
        scratch_shapes=[
            table, table, table,
            vmem(1, 1024), vmem(1, 1024), ints(1024), vmem(8, 128), vmem(8, 128), ints(8, 128),
            vmem(3, 2, 8, ROWS), vmem(2, 2, 8, ROWS),
            vmem(2, 8, ROWS), vmem(2, 8, ROWS), vmem(2, 8, ROWS), vmem(2, 8, ROWS), vmem(2, HALF), vmem(10, ROWS), vmem(8, ROWS), vmem(10, ROWS),
            ints(8, EDGE), vmem(2, 2, 8, EDGE), vmem(2, 8, EDGE), vmem(8, EDGE), vmem(8, EDGE), vmem(8, EDGE), vmem(8, EDGE),
            vmem(8, EDGE), vmem(8, EDGE), vmem(8, EDGE), vmem(2, 8, 8), vmem(8, 8), vmem(2, 8, 8), vmem(2, 8, 8, 8),
            vmem(2, 2, 8, HALF), vmem(2, 8, HALF), vmem(2, 8, HALF), vmem(2, 8, HALF), vmem(2, 8, HALF),
            pltpu.SemaphoreType.REGULAR, sem(4, 4), sem(2), sem(2), sem(2, 2), sem(2, 2), one, one,
            sem(2, 8), sem(2, 8), sem(2, 8), sem(2, 8), sem(2, 7), sem(2, 7), one, one,
            one, one, sem(9), sem(9),
        ],
        compiler_params=pltpu.CompilerParams(
            collective_id=0, has_side_effects=True, vmem_limit_bytes=40 * 2**20
        ),
        name="parareal",
    )(*[pltpu.with_memory_space_constraint(x, pltpu.HBM) for x in args])
    return pl.pallas_call(
        hand_out,
        out_shape=(block, block),
        in_specs=[in_vmem] * 2,
        out_specs=(hbm, hbm),
        scratch_shapes=[vmem(2, 1, 1024), sem(2)],
        compiler_params=pltpu.CompilerParams(vmem_limit_bytes=16 * 2**20),
        name="hand_out",
    )(*kept)


def solution(mesh):
    in_specs = (P("tm", None, "space"), P("tm", None, "space"), P(None, "space"), P(), P(), P())
    out_specs = (P("tm", None, "space"), P("tm", None, "space"))
    return jax.shard_map(local, mesh=mesh, in_specs=in_specs, out_specs=out_specs, check_vma=False)
```

```python
import jax
import jax.numpy as jnp
from jax import lax
from jax.experimental import pallas as pl
from jax.experimental.pallas import tpu as pltpu
from jax.sharding import PartitionSpec as P

MESH = pl.DeviceIdType.MESH
HALF = 64
OWN = 80
PAD = 8
MID = 16
ROWS = 96
EDGE = 40
F32 = jnp.float32
OFFSETS = ((1, 2), (1, 1), (0, 2), (1, 3), (0, 1), (1, 0), (0, 3))


def part(start, size):
    if not isinstance(start, int):
        start = pl.multiple_of(start, 8)
    return pl.ds(start, size)


def up(x, end):
    return jnp.where(lax.broadcasted_iota(jnp.int32, x.shape, 1) == 127, end, pltpu.roll(x, 127, 1))


def down(x, end):
    return jnp.where(lax.broadcasted_iota(jnp.int32, x.shape, 1) == 0, end, pltpu.roll(x, 1, 1))


def blocks(at, size):
    step = size // 2 if size >= 64 else size
    return [(at + k, step) for k in range(0, size, step)]


def reluctivity(a, coef_a, coef_b, nu, at, size):
    for start, step in blocks(at, size):
        rows = pl.ds(start, step)
        here = [x[rows] for x in a]
        for t in range(8):
            north = here[t + 1] if t < 7 else up(here[0], 0.0)
            south = here[t - 1] if t > 0 else down(here[7], 0.0)
            br = north - south
            bt = a[t][pl.ds(start + 1, step)] - a[t][pl.ds(start - 1, step)]
            nu[t][rows] = coef_a[t, rows] - coef_b[t, rows] / (4.0 + (br * br + bt * bt))


def turning(a, nu, here, mid, at, size):
    flux = (mid + nu[pl.ds(at + 1, size)]) * (a[pl.ds(at + 1, size)] - here)
    return flux + (mid + nu[pl.ds(at - 1, size)]) * (a[pl.ds(at - 1, size)] - here)


def update(a, nu, drive, mobile, at, size, put):
    for start, step in blocks(at, size):
        rows = pl.ds(start, step)
        mid, nu7, here, a7 = nu[0][rows], nu[7][rows], a[0][rows], a[7][rows]
        top = (nu7 + up(mid, nu7)) * (up(here, 0.0) - a7)
        below = down(top, 2.0 * mid * here)
        for t in range(8):
            if t < 7:
                following, next_nu = a[t + 1][rows], nu[t + 1][rows]
                above = (mid + next_nu) * (following - here)
            else:
                above = top
            total = turning(a[t], nu[t], here, mid, start, step) + (above - below) + drive[t, rows]
            put(t, pl.ds(start - at, step), here + mobile[t, rows] * total)
            below, here, mid = above, following, next_nu


def kernel(
    base_hbm, satur_hbm, mob_hbm, a_hbm, j_hbm, r_hbm, out_s, out_e,
    base_ref, satur_ref, mob_ref, in_a, in_j, in_r, ta, tj, tr, starts, drive,
    coef_a, coef_b, mobile, gain, carry_gain, reluct, work, later,
    rim_r, rim, rim_drive, rim_a, rim_b, rim_mobile, rim_gain, rim_reluct, rim_work, rim_later, rim_ends, rim_corr0, rim_items, rim_got,
    ends, corr0, items, got, sums,
    word, in_sem, pair_send, pair_recv, edge_send, edge_recv, reg_send, reg_recv,
    there_send, there_recv, back_send, back_recv, rim_send, rim_recv, halo_send, halo_recv,
    oute_send, oute_recv, outs_send, outs_recv,
):
    tm = lax.axis_index("tm")
    sp = lax.axis_index("space")
    core = lax.rem(tm, 2)
    other = 1 - core
    pair = tm - core
    chip = tm // 2
    right = lax.rem(sp + 1, 16)
    left = lax.rem(sp + 15, 16)
    outer = jnp.where(core == 0, left, right)
    partner = (pair + other, sp)

    def far(dy, dx):
        return 4 * lax.rem(chip // 4 + dy, 2) + lax.rem(lax.rem(chip, 4) + dx, 4)

    def source(dy, dx):
        return far(dy, (4 - dx) % 4)

    def remote(src, dst, send, recv, target):
        return pltpu.make_async_remote_copy(src, dst, send, recv, device_id=target, device_id_type=MESH)

    barrier = pltpu.get_barrier_semaphore()
    tellers = [(2 * far(1, 0) + core, sp), (2 * far(1, 0) + other, sp), partner]
    near = [(2 * far(0, dx) + core, sp) for dx in (1, 3, 2)] + tellers
    plane = lax.rem(sp, 8)
    is_first, is_last = plane == 0, plane == 7
    edge_sources = [(pair, outer), (pair + 1, outer)]

    def greet(devices):
        for device in devices:
            pl.semaphore_signal(barrier, inc=1, device_id=device, device_id_type=MESH)

    greet(near)
    later_greeting = (is_first & (core == 0)) | (is_last & (core == 1))

    @pl.when(jnp.logical_not(later_greeting))
    def _():
        greet(edge_sources)

    loads = []
    for n, (src, dst, pieces) in enumerate(((a_hbm.at[0], in_a.at[0], 2), (j_hbm.at[0], in_j.at[0], 1), (r_hbm, in_r, 1))):
        size = 1024 // pieces
        loads.append([])
        for k in range(pieces):
            cp = pltpu.make_async_copy(src.at[pl.ds(size * k, size)], dst.at[pl.ds(size * k, size)], in_sem.at[n, k])
            cp.start()
            loads[-1].append(cp)
    tables = []
    for n, (src, dst) in enumerate(((base_hbm, base_ref), (satur_hbm, satur_ref), (mob_hbm, mob_ref))):
        cp = pltpu.make_async_copy(src, dst, in_sem.at[3, n])
        cp.start()
        tables.append(cp)

    def arrived(copies):
        for cp in copies:
            cp.wait()

    def turn(src, dst):
        for t in range(8):
            dst[t] = src[pl.ds(t, 128, stride=8), :].T

    sends = []

    def go(cp):
        cp.start()
        sends.append(cp)
        return cp

    wide = pl.ds(PAD, OWN)
    inner = pl.ds(MID, HALF)
    mine = part((128 - OWN) * core, OWN)
    theirs = part((128 - OWN) * other, OWN)
    rim_halo = part(8 + 16 * core, 8)
    rim_own = part(8 + 8 * other, 16)
    rim_from = part(PAD + 64 * core, 16)
    rim_out = pl.ds(16, 8)
    kept, kept_at = part(PAD + 8 * core, 72), part(PAD + 8 * other, 72)
    window, their_window = part(8 * other, 56), part(8 * core, 56)
    rim_at = part(MID + 56 * core, 8)
    own_half = part(HALF * core, HALF)

    arrived(loads[0])
    turn(in_a.at[0], ta)

    arrived(loads[1])
    turn(in_j.at[0], tj)
    arrived(loads[2])
    turn(in_r, tr)
    arrived(tables)
    base = [base_ref[k] for k in range(8)]
    satur = [satur_ref[k] for k in range(8)]
    full = lambda x: jnp.full((8, 128), x, F32)
    tab_a = [full(0.5 * b * (1.0 + s)) for b, s in zip(base, satur)]
    tab_b = [full(2.0 * b * s) for b, s in zip(base, satur)]
    tab_m = [full(mob_ref[k]) for k in range(8)]
    tab_c = [1.0 / (1.0 + 12.0 * m * full(b)) for b, m in zip(base, tab_m)]

    def look_up(src, first, size, put):
        for t in range(8):
            for k in range(0, size, 8):
                r = src[t, part(first + k, 8)]
                bits = [(r & 1) != 0, (r & 2) != 0, (r & 4) != 0]
                for n, tab in enumerate((tab_a, tab_b, tab_m, tab_c)):
                    level = tab
                    for bit in bits:
                        level = [jnp.where(bit, hi, lo) for lo, hi in zip(level[::2], level[1::2])]
                    put(n, t, k, level[0])

    coefs = (coef_a, coef_b, mobile, gain)
    rim_coefs = (rim_a, rim_b, rim_mobile, rim_gain)

    def put_own(n, t, k, x):
        coefs[n][0, t, pl.ds(PAD + k, 8)] = x

    def put_rim(n, t, k, x):
        rim_coefs[n][t, rim_halo] = x

    look_up(tr, (128 - OWN) * core, OWN, put_own)
    for it, first in enumerate((8 + 48 * other, HALF * other)):
        for k in range(0, HALF, 8):
            r = tr[chip, part(first + k, 8)]
            level = tab_c
            for bit in ((r & 1) != 0, (r & 2) != 0, (r & 4) != 0):
                level = [jnp.where(bit, hi, lo) for lo, hi in zip(level[::2], level[1::2])]
            carry_gain[it, pl.ds(k, 8)] = level[0]
    starts[0, core, :, wide] = ta[:, mine]
    drive[0, core, :, wide] = tj[:, mine]

    @pl.when(is_first)
    def _():
        pl.semaphore_wait(barrier, len(near) + 1)
        greet([(pair + 1, left)])

        @pl.when(core == 0)
        def _():
            greet([(pair, left)])

    @pl.when(is_last & (core == 1))
    def _():
        pl.semaphore_wait(barrier, len(near) + 3)
        greet(edge_sources)

    @pl.when(jnp.logical_not(is_first | (is_last & (core == 1))))
    def _():
        pl.semaphore_wait(barrier, len(near) + 2)

    for device in tellers:
        pl.semaphore_signal(word, inc=1, device_id=device, device_id_type=MESH)

    def right_edge(n, src, dst):
        return remote(src.at[:, pl.ds(120, 8)], dst.at[core, :, pl.ds(8, 8)], edge_send.at[n, 0], edge_recv.at[n, core], (pair, right))

    def left_edge(n, src, dst):
        return remote(src.at[:, pl.ds(0, 8)], dst.at[core, :, pl.ds(24, 8)], edge_send.at[n, 1], edge_recv.at[n, core], (pair + 1, left))

    def region_edge():
        ahead = (tm, jnp.where(core == 0, right, left))
        return remote(tr.at[:, part(120 * other, 8)], rim_r.at[:, rim_halo], reg_send, reg_recv, ahead)

    edges = ((0, ta, rim.at[0]), (1, tj, rim_drive))

    def send_pair(n, src, dst):
        return go(remote(src.at[:, theirs], dst.at[core, :, wide], pair_send.at[n], pair_recv.at[n], partner))

    pairs = [send_pair(0, ta, starts.at[0]), send_pair(1, tj, drive.at[0])]

    for edge in edges:
        right_edge(*edge).start()

        @pl.when(jnp.logical_not(is_first))
        def _():
            left_edge(*edge).start()

    @pl.when(jnp.logical_not(is_first & (core == 1)))
    def _():
        region_edge().start()

    chip7 = chip == 7

    def phases(ref):
        return [ref.at[t] for t in range(8)]

    nus = [reluct.at[t + 1] for t in range(8)]
    lates = [later.at[t + 1] for t in range(8)]

    def put_work(t, rows, x):
        work[t, pl.ds(PAD + rows.start, rows.size)] = x

    def put_later(t, rows, x):
        later[t + 1, pl.ds(PAD + rows.start, rows.size)] = x

    def two_steps(it, p):
        ca, cb, cm, force = coef_a.at[it], coef_b.at[it], mobile.at[it], drive.at[it, p]
        a = phases(starts.at[it, p])
        reluctivity(a, ca, cb, nus, PAD, OWN)
        update(a, nus, force, cm, PAD, OWN, put_work)
        a = phases(work)
        reluctivity(a, ca, cb, nus, PAD, OWN)
        update(a, nus, force, cm, PAD, OWN, put_later)
        reluctivity(lates, ca, cb, nus, PAD, OWN)

    def last_step(it, p, t):
        here, mid = later[t + 1, inner], reluct[t + 1, inner]
        total = turning(later.at[t + 1], reluct.at[t + 1], here, mid, MID, HALF) + drive[it, p, t, inner]
        total += (mid + reluct[t + 2, inner]) * (later[t + 2, inner] - here)
        total += (mid + reluct[t, inner]) * (later[t, inner] - here)
        return here + mobile[it, t, inner] * total

    for it in range(2):
        def put_ends(t, rows, x):
            ends[it, core, t, rows] = x
            if it == 1:
                out_e[t, part(HALF * core + rows.start, rows.size)] = x

        two_steps(it, core)
        update(lates, nus, drive.at[it, core], mobile.at[it], MID, HALF, put_ends)
        if it == 0:
            for cp in pairs:
                cp.wait_recv()
        two_steps(it, other)
        later[0, wide] = down(later[8, wide], 0.0)
        later[9, wide] = up(later[1, wide], 0.0)
        reluct[0, wide] = down(reluct[8, wide], reluct[1, wide])
        reluct[9, wide] = up(reluct[1, wide], reluct[8, wide])

        def finish(t):
            theirs_end = last_step(it, other, t)
            ends[it, other, t] = theirs_end
            own_end = ends[it, core, t]
            c = gain[it, t, inner]
            own_corr = own_end - c * starts[it, core, t, inner]
            theirs_corr = theirs_end - c * starts[it, other, t, inner]
            first = jnp.where(core == 0, own_corr, theirs_corr)
            second = jnp.where(core == 0, theirs_corr, own_corr)
            corr0[it, t] = first
            items[it, t] = jnp.where(chip7, jnp.where(core == 0, theirs_end, own_end), c * first + second)

        if it == 0:
            pl.semaphore_wait(word, len(tellers))
        there = []
        for n, (dy, dx) in enumerate(OFFSETS):
            q = far(dy, dx)
            finish(q)
            mine_out = items.at[it, q] if it == 0 else items.at[it, q, window]
            there.append(
                go(remote(mine_out, got.at[it, chip] if it == 0 else got.at[it, chip, window], there_send.at[it, n], there_recv.at[it, n], (2 * q + other, sp)))
            )
        finish(chip)
        mine_out = items.at[it, chip] if it == 0 else items.at[it, chip, window]
        land = got.at[it, chip] if it == 0 else got.at[it, chip, window]
        there.append(go(remote(mine_out, land, there_send.at[it, 7], there_recv.at[it, 7], partner)))

        if it == 0:
            @pl.when(is_first)
            def _():
                pl.semaphore_wait(barrier, 1)
                for edge in edges:
                    left_edge(*edge).start()

                @pl.when(core == 1)
                def _():
                    region_edge().start()

            region_edge().wait_recv()
            look_up(rim_r, 8 + 16 * core, 8, put_rim)
            for ref, into in zip(coefs, rim_coefs):
                into[:, rim_own] = ref[0, :, rim_from]
            for n in range(2):
                for p in range(2):
                    remote(
                        ta.at[:, pl.ds(0, 8)], rim.at[0, 0, :, pl.ds(8, 8)], edge_send.at[n, 0], edge_recv.at[n, p], partner
                    ).wait_recv()
            rim_drive[:, :, rim_own] = drive[0, :, :, rim_from]
            rim[0, :, :, rim_own] = starts[0, :, :, rim_from]
        else:
            outer_halo.wait_recv()
            rim[1, :, :, rim_own] = starts[1, :, :, part(MID + 48 * core, 16)]
        rim_nus = phases(rim_reluct)
        for p in range(2):
            def put_rim_work(t, rows, x):
                rim_work[t, pl.ds(8, 24)] = x

            def put_rim_later(t, rows, x):
                rim_later[t, pl.ds(8, 24)] = x

            def put_rim_ends(t, rows, x):
                rim_ends[p, t] = x

            for a, put in ((rim.at[it, p], put_rim_work), (rim_work, put_rim_later)):
                reluctivity(phases(a), rim_a, rim_b, rim_nus, 8, 24)
                update(phases(a), rim_nus, rim_drive.at[p], rim_mobile, 8, 24, put)
            reluctivity(phases(rim_later), rim_a, rim_b, rim_nus, 8, 24)
            update(phases(rim_later), rim_nus, rim_drive.at[p], rim_mobile, 16, 8, put_rim_ends)
        rim_c = rim_gain[:, rim_out]
        k0 = rim_ends[0] - rim_c * rim[it, 0, :, rim_out]
        k1 = rim_ends[1] - rim_c * rim[it, 1, :, rim_out]
        rim_corr0[...] = k0
        rim_items[it] = jnp.where(chip7, rim_ends[1], rim_c * k0 + k1)
        rim_got[it, chip] = rim_items[it]

        def rim_copy(it, n):
            q = far(*OFFSETS[n])
            return remote(rim_items.at[it], rim_got.at[it, chip], rim_send.at[it, n], rim_recv.at[it, n], (2 * q + core, sp))

        for n, offset in enumerate(OFFSETS):
            @pl.when((far(*offset) > chip) | chip7)
            def _():
                rim_copy(it, n).start()

        if it == 1:
            ends[1, other, :, part(56 * core, 8)] = rim_ends[other]
            out_e[:, part(120 * core, 8)] = rim_ends[core]
            cp_e = go(remote(ends.at[1, other], out_e.at[:, own_half], oute_send, oute_recv, partner))
        else:
            for ref in coefs:
                ref[1, :, kept_at] = ref[0, :, kept]
            drive[1, :, :, kept_at] = drive[0, :, :, kept]

        for cp in there:
            cp.wait_recv()
        c = carry_gain[it]
        c2 = c * c
        total = got[it, 7]
        sums[it, 0] = total
        for k in range(7):
            total = c2 * total + got[it, k]
            sums[it, k + 1] = total
        rows = pl.ds(0, HALF) if it == 0 else window
        their_rows = pl.ds(0, HALF) if it == 0 else their_window
        frame_rows = inner if it == 0 else part(MID + 8 * other, 56)
        land = part(PAD + 16 * other, HALF) if it == 0 else frame_rows
        their_land = part(PAD + 16 * core, HALF) if it == 0 else part(MID + 8 * core, 56)
        back = []
        for n, (dy, dx) in enumerate(OFFSETS):
            q = far(dy, dx)
            back.append(
                go(remote(sums.at[it, q, their_rows], starts.at[it + 1, 0, chip, their_land], back_send.at[it, n], back_recv.at[it, n], (2 * q + other, sp)))
            )
        back.append(go(remote(sums.at[it, chip, their_rows], starts.at[it + 1, 0, chip, their_land], back_send.at[it, 7], back_recv.at[it, 7], partner)))

        for n, (dy, dx) in enumerate(OFFSETS):
            @pl.when((source(dy, dx) < chip) | (source(dy, dx) == 7))
            def _():
                rim_copy(it, n).wait_recv()
        rim_c = rim_gain[:, rim_out]
        rim_c2 = rim_c * rim_c
        total = rim_got[it, 7]
        for k in range(7):
            total = jnp.where(k < chip, rim_c2 * total + rim_got[it, k], total)
        starts[it + 1, 0, :, rim_at] = total
        starts[it + 1, 1, :, rim_at] = rim_c * total + rim_corr0[...]
        if it == 0:
            outer_halo = go(
                remote(starts.at[1, :, :, rim_at], rim.at[1, :, :, part(8 + 16 * other, 8)], halo_send, halo_recv, (pair + other, outer))
            )
        else:
            outs = [
                go(remote(starts.at[2, other, :, rim_at], out_s.at[:, part(120 * core, 8)], outs_send.at[8], outs_recv.at[8], partner))
            ]
            out_s[:, part(120 * core, 8)] = starts[2, core, :, rim_at]

        def spread(t):
            starts[it + 1, 1, t, land] = gain[it, t, frame_rows] * starts[it + 1, 0, t, land] + corr0[it, t, rows]

        if it == 0:
            for n in reversed(range(8)):
                back[n].wait_recv()
                spread(source(*OFFSETS[n]) if n < 7 else chip)
        else:
            out_rows = part(HALF * core + 8 * other, 56)
            for n in reversed(range(8)):
                back[n].wait_recv()
                t = source(*OFFSETS[n]) if n < 7 else chip
                spread(t)
                outs.append(
                    go(remote(starts.at[2, other, t, land], out_s.at[t, out_rows], outs_send.at[n], outs_recv.at[n], partner))
                )
                out_s[t, out_rows] = starts[2, core, t, land]

    for edge in edges:
        right_edge(*edge).wait_send()
        left_edge(*edge).wait_send()
    region_edge().wait_send()
    cp_e.wait_recv()
    for cp in outs:
        cp.wait_recv()
    for cp in sends:
        cp.wait_send()
    for n, offset in enumerate(OFFSETS):
        @pl.when((far(*offset) > chip) | chip7)
        def _():
            for it in range(2):
                rim_copy(it, n).wait_send()


def hand_out(s_ref, e_ref, starts_hbm, ends_hbm, buf, sem):
    copies = []
    for n, (src, dst) in enumerate(((e_ref, ends_hbm), (s_ref, starts_hbm))):
        for t in range(8):
            buf[n, 0, pl.ds(t, 128, stride=8), :] = src[t].T
        cp = pltpu.make_async_copy(buf.at[n], dst, sem.at[n])
        cp.start()
        copies.append(cp)
    for cp in copies:
        cp.wait()


def local(initial_starts, source, region, base_reluctivity, saturation, mobility):
    held = jax.ShapeDtypeStruct((8, 128, 128), F32)
    block = jax.ShapeDtypeStruct((1, 1024, 128), F32)
    hbm = pl.BlockSpec(memory_space=pltpu.HBM)
    in_vmem = pl.BlockSpec(memory_space=pltpu.VMEM)
    vmem = lambda *shape: pltpu.VMEM(shape + (128,), F32)
    ints = lambda *shape: pltpu.VMEM(shape + (128,), jnp.int32)
    table = pltpu.SMEM((8,), F32)
    sem = lambda *shape: pltpu.SemaphoreType.DMA(shape)
    one = pltpu.SemaphoreType.DMA
    args = (base_reluctivity, saturation, mobility, initial_starts, source, region)
    kept = pl.pallas_call(
        kernel,
        out_shape=(held, held),
        in_specs=[hbm] * 6,
        out_specs=(in_vmem, in_vmem),
        scratch_shapes=[
            table, table, table,
            vmem(1, 1024), vmem(1, 1024), ints(1024), vmem(8, 128), vmem(8, 128), ints(8, 128),
            vmem(3, 2, 8, ROWS), vmem(2, 2, 8, ROWS),
            vmem(2, 8, ROWS), vmem(2, 8, ROWS), vmem(2, 8, ROWS), vmem(2, 8, ROWS), vmem(2, HALF), vmem(10, ROWS), vmem(8, ROWS), vmem(10, ROWS),
            ints(8, EDGE), vmem(2, 2, 8, EDGE), vmem(2, 8, EDGE), vmem(8, EDGE), vmem(8, EDGE), vmem(8, EDGE), vmem(8, EDGE),
            vmem(8, EDGE), vmem(8, EDGE), vmem(8, EDGE), vmem(2, 8, 8), vmem(8, 8), vmem(2, 8, 8), vmem(2, 8, 8, 8),
            vmem(2, 2, 8, HALF), vmem(2, 8, HALF), vmem(2, 8, HALF), vmem(2, 8, HALF), vmem(2, 8, HALF),
            pltpu.SemaphoreType.REGULAR, sem(4, 4), sem(2), sem(2), sem(2, 2), sem(2, 2), one, one,
            sem(2, 8), sem(2, 8), sem(2, 8), sem(2, 8), sem(2, 7), sem(2, 7), one, one,
            one, one, sem(9), sem(9),
        ],
        compiler_params=pltpu.CompilerParams(
            collective_id=0, has_side_effects=True, vmem_limit_bytes=40 * 2**20
        ),
        name="parareal",
    )(*[pltpu.with_memory_space_constraint(x, pltpu.HBM) for x in args])
    return pl.pallas_call(
        hand_out,
        out_shape=(block, block),
        in_specs=[in_vmem] * 2,
        out_specs=(hbm, hbm),
        scratch_shapes=[vmem(2, 1, 1024), sem(2)],
        compiler_params=pltpu.CompilerParams(vmem_limit_bytes=16 * 2**20),
        name="hand_out",
    )(*kept)


def solution(mesh):
    in_specs = (P("tm", None, "space"), P("tm", None, "space"), P(None, "space"), P(), P(), P())
    out_specs = (P("tm", None, "space"), P("tm", None, "space"))
    return jax.shard_map(local, mesh=mesh, in_specs=in_specs, out_specs=out_specs, check_vma=False)
```
